32 devices in a mesh: expert: 8 (over y, x, core), hidden: 4 (over z).
Axes of the slice: x: 2, y: 2, z: 4, core: 2. Of those that a mesh axis runs over, the one named last changes fastest.
Arguments:
- tokens: bfloat16 [16384, 768], P(('expert', 'hidden')), may hold values from -6 to 6
- cotangent: bfloat16 [16384, 768], P(('expert', 'hidden')), may hold values from -6 to 6
- segments: int32 [32, 512], P(('expert', 'hidden')), may hold values from 0 to 7, never falling along the last dimension, each value on 1 to 256 neighbouring positions
- routes: int32 [16384], P(('expert', 'hidden')), may hold values from 0 to 15
- slot_ids: int32 [16384], P(('expert', 'hidden')), may hold values from 0 to 39, as said below
- kept_flags: int32 [16384], P(('expert', 'hidden')), may hold values from 0 to 1, as said below
- gain_one: float32 [768], replicated, may hold values from 0.1 to 1.9
- w_qkv: bfloat16 [768, 2304], replicated, may hold values from -0.21875 to 0.21875
- w_out: bfloat16 [768, 768], replicated, may hold values from -0.875 to 0.875
- bias_table: float32 [32, 12], replicated, may hold values from -4 to 4
- gain_two: float32 [768], replicated, may hold values from 0.1 to 1.9
- w_router: float32 [768, 16], replicated, may hold values from -0.109375 to 0.109375
- w_in: bfloat16 [16, 768, 3072], P('expert', None, 'hidden'), may hold values from -0.21875 to 0.21875
- w_back: bfloat16 [16, 3072, 768], P('expert', 'hidden'), may hold values from -3 to 3
Outputs:
- output: bfloat16 [16384, 768], P(('expert', 'hidden'))
- grad_tokens: float32 [16384, 768], P(('expert', 'hidden'))
- grad_gain_one: float32 [768], replicated
- grad_w_qkv: float32 [768, 2304], replicated
- grad_w_out: float32 [768, 768], replicated
- grad_bias: float32 [32, 12], replicated
- grad_gain_two: float32 [768], replicated
- grad_router: float32 [768, 16], replicated
- grad_w_in: float32 [16, 768, 3072], P('expert', None, 'hidden')
- grad_w_back: float32 [16, 3072, 768], P('expert', 'hidden')
The draws below stay inside these ranges and needn't reach their ends.
Inputs may be any that keep to these rules, and one draw needn't show every extreme that they name: `slot_ids`: among the tokens of one device (aligned blocks of 512) that name one expert, the kept ones hold slots 0, 1, 2, ... in token order and at most 40 are kept; later ones are dropped and hold slot 39. In every draw some expert gets more than 40 tokens from every device. `kept_flags`: 1 exactly where the token's place among its device's tokens for its expert is below 40. `segments`: ids are per packed row and never fall along it.
All inputs are finite; a program needn't handle non-finite values.
Results may differ from the reference program's by a relative error of at most 0.014.
Values may be sent and summed in bfloat16 or wider, within the bound.
No kernel may reach another device: no remote copies, remote signals or barrier semaphores. Data moves between devices by JAX's collectives and lax.ppermute only.
A program may use at most 320 MiB of HBM per device.

```python
import math
import jax
import jax.numpy as jnp
import numpy as np
from jax import lax

D = 768
HEADS = 12
HEAD_DIM = 64
FF = 3072
BUCKETS = 32
LEN = 512
DOCS = 8
DOC_MOST = 256
TOK_DEV = 512
SEQS = 32
TOKENS = 16384
EXPERTS = 16
CAP = 40


def route_parts(key):
    base_key = jax.random.fold_in(key, 7)
    key_left, key_right, key_order, key_common, key_start = jax.random.split(base_key, 5)
    left_pick = jax.random.randint(key_left, (TOKENS,), 0, EXPERTS)
    right_pick = jax.random.randint(key_right, (TOKENS,), 0, EXPERTS)
    relabel = jax.random.permutation(key_order, EXPERTS)
    routes = relabel[jnp.minimum(left_pick, right_pick)]
    common = jax.random.randint(key_common, (), 0, EXPERTS)
    forced_start = jax.random.randint(key_start, (TOKENS // TOK_DEV,), 0, TOK_DEV - CAP - 1)
    position_in = jnp.arange(TOKENS, dtype=jnp.int32) % TOK_DEV
    start_of = jnp.repeat(forced_start, TOK_DEV)
    forced = (position_in >= start_of) & (position_in < start_of + CAP + 2)
    routes = jnp.where(forced, common, routes).astype(jnp.int32)
    grouped = routes.reshape(TOKENS // TOK_DEV, TOK_DEV)
    member = (grouped[:, :, None] == jnp.arange(EXPERTS, dtype=jnp.int32)[None, None, :]).astype(jnp.int32)
    before = jnp.cumsum(member, axis=1) - member
    position = jnp.sum(before * member, axis=2).reshape(TOKENS)
    kept_flags = (position < CAP).astype(jnp.int32)
    slot_ids = jnp.where(position < CAP, position, CAP - 1).astype(jnp.int32)
    return (routes, slot_ids, kept_flags)


def draw_routes(key, part):
    return route_parts(key)[0]


def draw_slot_ids(key, part):
    return route_parts(key)[1]


def draw_kept_flags(key, part):
    return route_parts(key)[2]


def levels(key, extent, cuts, least, top_value):
    gain = 1.0
    for dim, parts in cuts:
        draws = jax.random.uniform(jax.random.fold_in(jax.random.fold_in(key, 6), dim), (parts,), jnp.float32, least / len(cuts), top_value / len(cuts))
        gain = gain * jnp.repeat(jnp.exp(draws), extent[dim] // parts).reshape((-1,) + (1,) * (len(extent) - 1 - dim))
    return gain


def length_profile(amount, total, reach, slope):
    loads = [(1 << 20) // math.isqrt(grade ** slope) + 1 for grade in range(2, amount + 1)]
    rest, given = total - reach - (amount - 1), [1] * (amount - 1)
    while rest > 0:
        free = [i for i in range(amount - 1) if given[i] < reach]
        whole, budget = sum([loads[i] for i in free]), rest
        for i in free:
            extra = min(reach - given[i], max(1, budget * loads[i] // whole), rest)
            given[i] = given[i] + extra
            rest = rest - extra
    return np.array([reach] + given)


def uneven(own_key, number_of, total, bound, slope):
    if number_of == 2:
        one = jax.random.randint(own_key, (), max(1, total - bound), min(bound, total - 1) + 1)
        return jnp.stack([one, total - one])
    sizes = jnp.asarray(length_profile(number_of, total, bound, slope), jnp.int32)
    couples = (number_of - 1) // 2
    giver, sink = sizes[1:1 + 2 * couples:2], sizes[2:2 + 2 * couples:2]
    room = jnp.minimum(giver - 1, bound - sink)
    moved = jax.random.randint(jax.random.fold_in(own_key, 1), (couples,), 0, 1 << 20) % (room + 1)
    sizes = sizes.at[1:1 + 2 * couples:2].set(giver - moved).at[2:2 + 2 * couples:2].set(sink + moved)
    return sizes[jax.random.permutation(jax.random.fold_in(own_key, 2), number_of)]


def bell_draw(rng, dims, spread, most, cuts=(), held_as=jnp.bfloat16):
    values = jax.random.normal(rng, dims, jnp.float32) * spread
    if len(cuts) > 0:
        values = levels(rng, dims, cuts, -0.22, 0.18) * values
    return jnp.clip(values, min=-most, max=most).astype(held_as)


def setup_inputs(seed: int = 0) -> dict:
    key_list = jax.random.split(jax.random.key(seed), 15)
    return {
        "tokens": bell_draw(key_list[0], (TOKENS, D), 1.0, 6.0, ((0, 32),)),
        "cotangent": bell_draw(key_list[1], (TOKENS, D), 1.0, 6.0, ((0, 32),)),
        "segments": jax.vmap(lambda own: jnp.searchsorted(jnp.cumsum(uneven(own, DOCS, LEN, DOC_MOST, 2)), jnp.arange(LEN), side="right"))(jax.random.split(key_list[2], SEQS)).reshape((SEQS, LEN)).astype(jnp.int32),
        "routes": draw_routes(jax.random.fold_in(key_list[14], 71), 0),
        "slot_ids": draw_slot_ids(jax.random.fold_in(key_list[14], 71), 0),
        "kept_flags": draw_kept_flags(jax.random.fold_in(key_list[14], 71), 0),
        "gain_one": jnp.clip(1.0 + 0.18 * jax.random.normal(key_list[6], (D,), jnp.float32), 0.1, 1.9),
        "w_qkv": bell_draw(key_list[7], (D, 3 * D), D ** -0.5, 0.21875),
        "w_out": bell_draw(key_list[8], (D, D), (D // 16) ** -0.5, 0.875),
        "bias_table": bell_draw(key_list[9], (BUCKETS, HEADS), 1.0, 4.0, (), jnp.float32),
        "gain_two": jnp.clip(1.0 + 0.18 * jax.random.normal(key_list[10], (D,), jnp.float32), 0.1, 1.9),
        "w_router": bell_draw(key_list[11], (D, EXPERTS), (4 * D) ** -0.5, 0.109375, (), jnp.float32),
        "w_in": bell_draw(key_list[12], (EXPERTS, D, FF), D ** -0.5, 0.21875, ((0, 8), (2, 4))),
        "w_back": bell_draw(key_list[13], (EXPERTS, FF, D), (EXPERTS * 2 ** -5), 3.0, ((0, 8), (1, 4))),
    }


@jax.custom_vjp
def low(v):
    return lax.optimization_barrier(v.astype(jnp.bfloat16)).astype(jnp.float32)

@jax.custom_vjp
def low_back(v):
    return v

def low_keep(v):
    return (low(v), None)

def low_pass(kept, grad):
    return (grad,)

def back_keep(v):
    return (v, None)

def back_low(kept, grad):
    return (low(grad),)
low.defvjp(low_keep, low_pass)
low_back.defvjp(back_keep, back_low)
eps = 1e-06
bucket_edges = (12, 16, 23, 32, 46, 64, 91)
highest = lax.Precision.HIGHEST

def bucket_index(length):
    positions = jnp.arange(length, dtype=jnp.int32)
    offset = positions[None, :] - positions[:, None]
    distance = jnp.abs(offset)
    coarse = jnp.full_like(distance, 8)
    for edge_value in bucket_edges:
        coarse = coarse + (distance >= edge_value).astype(jnp.int32)
    bucket = jnp.where(distance < 8, distance, coarse)
    return bucket + 16 * (offset > 0).astype(jnp.int32)

def rms_norm(values, gain_vec):
    return values * lax.rsqrt(lax.optimization_barrier(jnp.mean(values * values, axis=-1, keepdims=True)) + eps) * gain_vec

def attend(queries, key_rows, value_rows, doc_ids, bias_table):
    bias_full = jnp.transpose(bias_table[bucket_index(queries.shape[0])], (2, 0, 1))
    scores = jnp.einsum('qhd,khd->hqk', queries, key_rows, precision=highest) * HEAD_DIM ** (-0.5) + bias_full
    scores = low_back(scores)
    same_doc = doc_ids[:, None] == doc_ids[None, :]
    scores = jnp.where(same_doc[None], scores, -1000000000.0)
    attn_probs = jax.nn.softmax(scores, axis=-1)
    return jnp.einsum('hqk,khd->qhd', low(attn_probs), value_rows, precision=highest)

def block_forward(inputs, gain_one, w_qkv, w_out, bias_table, gain_two, w_router, w_in, w_back, segments, routes, slot_ids, kept_flags):
    normed_one = low(rms_norm(inputs, gain_one))
    qkv_rows = low_back(low(jnp.dot(normed_one, w_qkv, precision=highest)))
    shaped = qkv_rows.reshape(SEQS, LEN, 3, HEADS, HEAD_DIM)

    def attend_item(seq_item):
        return jax.checkpoint(attend)(seq_item[0], seq_item[1], seq_item[2], seq_item[3], bias_table)
    attended = lax.map(attend_item, (shaped[:, :, 0], shaped[:, :, 1], shaped[:, :, 2], segments))
    attended = low_back(low(attended.reshape(TOKENS, D)))
    residual = inputs + low_back(jnp.dot(attended, w_out, precision=highest))
    normed_two = rms_norm(residual, gain_two)
    router = jax.nn.softmax(jnp.dot(normed_two, w_router, precision=highest), axis=-1)
    kept_mask = kept_flags.astype(jnp.float32)
    gate_value = jnp.take_along_axis(router, routes[:, None], axis=1)[:, 0] * kept_mask
    device_ids = (jnp.arange(TOKENS, dtype=jnp.int32) // TOK_DEV).astype(jnp.int32)
    sent_rows = low(normed_two) * kept_mask[:, None]
    buffer = jnp.zeros((TOKENS // TOK_DEV, EXPERTS, CAP, D), jnp.float32).at[device_ids, routes, slot_ids].add(sent_rows)
    buffer = low_back(buffer)
    expert_rows = jnp.transpose(buffer, (1, 0, 2, 3)).reshape(EXPERTS, TOKENS // TOK_DEV * CAP, D)
    pre_act = low_back(jnp.einsum('erd,edf->erf', expert_rows, w_in, precision=highest))
    active = low(jax.nn.gelu(pre_act, approximate=True))
    expert_out = low_back(low(jnp.einsum('erf,efd->erd', active, w_back, precision=highest)))
    expert_out = jnp.transpose(expert_out.reshape(EXPERTS, TOKENS // TOK_DEV, CAP, D), (1, 0, 2, 3))
    picked = expert_out[device_ids, routes, slot_ids]
    return residual + gate_value[:, None] * picked

def reference(tokens, cotangent, segments, routes, slot_ids, kept_flags, gain_one, w_qkv, w_out, bias_table, gain_two, w_router, w_in, w_back):
    floats = (tokens.astype(jnp.float32), gain_one.astype(jnp.float32), w_qkv.astype(jnp.float32), w_out.astype(jnp.float32), bias_table.astype(jnp.float32), gain_two.astype(jnp.float32), w_router.astype(jnp.float32), w_in.astype(jnp.float32), w_back.astype(jnp.float32))

    def forward(*weights):
        return block_forward(*weights, segments, routes, slot_ids, kept_flags)
    output, pull_back = jax.vjp(forward, *floats)
    gradients = pull_back(cotangent.astype(jnp.float32))
    return (output.astype(jnp.bfloat16), gradients[0], gradients[1], gradients[2], gradients[3], gradients[4], gradients[5], gradients[6], gradients[7], gradients[8])
```

```python
import functools

import jax
import jax.numpy as jnp
from jax import lax
from jax.experimental import pallas as pl
from jax.experimental.pallas import tpu as pltpu
from jax.sharding import PartitionSpec as P

eps = 1e-06
bucket_edges = (12, 16, 23, 32, 46, 64, 91)
highest = lax.Precision.HIGHEST
f32 = jnp.float32
bf16 = jnp.bfloat16
i32 = jnp.int32
BLOCK = 128
VMEM_BYTES = 56 << 20
NN = (((1,), (0,)), ((), ()))
NT = (((1,), (1,)), ((), ()))
TN = (((0,), (0,)), ((), ()))


def mm(left, right, dims=NN):
    return lax.dot_general(left, right, dims, preferred_element_type=f32)


def mm_exact(left, right, dims=NN):
    return lax.dot_general(left, right, dims, precision=highest, preferred_element_type=f32)


def params(semantics=None):
    if semantics is None:
        return pltpu.CompilerParams(vmem_limit_bytes=VMEM_BYTES)
    return pltpu.CompilerParams(vmem_limit_bytes=VMEM_BYTES, dimension_semantics=semantics)


def cost(flops, moved):
    return pl.CostEstimate(flops=int(flops), bytes_accessed=int(moved), transcendentals=0)


def bucket_of(offset):
    distance = jnp.abs(offset)
    coarse = jnp.full_like(distance, 8)
    for edge_value in bucket_edges:
        coarse = coarse + (distance >= edge_value).astype(i32)
    return jnp.where(distance < 8, distance, coarse) + 16 * (offset > 0).astype(i32)


def one_hot(mask):
    return mask.astype(f32).astype(bf16)


def lane_numbers(rows, width):
    return lax.broadcasted_iota(i32, (rows, width), 1)


def place_kernel(routes_ref, slot_ref, kept_ref, seg_ref, bias_ref, cot_ref, out_ref, row_ref, col_ref, diag_ref, *, capacity):
    local_experts, slots = out_ref.shape[:2]
    tokens = cot_ref.shape[0]
    routes = routes_ref[...]
    seat = (routes // local_experts) * capacity + slot_ref[...]
    kept = kept_ref[...] == 1
    line = lax.broadcasted_iota(i32, (BLOCK, tokens), 0)
    stacked = jnp.where(line == local_experts, routes, 0)
    stacked = jnp.where(line == local_experts + 1, seg_ref[...], stacked)
    rows = cot_ref[...]
    for le in range(local_experts):
        key = jnp.where(kept & (routes % local_experts == le), seat, -1)
        stacked = jnp.where(line == le, key, stacked)
        table = lax.broadcasted_iota(i32, (slots, tokens), 0) == key
        out_ref[le] = mm(one_hot(table), rows).astype(bf16)
    row_ref[...] = stacked[: row_ref.shape[0]]
    col_ref[...] = stacked.T
    buckets = bias_ref.shape[0]
    offset = lane_numbers(buckets, 4 * BLOCK) - 2 * BLOCK
    pick = bucket_of(offset) == lax.broadcasted_iota(i32, (buckets, 4 * BLOCK), 0)
    diag_ref[...] = mm_exact(bias_ref[...], pick.astype(f32), TN)


def qkv_kernel(tok_ref, gain_ref, w_ref, qkv_ref, turned_ref, low_ref):
    @pl.when(pl.program_id(0) == 0)
    def _():
        values = tok_ref[...].astype(f32)
        inverse = lax.rsqrt(jnp.mean(values * values, axis=-1, keepdims=True) + eps)
        normed = values * inverse * gain_ref[...]
        low_ref[...] = normed.astype(bf16)
        turned_ref[...] = normed.T.astype(bf16)

    qkv_ref[...] = mm(low_ref[...], w_ref[...]).astype(bf16)


def attend_kernel(q_ref, k_ref, v_ref, row_ids_ref, cols_ref, diag_ref, att_ref, probs_ref, *, seg_line, head_start):
    length = k_ref.shape[0]
    blocks = length // BLOCK
    lane = lane_numbers(1, BLOCK)
    half = BLOCK // 2
    scale = half**-0.5
    keys = k_ref[...]
    vals = v_ref[...]
    row_ids = row_ids_ref[seg_line : seg_line + 1, :]
    bias_tiles = []
    for s in range(2):
        diag = diag_ref[pl.ds(head_start + 2 * pl.program_id(0) + s, 1), :]
        spread = jnp.broadcast_to(diag, (BLOCK, 4 * BLOCK))
        tile = pltpu.roll(spread, 0, 1, stride=1, stride_axis=0)
        low_far = jnp.broadcast_to(diag[:, 1:2], (BLOCK, BLOCK))
        high_far = jnp.broadcast_to(diag[:, 4 * BLOCK - 1 :], (BLOCK, BLOCK))
        bias_tiles.append((low_far, tile, high_far))
    for i in range(blocks):
        rows = slice(i * BLOCK, (i + 1) * BLOCK)
        same = cols_ref[rows, seg_line : seg_line + 1] == row_ids
        queries = q_ref[rows, :]
        outs = []
        for s in range(2):
            mask = jnp.where(lane // half == s, scale, 0.0).astype(bf16)
            scores = mm(queries * mask, keys, NT)
            low_far, tile, high_far = bias_tiles[s]
            pieces = []
            for j in range(blocks):
                if j - i < -1:
                    pieces.append(low_far)
                elif j - i > 1:
                    pieces.append(high_far)
                else:
                    start = (j - i + 2) * BLOCK
                    pieces.append(tile[:, start : start + BLOCK])
            scores = scores + jnp.concatenate(pieces, axis=1)
            scores = jnp.where(same, scores, -1000000000.0)
            top = jnp.max(scores, axis=-1, keepdims=True)
            grown = jnp.exp(scores - top)
            probs = (grown * (1.0 / jnp.sum(grown, axis=-1, keepdims=True))).astype(bf16)
            probs_ref[s, rows, :] = probs
            outs.append(mm(probs, vals))
        att_ref[rows, :] = jnp.where(lane < half, outs[0], outs[1]).astype(bf16)


def chosen_of(router, cols_ref, line):
    pick = cols_ref[:, line : line + 1] == lane_numbers(*router.shape)
    return pick, jnp.sum(jnp.where(pick, router, 0.0), axis=-1, keepdims=True)


def route_kernel(tok_ref, att_a_ref, att_b_ref, w_out_ref, gain_ref, w_router_ref, rows_ref, cols_ref, residual_ref, router_ref, gates_ref, *sent_refs):
    local_experts = len(sent_refs)
    near = att_a_ref.shape[1]
    branch = mm(att_a_ref[...], w_out_ref[:near]) + mm(att_b_ref[...], w_out_ref[near:])
    residual = tok_ref[...].astype(f32) + branch
    residual_ref[...] = residual
    inverse = lax.rsqrt(jnp.mean(residual * residual, axis=-1, keepdims=True) + eps)
    normed = residual * inverse * gain_ref[...]
    low = normed.astype(bf16)
    tokens = low.shape[0]
    for index, sent_ref in enumerate(sent_refs):
        slots = sent_ref.shape[0]
        table = lax.broadcasted_iota(i32, (slots, tokens), 0) == rows_ref[index : index + 1, :]
        sent_ref[...] = mm(one_hot(table), low).astype(bf16)
    logits = mm_exact(normed, w_router_ref[...])
    top = jnp.max(logits, axis=-1, keepdims=True)
    grown = jnp.exp(logits - top)
    router = grown / jnp.sum(grown, axis=-1, keepdims=True)
    router_ref[...] = router
    _, chosen = chosen_of(router, cols_ref, local_experts)
    for index in range(local_experts):
        turned = cols_ref[:, index : index + 1] == lane_numbers(tokens, gates_ref.shape[1])
        gates_ref[index : index + 1, :] = jnp.sum(
            jnp.where(turned, chosen, 0.0), axis=0, keepdims=True
        )


def expert_kernel(place_ref, *refs, parts, le, order, olds):
    sources = {}
    refs = list(refs)
    for j in order:
        sources[j] = [refs.pop(0)] if j == 0 else [refs.pop(0), refs.pop(0)]
    cot_ref, w_in_ref, w_back_ref = refs[:3]
    rest = refs[3 + olds :]
    count = len(order)
    back_refs = rest[:count]
    out_ref, x_all_ref, act_ref, gp_ref, dots_ref = rest[count : count + 5]
    rest = rest[count + 5 :]
    x_buf, g_buf, w_in_buf, w_back_buf, act_buf, gp_buf, back_buf, out_buf = rest[:8]
    x_sem, g_sem, w_sem, put_sem = rest[8:]
    place = place_ref[0]

    def bring_x(at, j):
        if j == 0:
            pltpu.make_async_copy(sources[0][0], x_buf.at[at], x_sem.at[at]).start()
            return
        near = place + j < parts

        @pl.when(near)
        def _():
            pltpu.make_async_copy(sources[j][0], x_buf.at[at], x_sem.at[at]).start()

        @pl.when(jnp.logical_not(near))
        def _():
            pltpu.make_async_copy(sources[j][1], x_buf.at[at], x_sem.at[at]).start()

    whole = [(place + j) % parts for j in order]
    load_in = pltpu.make_async_copy(w_in_ref.at[le], w_in_buf, w_sem.at[0])
    load_back = pltpu.make_async_copy(w_back_ref.at[le], w_back_buf, w_sem.at[1])
    load_in.start()
    loads = []
    for at, j in enumerate(order):
        bring_x(at, j)
        loads.append(pltpu.make_async_copy(cot_ref.at[whole[at], le], g_buf.at[at], g_sem.at[at]))
        loads[at].start()
        if at == 0:
            load_back.start()
    load_in.wait()
    scale = (2.0 / jnp.pi) ** 0.5
    puts = []

    def put(source, target, kind, at):
        copy = pltpu.make_async_copy(source, target, put_sem.at[kind, at])
        copy.start()
        puts.append(copy)

    for at, j in enumerate(order):
        pltpu.make_async_copy(sources[j][0], x_buf.at[at], x_sem.at[at]).wait()
        put(x_buf.at[at], x_all_ref.at[whole[at]], 0, at)
        pre = mm(x_buf[at], w_in_buf[...])
        if at == 0:
            load_back.wait()
        loads[at].wait()
        grad = g_buf[at]
        square = pre * pre
        slant = jnp.tanh(scale * pre * (1.0 + 0.044715 * square))
        act = (0.5 * pre * (1.0 + slant)).astype(bf16)
        act_buf[at] = act
        put(act_buf.at[at], act_ref.at[whole[at]], 1, at)
        slope = 0.5 * (1.0 + slant) + 0.5 * pre * (1.0 - slant * slant) * (
            scale * (1.0 + 3.0 * 0.044715 * square)
        )
        gp = (mm(grad, w_back_buf[...], NT) * slope).astype(bf16)
        gp_buf[at] = gp
        put(gp_buf.at[at], gp_ref.at[whole[at]], 2, at)
        back_buf[at] = mm(gp, w_in_buf[...], NT).astype(bf16)
        put(back_buf.at[at], back_refs[at], 3, at)
        out = mm(act, w_back_buf[...])
        out_buf[at] = out.astype(bf16)
        put(out_buf.at[at], out_ref.at[whole[at], le], 4, at)
        dots = jnp.sum(out * grad.astype(f32), axis=-1, keepdims=True)
        dots_ref[at : at + 1, :] = jnp.broadcast_to(dots, (dots.shape[0], BLOCK)).T[0:1, :]
    for copy in puts:
        copy.wait()


def expert_weights_kernel(place_ref, x_ref, act_ref, cot_ref, gp_ref, gates_ref, *refs):
    in_ref, back_ref, gs_ref, gate_ref = refs[-4:]
    parts, slots = x_ref.shape[:2]

    @pl.when(pl.program_id(0) == 0)
    def _():
        gates = [
            gates_ref[0, pl.ds((part + parts - place_ref[0]) % parts, 1), :]
            for part in range(parts)
        ]
        gates = jnp.concatenate(gates + [jnp.zeros((BLOCK - parts, slots), f32)], axis=0).T
        for part in range(parts):
            gate_ref[part] = gates[:, part : part + 1]
        gs_ref[...] = (cot_ref[:, 0].astype(f32) * gate_ref[...]).astype(bf16)

    def flat(values):
        return values.reshape(-1, values.shape[-1])

    gp = (gp_ref[...].astype(f32) * gate_ref[...]).astype(bf16)
    in_ref[0] = mm(flat(x_ref[...]), flat(gp), TN)
    back_ref[0] = mm(flat(act_ref[...]), flat(gs_ref[...]), TN)


def middle_kernel(residual_ref, cot_ref, gain_ref, w_router_ref, router_ref, cols_ref, dots_ref, w_out_ref, *refs):
    grad_res_ref, branch_ref, att_ref, extra_ref = refs[-4:]
    back_refs = refs[:-4]
    local_experts = len(back_refs)
    tokens = residual_ref.shape[0]
    rows = None
    grad_gate = None
    for index, back_ref in enumerate(back_refs):
        turned = cols_ref[:, index : index + 1] == lane_numbers(tokens, back_ref.shape[0])
        part = mm(one_hot(turned), back_ref[...])
        picked = jnp.sum(
            jnp.where(turned, dots_ref[index : index + 1, :], 0.0), axis=-1, keepdims=True
        )
        rows = part if rows is None else rows + part
        grad_gate = picked if grad_gate is None else grad_gate + picked
    router = router_ref[...]
    pick, chosen = chosen_of(router, cols_ref, local_experts)
    grad_logits = router * (pick.astype(f32) - chosen) * grad_gate
    residual = residual_ref[...]
    inverse = lax.rsqrt(jnp.mean(residual * residual, axis=-1, keepdims=True) + eps)
    gain = gain_ref[...]
    scaled = residual * inverse
    grad_normed = chosen * rows + mm_exact(grad_logits, w_router_ref[...], NT)
    weighted = grad_normed * gain
    lean = jnp.mean(weighted * residual, axis=-1, keepdims=True)
    grad_res = cot_ref[...].astype(f32) + (
        inverse * weighted - residual * (inverse * inverse * inverse) * lean
    )
    grad_res_ref[...] = grad_res
    low = grad_res.astype(bf16)
    branch_ref[...] = low
    att_ref[...] = mm(low, w_out_ref[...], NT).astype(bf16)
    gain_grad = jnp.sum(grad_normed * scaled, axis=0, keepdims=True)
    router_grad = mm_exact(grad_logits, scaled * gain, TN)
    spare = extra_ref.shape[1] - router_grad.shape[0] - 1
    both = jnp.concatenate(
        [router_grad, gain_grad, jnp.zeros((spare, gain_grad.shape[1]), f32)], axis=0
    )
    extra_ref[...] = both.T.astype(bf16)


def attend_back_kernel(q_ref, k_ref, v_ref, probs_ref, grad_ref, turned_ref, *refs, first_group, head_start, buckets):
    if first_group:
        att_a_ref, att_b_ref, branch_ref, extra_ref = refs[:4]
    else:
        old_diag_ref = refs[0]
    dq_ref, dk_ref, dv_ref, weight_ref, diag_ref, slope_ref = refs[-6:]
    step = pl.program_id(0)
    length = k_ref.shape[0]
    blocks = length // BLOCK
    lane = lane_numbers(1, BLOCK)
    half = BLOCK // 2
    scale = half**-0.5
    keys = k_ref[...]
    vals = v_ref[...]
    queries = q_ref[...]
    grads = grad_ref[...]
    columns = 3 * BLOCK * pl.num_programs(0)
    static_columns = weight_ref.shape[1]

    @pl.when(step == 0)
    def _():
        if first_group:
            diag_ref[...] = jnp.zeros_like(diag_ref)
            model = branch_ref.shape[1]
            tail = extra_ref.shape[1]
            begin = static_columns - tail - model
            near = att_a_ref.shape[1]
            branch = branch_ref[...]
            weight_ref[:near, begin : begin + model] = mm(att_a_ref[...], branch, TN).astype(bf16)
            weight_ref[near:, begin : begin + model] = mm(att_b_ref[...], branch, TN).astype(bf16)
            weight_ref[:, begin + model :] = extra_ref[...]
        else:
            diag_ref[...] = old_diag_ref[...]

    across = lax.broadcasted_iota(i32, (BLOCK, BLOCK), 0) + lane_numbers(BLOCK, BLOCK)
    flip = (across == BLOCK - 1).astype(f32)
    dq, dk, dv = [], [], []
    for s in range(2):
        mask = jnp.where(lane // half == s, 1.0, 0.0).astype(bf16)
        near = [None, None, None]
        far = [None, None]
        dq_rows = []
        for i in range(blocks):
            rows = slice(i * BLOCK, (i + 1) * BLOCK)
            probs = probs_ref[s, rows, :].astype(f32)
            grad_probs = mm(grads[rows] * mask, vals, NT)
            delta = jnp.sum(probs * grad_probs, axis=-1, keepdims=True)
            slope = probs * (grad_probs - delta)
            low = slope.astype(bf16)
            slope_ref[rows, :] = low
            dq_rows.append(mm(low, keys))
            for j in range(blocks):
                piece = slope[:, j * BLOCK : (j + 1) * BLOCK]
                apart = j - i
                if abs(apart) <= 1:
                    old = near[apart + 1]
                    near[apart + 1] = piece if old is None else old + piece
                else:
                    old = far[int(apart > 0)]
                    far[int(apart > 0)] = piece if old is None else old + piece
        dq.append(jnp.concatenate(dq_rows, axis=0))
        dk.append(mm(slope_ref[...], queries, TN))
        dv.append(mm(probs_ref[s], grads, TN))
        wide = jnp.concatenate([jnp.zeros_like(near[0])] + near, axis=1)
        lined = pltpu.roll(mm_exact(flip, wide), 3 * BLOCK + 1, 1, stride=1, stride_axis=0)
        lined = jnp.concatenate([lined, far[0], far[1]], axis=1)
        diag_ref[pl.ds(head_start + 2 * step + s, 1), :] = jnp.sum(lined, axis=0, keepdims=True)
    left = lane < half
    dq_low = (jnp.where(left, dq[0], dq[1]) * scale).astype(bf16)
    dk_low = (jnp.where(left, dk[0], dk[1]) * scale).astype(bf16)
    dv_low = jnp.where(left, dv[0], dv[1]).astype(bf16)
    dq_ref[...] = dq_low
    dk_ref[...] = dk_low
    dv_ref[...] = dv_low
    begin = pl.multiple_of(step * (3 * BLOCK), 3 * BLOCK)
    weight_ref[:, pl.ds(begin, 3 * BLOCK)] = mm(
        turned_ref[...], jnp.concatenate([dq_low, dk_low, dv_low], axis=1)
    ).astype(bf16)
    if not first_group:

        @pl.when(step == pl.num_programs(0) - 1)
        def _():
            wide = diag_ref.shape[1]
            number = lane_numbers(buckets, wide)
            bucket = bucket_of(number - 2 * BLOCK)
            bucket = jnp.where(number >= 4 * BLOCK, 15, bucket)
            bucket = jnp.where(number >= 5 * BLOCK, 31, bucket)
            pick = bucket == lax.broadcasted_iota(i32, (buckets, wide), 0)
            rows = jnp.concatenate(
                [diag_ref[...], jnp.zeros((BLOCK - diag_ref.shape[0], wide), f32)], axis=0
            )
            bias = mm_exact(pick.astype(f32), rows, NT)
            begin = static_columns - BLOCK
            weight_ref[:, begin:] = jnp.zeros((weight_ref.shape[0], BLOCK), bf16)
            weight_ref[:buckets, begin:] = bias.astype(bf16)


def tokens_kernel(tok_ref, gain_ref, w_ref, grad_res_ref, *refs):
    out_ref = refs[-1]
    parts = refs[:-1]
    groups = len(parts) // 3
    model = tok_ref.shape[1]
    grad_normed = None
    for part in range(3):
        start = part * model
        for group in range(groups):
            block = parts[3 * group + part]
            width = block.shape[1]
            piece = mm(block[...], w_ref[:, start : start + width], NT)
            grad_normed = piece if grad_normed is None else grad_normed + piece
            start += width
    values = tok_ref[...].astype(f32)
    inverse = lax.rsqrt(jnp.mean(values * values, axis=-1, keepdims=True) + eps)
    weighted = grad_normed * gain_ref[...]
    lean = jnp.mean(weighted * values, axis=-1, keepdims=True)
    out_ref[...] = grad_res_ref[...] + (
        inverse * weighted - values * (inverse * inverse * inverse) * lean
    )


def output_kernel(residual_ref, router_ref, cols_ref, rows_ref, out_ref):
    tokens = residual_ref.shape[0]
    local_experts, slots = rows_ref.shape[:2]
    mixture = None
    for index in range(local_experts):
        turned = cols_ref[:, index : index + 1] == lane_numbers(tokens, slots)
        part = mm(one_hot(turned), rows_ref[index])
        mixture = part if mixture is None else mixture + part
    _, chosen = chosen_of(router_ref[...], cols_ref, local_experts)
    out_ref[...] = (residual_ref[...] + chosen * mixture).astype(bf16)


def finish_kernel(where_ref, own_a_ref, got_a_ref, own_b_ref, got_b_ref, w_ref, qkv_ref, out_ref, gain_ref, extra_ref):
    place = where_ref[2]
    parts = own_a_ref.shape[1]
    model = out_ref.shape[3]
    pairs = model // BLOCK
    near = pairs // 2

    def write(a_ref, b_ref):
        for k in range(parts):
            z = (place + parts - k) % parts
            a = a_ref[0, k].astype(f32)
            b = b_ref[0, k].astype(f32)
            total = None
            for part in range(3):
                pieces = [
                    (a if p < near else b)[:, ((p % near) * 3 + part) * BLOCK :][:, :BLOCK]
                    for p in range(pairs)
                ]
                whole = jnp.concatenate(pieces, axis=1)
                span = slice(part * model, (part + 1) * model)
                qkv_ref[0, z, :, span] = whole
                w = w_ref[0, z, :, span].astype(f32)
                share = jnp.sum(whole * w, axis=-1, keepdims=True)
                total = share if total is None else total + share
            gain_ref[0, z] = jnp.broadcast_to(total, gain_ref.shape[2:])
            begin = near * 3 * BLOCK
            out_ref[0, z] = a[:, begin : begin + model]
            tail = a.shape[1] - begin - model
            extra_ref[0, z, :, :tail] = a[:, begin + model :]
            extra_ref[0, z, :, tail:] = b[:, begin:]

    @pl.when(pl.program_id(0) == 0)
    def _():
        write(own_a_ref, own_b_ref)

    @pl.when(pl.program_id(0) == 1)
    def _():
        write(got_a_ref, got_b_ref)


def add_low(left, right):
    return (left.astype(f32) + right.astype(f32)).astype(bf16)


def line_gather(block, after=None):
    parts = lax.axis_size("hidden")
    right, left = [], []
    if after is not None:
        block, _ = lax.optimization_barrier((block, after))
    moving_right = moving_left = block
    for step in range(1, parts):
        moving_right = lax.ppermute(
            moving_right, "hidden", [(a, a + 1) for a in range(step - 1, parts - 1)]
        )
        moving_left = lax.ppermute(
            moving_left, "hidden", [(a, a - 1) for a in range(1, parts - step + 1)]
        )
        right.append(moving_right)
        left.append(moving_left)
    return block, right, left


def line_scatter(blocks):
    parts = lax.axis_size("hidden")
    right = left = None
    for step in range(1, parts):
        out_right = blocks[parts - step]
        out_left = blocks[step]
        if right is not None:
            out_right = add_low(out_right, right)
            out_left = add_low(out_left, left)
        right = lax.ppermute(out_right, "hidden", [(a, a + 1) for a in range(step)])
        left = lax.ppermute(out_left, "hidden", [(a, a - 1) for a in range(parts - step, parts)])
    return (blocks[0].astype(f32) + right.astype(f32) + left.astype(f32)).astype(bf16)


def pick_block(blocks, index):
    return lax.dynamic_index_in_dim(blocks, index, 0, keepdims=False)


class Sum:
    def __init__(self, values):
        self.groups = lax.axis_size("expert")
        self.parts = lax.axis_size("hidden")
        self.own = lax.axis_index("expert")
        self.place = lax.axis_index("hidden")
        self.core = self.own % 2
        self.chip = self.own // 2
        self.chips = self.groups // 2
        self.pair = [(a, a ^ 1) for a in range(self.groups)]
        self.width = values.shape[1]
        self.values = values

    def cores(self):
        halves = self.values.reshape(2, -1, self.width)
        got = lax.ppermute(pick_block(halves, 1 - self.core), "expert", self.pair)
        self.values = add_low(pick_block(halves, self.core), got)

    def plane(self):
        pieces = self.values.reshape(self.chips, -1, self.width)
        total = pick_block(pieces, self.chip).astype(f32)
        for step in range(1, self.chips):
            ways = [(a, a ^ (2 * step)) for a in range(self.groups)]
            got = lax.ppermute(pick_block(pieces, self.chip ^ step), "expert", ways)
            total = total + got.astype(f32)
        self.values = total.astype(bf16)

    def line(self):
        pieces = self.values.reshape(self.parts, -1, self.width)
        total = pick_block(pieces, self.place).astype(f32)
        for step in range(1, self.parts):
            ways = [(a, (a + step) % self.parts) for a in range(self.parts)]
            got = lax.ppermute(pick_block(pieces, (self.place + step) % self.parts), "hidden", ways)
            total = total + got.astype(f32)
        self.values = total.astype(bf16)

    def line_back(self):
        pieces = [self.values]
        for step in range(1, self.parts):
            ways = [(a, (a + step) % self.parts) for a in range(self.parts)]
            pieces.append(lax.ppermute(self.values, "hidden", ways))
        self.values = jnp.stack(pieces)

    def plane_back(self):
        pieces = [self.values]
        for step in range(1, self.chips):
            ways = [(a, a ^ (2 * step)) for a in range(self.groups)]
            pieces.append(lax.ppermute(self.values, "expert", ways))
        self.values = jnp.stack(pieces)

    def cores_back(self):
        return self.values, lax.ppermute(self.values, "expert", self.pair)

    def run(self):
        self.cores()
        self.plane()
        self.line()
        self.line_back()
        self.plane_back()
        return self.cores_back()


def local(tokens, cotangent, segments, routes, slot_ids, kept_flags, gain_one, w_qkv, w_out, bias_table, gain_two, w_router, w_in, w_back):
    tok_rows, model = tokens.shape
    bucket_count, head_count = bias_table.shape
    experts = w_router.shape[1]
    local_experts = w_in.shape[0]
    hidden = w_in.shape[2]
    groups = lax.axis_size("expert")
    parts = lax.axis_size("hidden")
    own = lax.axis_index("expert")
    place = lax.axis_index("hidden")
    capacity = max(2, (5 * tok_rows + 4 * experts - 1) // (4 * experts))
    slots = groups * capacity
    pairs = head_count // 2
    shape = jax.ShapeDtypeStruct
    vmem = pl.BlockSpec(memory_space=pltpu.VMEM)
    any_space = pl.BlockSpec(memory_space=pl.ANY)
    gain_one_row = gain_one[None, :]
    gain_two_row = gain_two[None, :]
    seg_line = local_experts + 1

    def exchange(rows, axis=0):
        return lax.all_to_all(rows, "expert", split_axis=axis, concat_axis=axis, tiled=True)

    cot_rows, id_rows, id_cols, diag_bias = pl.pallas_call(
        functools.partial(place_kernel, capacity=capacity),
        out_shape=[
            shape((local_experts, slots, model), bf16),
            shape((8, tok_rows), i32),
            shape((tok_rows, BLOCK), i32),
            shape((head_count, 4 * BLOCK), f32),
        ],
        in_specs=[vmem] * 6,
        out_specs=[vmem] * 4,
        compiler_params=params(),
        cost_estimate=cost(2 * local_experts * slots * tok_rows * model, 4 * slots * model * 2),
        name="place",
    )(routes[None, :], slot_ids[None, :], kept_flags[None, :], segments, bias_table, cotangent)
    tokens, cot_rows = lax.optimization_barrier((tokens, cot_rows))
    cot_here = exchange(cot_rows, 1)

    qkv, turned = pl.pallas_call(
        qkv_kernel,
        grid=(3,),
        out_shape=[shape((tok_rows, 3 * model), bf16), shape((model, tok_rows), bf16)],
        in_specs=[
            pl.BlockSpec((tok_rows, model), lambda j: (0, 0)),
            pl.BlockSpec((1, model), lambda j: (0, 0)),
            pl.BlockSpec((model, model), lambda j: (0, j)),
        ],
        out_specs=[
            pl.BlockSpec((tok_rows, model), lambda j: (0, j)),
            pl.BlockSpec((model, tok_rows), lambda j: (0, 0)),
        ],
        scratch_shapes=[pltpu.VMEM((tok_rows, model), bf16)],
        compiler_params=params(("arbitrary",)),
        cost_estimate=cost(6 * tok_rows * model * model, 8 * model * model * 2),
        name="qkv",
    )(tokens, gain_one_row, w_qkv)

    def pair_spec(offset):
        return pl.BlockSpec((tok_rows, BLOCK), lambda p: (0, offset + p))

    steps = pairs // 2
    attended, probs = [], []
    for half in range(2):
        start = half * steps
        att, prob = pl.pallas_call(
            functools.partial(attend_kernel, seg_line=seg_line, head_start=2 * start),
            grid=(steps,),
            out_shape=[
                shape((tok_rows, steps * BLOCK), bf16),
                shape((2 * steps, tok_rows, tok_rows), bf16),
            ],
            in_specs=[
                pair_spec(start),
                pair_spec(pairs + start),
                pair_spec(2 * pairs + start),
                pl.BlockSpec((8, tok_rows), lambda p: (0, 0)),
                pl.BlockSpec((tok_rows, BLOCK), lambda p: (0, 0)),
                pl.BlockSpec((head_count, 4 * BLOCK), lambda p: (0, 0)),
            ],
            out_specs=[
                pair_spec(0),
                pl.BlockSpec((2, tok_rows, tok_rows), lambda p: (p, 0, 0)),
            ],
            compiler_params=params(("arbitrary",)),
            cost_estimate=cost(steps * 4e9, steps * 3e6),
            name="attend",
        )(qkv, qkv, qkv, id_rows, id_cols, diag_bias)
        if half == 0:
            qkv, att, cot_here = lax.optimization_barrier((qkv, att, cot_here))
            cot_all = lax.all_gather(cot_here, "hidden", axis=0, tiled=False)
        attended.append(att)
        probs.append(prob)

    residual, router, gates, *sent_rows = pl.pallas_call(
        route_kernel,
        out_shape=[
            shape((tok_rows, model), f32),
            shape((tok_rows, experts), f32),
            shape((local_experts, slots), f32),
        ]
        + [shape((slots, model), bf16)] * local_experts,
        in_specs=[vmem] * 8,
        out_specs=[vmem] * (3 + local_experts),
        compiler_params=params(),
        cost_estimate=cost(6e9, 6e6),
        name="route",
    )(tokens, *attended, w_out, gain_two_row, w_router, id_rows, id_cols)

    gate_here = exchange(gates, 1)
    gate_all = [gate_here]
    for step in range(1, parts):
        ways = [((a + step) % parts, a) for a in range(parts)]
        gate_all.append(lax.ppermute(gate_here, "hidden", ways))
    gate_all = jnp.stack(gate_all, axis=1)

    place_arr = place.astype(i32).reshape(1)
    block = shape((slots, model), bf16)
    stack = shape((parts, slots, hidden), bf16)
    wide_stack = shape((parts, slots, model), bf16)
    smem = pl.BlockSpec(memory_space=pltpu.SMEM)
    phases = [[0, parts // 2], [j for j in range(1, parts) if j != parts // 2]]
    out_sums = None
    hold = None
    back_sums, dot_parts, kept = [], [], []
    for le in range(local_experts):
        mine, right, left = line_gather(exchange(sent_rows[le]), hold)
        hold = right[1]
        x_all = act = gp = None
        backs = [None] * parts
        dot_rows = [None] * parts
        for order in phases:
            x_blocks = []
            for j in order:
                x_blocks += [mine] if j == 0 else [left[j - 1], right[parts - j - 1]]
            size = len(order)
            fresh = out_sums is None
            olds = [] if x_all is None else [out_sums, x_all, act, gp]
            if x_all is None and not fresh:
                olds = [out_sums]
            first = 1 + len(x_blocks) + 3
            results = pl.pallas_call(
                functools.partial(
                    expert_kernel, parts=parts, le=le, order=order, olds=len(olds)
                ),
                out_shape=[block] * size
                + [
                    shape((parts, local_experts, slots, model), bf16),
                    wide_stack,
                    stack,
                    stack,
                    shape((size, slots), f32),
                ],
                in_specs=[smem] + [any_space] * (len(x_blocks) + 3 + len(olds)),
                out_specs=[any_space] * (size + 4) + [vmem],
                input_output_aliases={first + n: size + n for n in range(len(olds))},
                scratch_shapes=[
                    pltpu.VMEM((size, slots, model), bf16),
                    pltpu.VMEM((size, slots, model), bf16),
                    pltpu.VMEM((model, hidden), bf16),
                    pltpu.VMEM((hidden, model), bf16),
                    pltpu.VMEM((size, slots, hidden), bf16),
                    pltpu.VMEM((size, slots, hidden), bf16),
                    pltpu.VMEM((size, slots, model), bf16),
                    pltpu.VMEM((size, slots, model), bf16),
                    pltpu.SemaphoreType.DMA((size,)),
                    pltpu.SemaphoreType.DMA((size,)),
                    pltpu.SemaphoreType.DMA((2,)),
                    pltpu.SemaphoreType.DMA((5, size)),
                ],
                compiler_params=params(),
                cost_estimate=cost(8 * size * slots * model * hidden, 1e7),
                name="experts",
            )(place_arr, *x_blocks, cot_all, w_in, w_back, *olds)
            out_sums, x_all, act, gp, dot_part = results[size:]
            for at, j in enumerate(order):
                backs[j] = results[at]
                dot_rows[j] = dot_part[at]
        back_sums.append(line_scatter(backs))
        dot_parts.append(dot_rows)
        kept.append((x_all, act, gp))

    grads = None
    third = hidden // 3
    for le in range(local_experts):
        x_all, act, gp = kept[le]
        stack_spec = pl.BlockSpec((parts, slots, model), lambda j: (0, 0, 0))
        hidden_spec = pl.BlockSpec((parts, slots, third), lambda j: (0, 0, j))
        grads = pl.pallas_call(
            expert_weights_kernel,
            grid=(3,),
            out_shape=[
                shape((local_experts, model, hidden), f32),
                shape((local_experts, hidden, model), f32),
            ],
            in_specs=[
                smem,
                stack_spec,
                hidden_spec,
                pl.BlockSpec((parts, 1, slots, model), lambda j, le=le: (0, le, 0, 0)),
                hidden_spec,
                pl.BlockSpec((1, parts, slots), lambda j, le=le: (le, 0, 0)),
            ]
            + ([] if grads is None else [any_space] * 2),
            out_specs=[
                pl.BlockSpec((1, model, third), lambda j, le=le: (le, 0, j)),
                pl.BlockSpec((1, third, model), lambda j, le=le: (le, j, 0)),
            ],
            scratch_shapes=[
                pltpu.VMEM((parts, slots, model), bf16),
                pltpu.VMEM((parts, slots, 1), f32),
            ],
            input_output_aliases={} if grads is None else {6: 0, 7: 1},
            compiler_params=params(("arbitrary",)),
            cost_estimate=cost(4 * parts * slots * model * hidden, 1.3e7),
            name="expert_weights",
        )(place_arr, x_all, act, cot_all, gp, gate_all, *([] if grads is None else grads))
    grad_w_in, grad_w_back = grads

    dots = None
    for step in range(parts):
        row = jnp.stack([dot_rows[step] for dot_rows in dot_parts])
        if step > 0:
            row = lax.ppermute(row, "hidden", [(a, (a + step) % parts) for a in range(parts)])
        dots = row if dots is None else dots + row
    dots = exchange(dots, 1)
    backs = [exchange(rows) for rows in back_sums]
    extra_width = -(-(experts + 1) // BLOCK) * BLOCK

    grad_res, grad_branch, grad_att, extra = pl.pallas_call(
        middle_kernel,
        out_shape=[
            shape((tok_rows, model), f32),
            shape((tok_rows, model), bf16),
            shape((tok_rows, model), bf16),
            shape((model, extra_width), bf16),
        ],
        in_specs=[vmem] * (8 + local_experts),
        out_specs=[vmem] * 4,
        compiler_params=params(),
        cost_estimate=cost(6e9, 8e6),
        name="middle",
    )(residual, cotangent, gain_two_row, w_router, router, id_cols, dots, w_out, *backs)

    out_sums, back_last = lax.optimization_barrier((out_sums, back_sums[-1]))
    out_rows = exchange(lax.psum_scatter(out_sums, "hidden", scatter_dimension=0, tiled=False), 1)
    output = pl.pallas_call(
        output_kernel,
        out_shape=shape((tok_rows, model), bf16),
        in_specs=[vmem] * 4,
        out_specs=vmem,
        compiler_params=params(),
        cost_estimate=cost(1e9, 4e6),
        name="output",
    )(residual, router, id_cols, out_rows)

    grad_parts, sums = [], []
    diag = None
    for group in range(2):
        start = group * steps
        width = 3 * BLOCK * steps + (model + extra_width if group == 0 else BLOCK)
        extras = [*attended, grad_branch, extra] if group == 0 else [diag]
        dq, dk, dv, weight, diag = pl.pallas_call(
            functools.partial(
                attend_back_kernel,
                first_group=group == 0,
                head_start=2 * start,
                buckets=bucket_count,
            ),
            grid=(steps,),
            out_shape=[shape((tok_rows, steps * BLOCK), bf16)] * 3
            + [shape((model, width), bf16), shape((16, 6 * BLOCK), f32)],
            in_specs=[
                pair_spec(start),
                pair_spec(pairs + start),
                pair_spec(2 * pairs + start),
                pl.BlockSpec((2, tok_rows, tok_rows), lambda p: (p, 0, 0)),
                pair_spec(start),
                pl.BlockSpec((model, tok_rows), lambda p: (0, 0)),
            ]
            + [pl.BlockSpec(item.shape, lambda p: (0, 0)) for item in extras],
            out_specs=[pair_spec(0)] * 3
            + [
                pl.BlockSpec((model, width), lambda p: (0, 0)),
                pl.BlockSpec((16, 6 * BLOCK), lambda p: (0, 0)),
            ],
            scratch_shapes=[pltpu.VMEM((tok_rows, tok_rows), bf16)],
            compiler_params=params(("arbitrary",)),
            cost_estimate=cost(steps * 4e9, steps * 3e6),
            name="attend_back",
        )(qkv, qkv, qkv, probs[group], grad_att, turned, *extras)
        grad_parts += [dq, dk, dv]
        sums.append(Sum(weight).run())

    grad_tokens = pl.pallas_call(
        tokens_kernel,
        out_shape=shape((tok_rows, model), f32),
        in_specs=[vmem] * (4 + len(grad_parts)),
        out_specs=vmem,
        compiler_params=params(),
        cost_estimate=cost(3e9, 1e7),
        name="tokens_grad",
    )(tokens, gain_one_row, w_qkv, grad_res, *grad_parts)

    chips = groups // 2
    rows = model // (groups * parts)
    where = jnp.stack([own % 2, own // 2, place]).astype(i32)

    def own_spec(width):
        return pl.BlockSpec(
            (1, parts, rows, width), lambda c, s, at: (jnp.where(c == 0, s, chips - 1), 0, 0, 0)
        )

    def got_spec(width):
        return pl.BlockSpec(
            (1, parts, rows, width), lambda c, s, at: (jnp.where(c == 0, 0, s), 0, 0, 0)
        )

    def whole_spec(width):
        return pl.BlockSpec(
            (1, parts, rows, width), lambda c, s, at: ((at[0] ^ c) * chips + (at[1] ^ s), 0, 0, 0)
        )

    (own_a, got_a), (own_b, got_b) = sums
    width_a, width_b = own_a.shape[-1], own_b.shape[-1]
    tail = extra_width + BLOCK
    finished = pl.pallas_call(
        finish_kernel,
        grid_spec=pltpu.PrefetchScalarGridSpec(
            num_scalar_prefetch=1,
            grid=(2, chips),
            in_specs=[
                own_spec(width_a),
                got_spec(width_a),
                own_spec(width_b),
                got_spec(width_b),
                whole_spec(3 * model),
            ],
            out_specs=[whole_spec(width) for width in (3 * model, model, BLOCK, tail)],
        ),
        out_shape=[
            shape((groups, parts, rows, width), f32) for width in (3 * model, model, BLOCK, tail)
        ],
        compiler_params=params(("arbitrary", "arbitrary")),
        cost_estimate=cost(1e8, 2e7),
        name="finish",
    )(where, own_a, got_a, own_b, got_b, w_qkv.reshape(groups, parts, rows, 3 * model))
    grad_w_qkv, grad_w_out, gain_sums, extras = [
        item.reshape(model, item.shape[-1]) for item in finished
    ]
    return (
        output,
        grad_tokens,
        gain_sums[:, 0] / gain_one,
        grad_w_qkv,
        grad_w_out,
        extras[:bucket_count, extra_width : extra_width + head_count],
        extras[:, experts],
        extras[:, :experts],
        grad_w_in,
        grad_w_back,
    )


def solution(mesh):
    return jax.shard_map(
        local,
        mesh=mesh,
        in_specs=(
            P(("expert", "hidden"), None),
            P(("expert", "hidden"), None),
            P(("expert", "hidden"), None),
            P(("expert", "hidden")),
            P(("expert", "hidden")),
            P(("expert", "hidden")),
            P(),
            P(),
            P(),
            P(),
            P(),
            P(),
            P("expert", None, "hidden"),
            P("expert", "hidden", None),
        ),
        out_specs=(
            P(("expert", "hidden"), None),
            P(("expert", "hidden"), None),
            P(),
            P(),
            P(),
            P(),
            P(),
            P(),
            P("expert", None, "hidden"),
            P("expert", "hidden", None),
        ),
        check_vma=False,
    )
```

```python
import functools

import jax
import jax.numpy as jnp
from jax import lax
from jax.experimental import pallas as pl
from jax.experimental.pallas import tpu as pltpu
from jax.sharding import PartitionSpec as P

eps = 1e-06
bucket_edges = (12, 16, 23, 32, 46, 64, 91)
highest = lax.Precision.HIGHEST
f32 = jnp.float32
bf16 = jnp.bfloat16
i32 = jnp.int32
BLOCK = 128
VMEM_BYTES = 56 << 20
NN = (((1,), (0,)), ((), ()))
NT = (((1,), (1,)), ((), ()))
TN = (((0,), (0,)), ((), ()))


def mm(left, right, dims=NN):
    return lax.dot_general(left, right, dims, preferred_element_type=f32)


def mm_exact(left, right, dims=NN):
    return lax.dot_general(left, right, dims, precision=highest, preferred_element_type=f32)


def params(semantics=None):
    if semantics is None:
        return pltpu.CompilerParams(vmem_limit_bytes=VMEM_BYTES)
    return pltpu.CompilerParams(vmem_limit_bytes=VMEM_BYTES, dimension_semantics=semantics)


def cost(flops, moved):
    return pl.CostEstimate(
        flops=int(flops) // 100, bytes_accessed=int(moved) // 100, transcendentals=0
    )


def bucket_of(offset):
    distance = jnp.abs(offset)
    coarse = jnp.full_like(distance, 8)
    for edge_value in bucket_edges:
        coarse = coarse + (distance >= edge_value).astype(i32)
    return jnp.where(distance < 8, distance, coarse) + 16 * (offset > 0).astype(i32)


def one_hot(mask):
    return mask.astype(f32).astype(bf16)


def lane_numbers(rows, width):
    return lax.broadcasted_iota(i32, (rows, width), 1)


def place_kernel(routes_ref, slot_ref, kept_ref, seg_ref, bias_ref, row_ref, col_ref, diag_ref, *, capacity, local_experts):
    tokens = seg_ref.shape[1]
    routes = routes_ref[...]
    seat = (routes // local_experts) * capacity + slot_ref[...]
    kept = kept_ref[...] == 1
    line = lax.broadcasted_iota(i32, (BLOCK, tokens), 0)
    stacked = jnp.where(line == local_experts, routes, 0)
    stacked = jnp.where(line == local_experts + 1, seg_ref[...], stacked)
    for le in range(local_experts):
        key = jnp.where(kept & (routes % local_experts == le), seat, -1)
        stacked = jnp.where(line == le, key, stacked)
    row_ref[...] = stacked[: row_ref.shape[0]]
    col_ref[...] = stacked.T
    buckets = bias_ref.shape[0]
    offset = lane_numbers(buckets, 4 * BLOCK) - 2 * BLOCK
    pick = bucket_of(offset) == lax.broadcasted_iota(i32, (buckets, 4 * BLOCK), 0)
    diag_ref[...] = mm_exact(bias_ref[...], pick.astype(f32), TN)


def slots_kernel(place_ref, *refs, parts, le):
    key_refs = refs[:parts]
    rows_ref, out_ref = refs[parts:]
    direct = len(out_ref.shape) == 4
    slots = out_ref.shape[0] * out_ref.shape[2] if direct else out_ref.shape[1]
    tokens = rows_ref.shape[1]
    for j in range(parts):
        whole = (place_ref[0] + j) % parts
        key = key_refs[j][le : le + 1, :]
        table = lax.broadcasted_iota(i32, (slots, tokens), 0) == key
        rows = mm(one_hot(table), rows_ref[whole])
        if direct:
            by_group(rows, out_ref, whole)
        else:
            out_ref[whole] = rows.astype(bf16)


def by_group(rows, out_ref, place):
    capacity = out_ref.shape[2]
    for group in range(out_ref.shape[0]):
        piece = rows[group * capacity : (group + 1) * capacity]
        out_ref[group, place] = piece.astype(bf16)


def qkv_kernel(tok_ref, gain_ref, w_ref, qkv_ref, turned_ref, low_ref):
    @pl.when(pl.program_id(0) == 0)
    def _():
        values = tok_ref[...].astype(f32)
        inverse = lax.rsqrt(jnp.mean(values * values, axis=-1, keepdims=True) + eps)
        normed = values * inverse * gain_ref[...]
        low_ref[...] = normed.astype(bf16)
        turned_ref[...] = normed.T.astype(bf16)

    qkv_ref[...] = mm(low_ref[...], w_ref[...]).astype(bf16)


def attend_kernel(q_ref, k_ref, v_ref, row_ids_ref, cols_ref, diag_ref, att_ref, probs_ref, *, seg_line, head_start):
    length = k_ref.shape[0]
    blocks = length // BLOCK
    lane = lane_numbers(1, BLOCK)
    half = BLOCK // 2
    scale = half**-0.5
    keys = k_ref[...]
    vals = v_ref[...]
    row_ids = row_ids_ref[seg_line : seg_line + 1, :]
    bias_tiles = []
    for s in range(2):
        diag = diag_ref[pl.ds(head_start + 2 * pl.program_id(0) + s, 1), :]
        spread = jnp.broadcast_to(diag, (BLOCK, 4 * BLOCK))
        tile = pltpu.roll(spread, 0, 1, stride=1, stride_axis=0)[:, BLOCK:].T
        low_far = jnp.broadcast_to(diag[:, 1:2], (BLOCK, BLOCK))
        high_far = jnp.broadcast_to(diag[:, 4 * BLOCK - 1 :], (BLOCK, BLOCK))
        bias_tiles.append((low_far, tile, high_far))
    turned_vals = vals.astype(f32).T.astype(bf16)
    upper = lax.broadcasted_iota(i32, (BLOCK, 1), 0) < half
    for i in range(blocks):
        rows = slice(i * BLOCK, (i + 1) * BLOCK)
        same = cols_ref[:, seg_line : seg_line + 1] == row_ids[:, rows]
        queries = q_ref[rows, :]
        outs = []
        for s in range(2):
            mask = jnp.where(lane // half == s, scale, 0.0).astype(bf16)
            scores = mm(keys, queries * mask, NT)
            low_far, tile, high_far = bias_tiles[s]
            pieces = []
            for j in range(blocks):
                if j - i < -1:
                    pieces.append(low_far)
                elif j - i > 1:
                    pieces.append(high_far)
                else:
                    start = (j - i + 1) * BLOCK
                    pieces.append(tile[start : start + BLOCK])
            scores = scores + jnp.concatenate(pieces, axis=0)
            scores = jnp.where(same, scores, -1000000000.0)
            top = jnp.max(scores, axis=0, keepdims=True)
            grown = jnp.exp(scores - top)
            probs = (grown * (1.0 / jnp.sum(grown, axis=0, keepdims=True))).astype(bf16)
            probs_ref[s, :, rows] = probs
            outs.append(mm(turned_vals, probs))
        att_ref[rows, :] = jnp.where(upper, outs[0], outs[1]).T.astype(bf16)


def chosen_of(router, cols_ref, line):
    pick = cols_ref[:, line : line + 1] == lane_numbers(*router.shape)
    return pick, jnp.sum(jnp.where(pick, router, 0.0), axis=-1, keepdims=True)


def route_kernel(tok_ref, att_a_ref, att_b_ref, w_out_ref, gain_ref, w_router_ref, rows_ref, residual_ref, router_ref, sent_ref):
    near = att_a_ref.shape[1]
    branch = mm(att_a_ref[...], w_out_ref[:near]) + mm(att_b_ref[...], w_out_ref[near:])
    residual = tok_ref[...].astype(f32) + branch
    residual_ref[...] = residual
    inverse = lax.rsqrt(jnp.mean(residual * residual, axis=-1, keepdims=True) + eps)
    normed = residual * inverse * gain_ref[...]
    low = normed.astype(bf16)
    tokens = low.shape[0]
    direct = len(sent_ref.shape) == 4
    local_experts = sent_ref.shape[1] if direct else sent_ref.shape[0]
    slots = sent_ref.shape[0] * sent_ref.shape[2] if direct else sent_ref.shape[1]
    for index in range(local_experts):
        table = lax.broadcasted_iota(i32, (slots, tokens), 0) == rows_ref[index : index + 1, :]
        rows = mm(one_hot(table), low)
        if direct:
            by_group(rows, sent_ref, index)
        else:
            sent_ref[index] = rows.astype(bf16)
    logits = mm_exact(normed, w_router_ref[...])
    top = jnp.max(logits, axis=-1, keepdims=True)
    grown = jnp.exp(logits - top)
    router = grown / jnp.sum(grown, axis=-1, keepdims=True)
    router_ref[...] = router


def expert_kernel(place_ref, x_ref, cot_ref, w_in_ref, w_back_ref, *refs, parts, le, fresh, groups):
    rest = refs if fresh else refs[1:]
    back_refs = rest[:parts]
    out_ref, act_ref, gp_ref = rest[parts : parts + 3]
    x_buf, g_buf, w_in_buf, w_back_buf, act_buf, gp_buf, back_buf, out_buf = rest[parts + 3 : -4]
    x_sem, g_sem, w_sem, put_sem = rest[-4:]
    place = place_ref[0]
    order = list(range(1, parts)) + [0]
    whole = [(place + j) % parts for j in order]
    load_in = pltpu.make_async_copy(w_in_ref.at[le], w_in_buf, w_sem.at[0])
    load_back = pltpu.make_async_copy(w_back_ref.at[le], w_back_buf, w_sem.at[1])
    load_in.start()
    loads = []
    for at in range(parts):
        loads.append(
            (
                pltpu.make_async_copy(x_ref.at[whole[at], le], x_buf.at[at], x_sem.at[at]),
                pltpu.make_async_copy(cot_ref.at[whole[at]], g_buf.at[at], g_sem.at[at]),
            )
        )
        loads[at][0].start()
        if at == 0:
            load_back.start()
        loads[at][1].start()
    load_in.wait()
    scale = (2.0 / jnp.pi) ** 0.5
    puts = []

    def put(source, target, kind, at):
        copy = pltpu.make_async_copy(source, target, put_sem.at[kind, at])
        copy.start()
        puts.append(copy)

    for at, j in enumerate(order):
        loads[at][0].wait()
        pre = mm(x_buf[at], w_in_buf[...])
        if at == 0:
            load_back.wait()
        loads[at][1].wait()
        grad = g_buf[at]
        square = pre * pre
        slant = jnp.tanh(scale * pre * (1.0 + 0.044715 * square))
        act = (0.5 * pre * (1.0 + slant)).astype(bf16)
        act_buf[at] = act
        put(act_buf.at[at], act_ref.at[whole[at]], 0, at)
        slope = 0.5 * (1.0 + slant) + 0.5 * pre * (1.0 - slant * slant) * (
            scale * (1.0 + 3.0 * 0.044715 * square)
        )
        gp = (mm(grad, w_back_buf[...], NT) * slope).astype(bf16)
        gp_buf[at] = gp
        put(gp_buf.at[at], gp_ref.at[whole[at]], 1, at)
        slots = grad.shape[0]
        back_buf[at, :slots] = mm(gp, w_in_buf[...], NT).astype(bf16)
        out = mm(act, w_back_buf[...])
        out_buf[at] = out.astype(bf16)
        put(out_buf.at[at], out_ref.at[whole[at], le], 3, at)
        dots = jnp.sum(out * grad.astype(f32), axis=-1, keepdims=True)
        dots = jnp.broadcast_to(dots, (slots, BLOCK)).T
        spare = back_buf.shape[1] - slots
        line = lax.broadcasted_iota(i32, (spare, BLOCK), 0)
        laid = jnp.zeros((spare, BLOCK), f32)
        capacity = slots // groups
        for group in range(groups):
            piece = dots[:1, group * capacity : (group + 1) * capacity]
            piece = jnp.concatenate([piece, jnp.zeros((1, BLOCK - capacity), f32)], axis=1)
            laid = jnp.where(line == group, piece, laid)
        back_buf[at, slots:] = jnp.zeros((spare, back_buf.shape[2]), bf16)
        back_buf[at, slots:, :BLOCK] = laid.astype(bf16)
        put(back_buf.at[at], back_refs[j], 2, at)
    for copy in puts:
        copy.wait()


def expert_weights_kernel(own_ref, x_ref, act_ref, cot_ref, gp_ref, w_router_ref, *refs, le, local_experts):
    x_ref = x_ref.at[:, 0]
    in_ref, back_ref, gs_ref, gate_ref = refs[-4:]
    parts = x_ref.shape[0]

    @pl.when(pl.program_id(0) == 0)
    def _():
        w_router = w_router_ref[...]
        high = w_router.astype(bf16)
        low = (w_router - high.astype(f32)).astype(bf16)
        number = own_ref[0] * local_experts + le
        for part in range(parts):
            rows = x_ref[part]
            logits = mm(rows, high) + mm(rows, low)
            grown = jnp.exp(logits - jnp.max(logits, axis=-1, keepdims=True))
            pick = lane_numbers(*logits.shape) == number
            gate = jnp.sum(jnp.where(pick, grown, 0.0), axis=-1, keepdims=True)
            gate = gate / jnp.sum(grown, axis=-1, keepdims=True)
            gate_ref[part] = gate
            gs_ref[part] = (cot_ref[part].astype(f32) * gate).astype(bf16)

    def flat(values):
        return values.reshape(-1, values.shape[-1])

    gp = (gp_ref[...].astype(f32) * gate_ref[...]).astype(bf16)
    in_ref[0] = mm(flat(x_ref[...]), flat(gp), TN)
    back_ref[0] = mm(flat(act_ref[...]), flat(gs_ref[...]), TN)


def middle_kernel(residual_ref, cot_ref, gain_ref, w_router_ref, router_ref, cols_ref, w_out_ref, *refs, capacity, stride):
    grad_res_ref, branch_ref, att_ref, extra_ref = refs[-4:]
    back_refs = refs[:-4]
    local_experts = len(back_refs)
    tokens = residual_ref.shape[0]
    rows = None
    grad_gate = None
    for index, back_ref in enumerate(back_refs):
        key = cols_ref[:, index : index + 1]
        group = key // capacity
        number = lane_numbers(tokens, back_ref.shape[0])
        back = back_ref[...]
        part = mm(one_hot(number == key + group * (stride - capacity)), back)
        lines = mm(one_hot(number == group * stride + capacity), back[:, :BLOCK])
        slot = lane_numbers(tokens, BLOCK) == key - group * capacity
        picked = jnp.sum(jnp.where(slot, lines, 0.0), axis=-1, keepdims=True)
        rows = part if rows is None else rows + part
        grad_gate = picked if grad_gate is None else grad_gate + picked
    router = router_ref[...]
    pick, chosen = chosen_of(router, cols_ref, local_experts)
    grad_logits = router * (pick.astype(f32) - chosen) * grad_gate
    residual = residual_ref[...]
    inverse = lax.rsqrt(jnp.mean(residual * residual, axis=-1, keepdims=True) + eps)
    gain = gain_ref[...]
    scaled = residual * inverse
    grad_normed = chosen * rows + mm_exact(grad_logits, w_router_ref[...], NT)
    weighted = grad_normed * gain
    lean = jnp.mean(weighted * residual, axis=-1, keepdims=True)
    grad_res = cot_ref[...].astype(f32) + (
        inverse * weighted - residual * (inverse * inverse * inverse) * lean
    )
    grad_res_ref[...] = grad_res
    low = grad_res.astype(bf16)
    branch_ref[...] = low
    att_ref[...] = mm(low, w_out_ref[...], NT).astype(bf16)
    gain_grad = jnp.sum(grad_normed * scaled, axis=0, keepdims=True)
    router_grad = mm_exact(grad_logits, scaled * gain, TN)
    spare = extra_ref.shape[1] - router_grad.shape[0] - 1
    both = jnp.concatenate(
        [router_grad, gain_grad, jnp.zeros((spare, gain_grad.shape[1]), f32)], axis=0
    )
    extra_ref[...] = both.T.astype(bf16)


def attend_back_kernel(q_ref, k_ref, v_ref, probs_ref, grad_ref, turned_ref, *refs, kind, head_start, buckets):
    if kind == 0:
        att_a_ref, att_b_ref, branch_ref, extra_ref = refs[:4]
    else:
        old_diag_ref = refs[0]
    if kind == 2:
        old_weight_ref = refs[1]
    dq_ref, dk_ref, dv_ref, weight_ref, diag_ref, slope_ref = refs[-6:]
    step = pl.program_id(0)
    length = k_ref.shape[0]
    blocks = length // BLOCK
    lane = lane_numbers(1, BLOCK)
    half = BLOCK // 2
    scale = half**-0.5
    keys = k_ref[...]
    vals = v_ref[...]
    queries = q_ref[...]
    grads = grad_ref[...]
    static_columns = weight_ref.shape[1]

    @pl.when(step == 0)
    def _():
        if kind == 0:
            diag_ref[...] = jnp.zeros_like(diag_ref)
            model = branch_ref.shape[1]
            tail = extra_ref.shape[1]
            begin = static_columns - tail - model
            near = att_a_ref.shape[1]
            branch = branch_ref[...]
            weight_ref[:near, begin : begin + model] = mm(att_a_ref[...], branch, TN).astype(bf16)
            weight_ref[near:, begin : begin + model] = mm(att_b_ref[...], branch, TN).astype(bf16)
            weight_ref[:, begin + model :] = extra_ref[...]
        else:
            diag_ref[...] = old_diag_ref[...]
        if kind == 2:
            weight_ref[:, : old_weight_ref.shape[1]] = old_weight_ref[...]

    across = lax.broadcasted_iota(i32, (BLOCK, BLOCK), 0) + lane_numbers(BLOCK, BLOCK)
    flip = (across == BLOCK - 1).astype(f32)
    turned_keys = keys.astype(f32).T.astype(bf16)
    dq = [[] for _ in range(blocks)]
    dk, dv = [], []
    for s in range(2):
        mask = jnp.where(lane // half == s, 1.0, 0.0).astype(bf16)
        near = [None, None, None]
        far = [None, None]
        for i in range(blocks):
            rows = slice(i * BLOCK, (i + 1) * BLOCK)
            probs = probs_ref[s, :, rows].astype(f32)
            grad_probs = mm(vals, grads[rows] * mask, NT)
            delta = jnp.sum(probs * grad_probs, axis=0, keepdims=True)
            slope = probs * (grad_probs - delta)
            low = slope.astype(bf16)
            slope_ref[:, rows] = low
            dq[i].append(mm(turned_keys, low))
            for j in range(blocks):
                piece = slope[j * BLOCK : (j + 1) * BLOCK]
                apart = j - i
                if abs(apart) <= 1:
                    old = near[1 - apart]
                    near[1 - apart] = piece if old is None else old + piece
                else:
                    old = far[int(apart > 0)]
                    far[int(apart > 0)] = piece if old is None else old + piece
        dk.append(mm(slope_ref[...], queries))
        dv.append(mm(probs_ref[s], grads))
        wide = jnp.concatenate([jnp.zeros_like(near[0])] + near, axis=1)
        lined = pltpu.roll(mm_exact(flip, wide), 3 * BLOCK + 1, 1, stride=1, stride_axis=0)
        lined = jnp.concatenate([lined, far[0], far[1]], axis=1)
        diag_ref[pl.ds(head_start + 2 * step + s, 1), :] = jnp.sum(lined, axis=0, keepdims=True)
    upper = lax.broadcasted_iota(i32, (BLOCK, 1), 0) < half
    dq_low = jnp.concatenate([jnp.where(upper, *item).T for item in dq], axis=0)
    dq_low = (dq_low * scale).astype(bf16)
    left = lane < half
    dk_low = (jnp.where(left, dk[0], dk[1]) * scale).astype(bf16)
    dv_low = jnp.where(left, dv[0], dv[1]).astype(bf16)
    dq_ref[...] = dq_low
    dk_ref[...] = dk_low
    dv_ref[...] = dv_low
    begin = 0 if kind < 2 else old_weight_ref.shape[1]
    begin = pl.multiple_of(step * (3 * BLOCK) + begin, 3 * BLOCK)
    weight_ref[:, pl.ds(begin, 3 * BLOCK)] = mm(
        turned_ref[...], jnp.concatenate([dq_low, dk_low, dv_low], axis=1)
    ).astype(bf16)
    if kind == 2:

        @pl.when(step == pl.num_programs(0) - 1)
        def _():
            wide = diag_ref.shape[1]
            number = lane_numbers(buckets, wide)
            bucket = bucket_of(2 * BLOCK - number)
            bucket = jnp.where(number >= 4 * BLOCK, 15, bucket)
            bucket = jnp.where(number >= 5 * BLOCK, 31, bucket)
            pick = bucket == lax.broadcasted_iota(i32, (buckets, wide), 0)
            rows = jnp.concatenate(
                [diag_ref[...], jnp.zeros((BLOCK - diag_ref.shape[0], wide), f32)], axis=0
            )
            bias = mm_exact(pick.astype(f32), rows, NT)
            begin = static_columns - BLOCK
            weight_ref[:, begin:] = jnp.zeros((weight_ref.shape[0], BLOCK), bf16)
            weight_ref[:buckets, begin:] = bias.astype(bf16)


def tokens_kernel(tok_ref, gain_ref, w_ref, grad_res_ref, *refs):
    out_ref = refs[-1]
    parts = refs[:-1]
    groups = len(parts) // 3
    model = tok_ref.shape[1]
    grad_normed = None
    for part in range(3):
        start = part * model
        for group in range(groups):
            block = parts[3 * group + part]
            width = block.shape[1]
            piece = mm(block[...], w_ref[:, start : start + width], NT)
            grad_normed = piece if grad_normed is None else grad_normed + piece
            start += width
    values = tok_ref[...].astype(f32)
    inverse = lax.rsqrt(jnp.mean(values * values, axis=-1, keepdims=True) + eps)
    weighted = grad_normed * gain_ref[...]
    lean = jnp.mean(weighted * values, axis=-1, keepdims=True)
    out_ref[...] = grad_res_ref[...] + (
        inverse * weighted - values * (inverse * inverse * inverse) * lean
    )


def output_kernel(residual_ref, router_ref, cols_ref, rows_ref, out_ref):
    tokens = residual_ref.shape[0]
    local_experts, slots = rows_ref.shape[:2]
    mixture = None
    for index in range(local_experts):
        turned = cols_ref[:, index : index + 1] == lane_numbers(tokens, slots)
        part = mm(one_hot(turned), rows_ref[index])
        mixture = part if mixture is None else mixture + part
    _, chosen = chosen_of(router_ref[...], cols_ref, local_experts)
    out_ref[...] = (residual_ref[...] + chosen * mixture).astype(bf16)


def finish_kernel(where_ref, own_a_ref, got_a_ref, own_b_ref, got_b_ref, w_ref, qkv_ref, out_ref, gain_ref, extra_ref):
    place = where_ref[2]
    parts = own_a_ref.shape[1]
    model = out_ref.shape[3]
    pairs = model // BLOCK
    near = pairs // 3

    def write(a_ref, b_ref):
        for k in range(parts):
            z = (place + parts - k) % parts
            a = a_ref[0, k].astype(f32)
            b = b_ref[0, k].astype(f32)
            total = None
            for part in range(3):
                pieces = [
                    (a if p < near else b)[
                        :, ((p if p < near else p - near) * 3 + part) * BLOCK :
                    ][:, :BLOCK]
                    for p in range(pairs)
                ]
                whole = jnp.concatenate(pieces, axis=1)
                span = slice(part * model, (part + 1) * model)
                qkv_ref[0, z, :, span] = whole
                w = w_ref[0, z, :, span].astype(f32)
                share = jnp.sum(whole * w, axis=-1, keepdims=True)
                total = share if total is None else total + share
            gain_ref[0, z] = jnp.broadcast_to(total, gain_ref.shape[2:])
            begin = near * 3 * BLOCK
            out_ref[0, z] = a[:, begin : begin + model]
            tail = a.shape[1] - begin - model
            extra_ref[0, z, :, :tail] = a[:, begin + model :]
            extra_ref[0, z, :, tail:] = b[:, (pairs - near) * 3 * BLOCK :]

    @pl.when(pl.program_id(0) == 0)
    def _():
        write(own_a_ref, own_b_ref)

    @pl.when(pl.program_id(0) == 1)
    def _():
        write(got_a_ref, got_b_ref)


def add_low(left, right):
    return (left.astype(f32) + right.astype(f32)).astype(bf16)


def tie(items, after):
    return lax.optimization_barrier((items, after))[0]


def held(kernel, start, after):
    def body(*refs):
        kernel(*refs[:start], *refs[start + len(after) :])

    return body


class Scatter:
    def __init__(self, blocks):
        self.parts = lax.axis_size("hidden")
        self.blocks = blocks
        self.count = 0

    def step(self, after=()):
        self.count += 1
        right, left = self.blocks[self.parts - self.count], self.blocks[self.count]
        if self.count > 1:
            right, left = add_low(right, self.right), add_low(left, self.left)
        right, left = tie((right, left), after)
        ways = [(a, a + 1) for a in range(self.count)]
        self.right = lax.ppermute(right, "hidden", ways)
        ways = [(a, a - 1) for a in range(self.parts - self.count, self.parts)]
        self.left = lax.ppermute(left, "hidden", ways)

    def last(self):
        return self.right, self.left

    def finish(self, after=()):
        right, left = tie(self.last(), after)
        total = self.blocks[0].astype(f32) + right.astype(f32) + left.astype(f32)
        return total.astype(bf16)


def pick_block(blocks, index):
    return lax.dynamic_index_in_dim(blocks, index, 0, keepdims=False)


class Sum:
    def __init__(self, values):
        self.groups = lax.axis_size("expert")
        self.parts = lax.axis_size("hidden")
        self.own = lax.axis_index("expert")
        self.place = lax.axis_index("hidden")
        self.core = self.own % 2
        self.chip = self.own // 2
        self.chips = self.groups // 2
        self.pair = [(a, a ^ 1) for a in range(self.groups)]
        self.width = values.shape[1]
        self.values = values

    def cores(self):
        halves = self.values.reshape(2, -1, self.width)
        got = lax.ppermute(pick_block(halves, 1 - self.core), "expert", self.pair)
        self.values = add_low(pick_block(halves, self.core), got)

    def cores_at_once(self):
        teams = [[2 * a, 2 * a + 1] for a in range(self.chips)]
        got = lax.all_to_all(
            self.values, "expert", split_axis=0, concat_axis=0, tiled=True, axis_index_groups=teams
        ).reshape(2, -1, self.width)
        self.values = add_low(got[0], got[1])

    def plane(self):
        pieces = self.values.reshape(self.chips, -1, self.width)
        total = pick_block(pieces, self.chip).astype(f32)
        for step in range(1, self.chips):
            ways = [(a, a ^ (2 * step)) for a in range(self.groups)]
            got = lax.ppermute(pick_block(pieces, self.chip ^ step), "expert", ways)
            total = total + got.astype(f32)
        self.values = total.astype(bf16)

    def line(self):
        pieces = self.values.reshape(self.parts, -1, self.width)
        total = pick_block(pieces, self.place).astype(f32)
        for step in range(1, self.parts):
            ways = [(a, (a + step) % self.parts) for a in range(self.parts)]
            got = lax.ppermute(pick_block(pieces, (self.place + step) % self.parts), "hidden", ways)
            total = total + got.astype(f32)
        self.values = total.astype(bf16)

    def line_back(self):
        pieces = [self.values]
        for step in range(1, self.parts):
            ways = [(a, (a + step) % self.parts) for a in range(self.parts)]
            pieces.append(lax.ppermute(self.values, "hidden", ways))
        self.values = jnp.stack(pieces)

    def plane_back(self):
        pieces = [self.values]
        for step in range(1, self.chips):
            ways = [(a, a ^ (2 * step)) for a in range(self.groups)]
            pieces.append(lax.ppermute(self.values, "expert", ways))
        self.values = jnp.stack(pieces)

    def cores_back(self):
        return self.values, lax.ppermute(self.values, "expert", self.pair)

    def run(self):
        self.cores()
        self.plane()
        self.line()
        self.line_back()
        self.plane_back()
        return self.cores_back()


def local(tokens, cotangent, segments, routes, slot_ids, kept_flags, gain_one, w_qkv, w_out, bias_table, gain_two, w_router, w_in, w_back):
    tok_rows, model = tokens.shape
    bucket_count, head_count = bias_table.shape
    experts = w_router.shape[1]
    local_experts = w_in.shape[0]
    hidden = w_in.shape[2]
    groups = lax.axis_size("expert")
    parts = lax.axis_size("hidden")
    own = lax.axis_index("expert")
    place = lax.axis_index("hidden")
    capacity = max(2, (5 * tok_rows + 4 * experts - 1) // (4 * experts))
    slots = groups * capacity
    pairs = head_count // 2
    shape = jax.ShapeDtypeStruct
    vmem = pl.BlockSpec(memory_space=pltpu.VMEM)
    any_space = pl.BlockSpec(memory_space=pl.ANY)
    gain_one_row = gain_one[None, :]
    gain_two_row = gain_two[None, :]
    seg_line = local_experts + 1

    def exchange(rows, axis=0):
        return lax.all_to_all(rows, "expert", split_axis=axis, concat_axis=axis, tiled=True)

    cot_near = lax.all_gather(cotangent, "hidden", axis=0, tiled=False)
    id_rows, id_cols, diag_bias = pl.pallas_call(
        functools.partial(place_kernel, capacity=capacity, local_experts=local_experts),
        out_shape=[
            shape((8, tok_rows), i32),
            shape((tok_rows, BLOCK), i32),
            shape((head_count, 4 * BLOCK), f32),
        ],
        in_specs=[vmem] * 5,
        out_specs=[vmem] * 3,
        compiler_params=params(),
        cost_estimate=cost(1e8, 1e6),
        name="place",
    )(routes[None, :], slot_ids[None, :], kept_flags[None, :], segments, bias_table)
    qkv, turned = pl.pallas_call(
        qkv_kernel,
        grid=(3,),
        out_shape=[shape((tok_rows, 3 * model), bf16), shape((model, tok_rows), bf16)],
        in_specs=[
            pl.BlockSpec((tok_rows, model), lambda j: (0, 0)),
            pl.BlockSpec((1, model), lambda j: (0, 0)),
            pl.BlockSpec((model, model), lambda j: (0, j)),
        ],
        out_specs=[
            pl.BlockSpec((tok_rows, model), lambda j: (0, j)),
            pl.BlockSpec((model, tok_rows), lambda j: (0, 0)),
        ],
        scratch_shapes=[pltpu.VMEM((tok_rows, model), bf16)],
        compiler_params=params(("arbitrary",)),
        cost_estimate=cost(6 * tok_rows * model * model, 8 * model * model * 2),
        name="qkv",
    )(tokens, gain_one_row, w_qkv)

    def pair_spec(offset):
        return pl.BlockSpec((tok_rows, BLOCK), lambda p: (0, offset + p))

    steps = pairs // 2
    attended, probs = [], []
    for half in range(2):
        start = half * steps
        att, prob = pl.pallas_call(
            functools.partial(attend_kernel, seg_line=seg_line, head_start=2 * start),
            grid=(steps,),
            out_shape=[
                shape((tok_rows, steps * BLOCK), bf16),
                shape((2 * steps, tok_rows, tok_rows), bf16),
            ],
            in_specs=[
                pair_spec(start),
                pair_spec(pairs + start),
                pair_spec(2 * pairs + start),
                pl.BlockSpec((8, tok_rows), lambda p: (0, 0)),
                pl.BlockSpec((tok_rows, BLOCK), lambda p: (0, 0)),
                pl.BlockSpec((head_count, 4 * BLOCK), lambda p: (0, 0)),
            ],
            out_specs=[
                pair_spec(0),
                pl.BlockSpec((2, tok_rows, tok_rows), lambda p: (p, 0, 0)),
            ],
            compiler_params=params(("arbitrary",)),
            cost_estimate=cost(steps * 4e9, steps * 3e6),
            name="attend",
        )(qkv, qkv, qkv, id_rows, id_cols, diag_bias)
        attended.append(att)
        probs.append(prob)

    def by_slots(count):
        if direct:
            return shape((groups, count, capacity, model), bf16)
        return shape((count, slots, model), bf16)

    direct = capacity % 8 == 0
    residual, router, sent_rows = pl.pallas_call(
        route_kernel,
        out_shape=[
            shape((tok_rows, model), f32),
            shape((tok_rows, experts), f32),
            by_slots(local_experts),
        ],
        in_specs=[vmem] * 7,
        out_specs=[vmem] * 3,
        compiler_params=params(),
        cost_estimate=cost(6e9, 6e6),
        name="route",
    )(tokens, *attended, w_out, gain_two_row, w_router, id_rows)

    place_arr = place.astype(i32).reshape(1)
    own_arr = own.astype(i32).reshape(1)
    spare = -(-groups // 16) * 16
    block = shape((slots + spare, model), bf16)
    stack = shape((parts, slots, hidden), bf16)
    wide_stack = shape((parts, slots, model), bf16)
    smem = pl.BlockSpec(memory_space=pltpu.SMEM)
    third = hidden // 3

    def run_experts(le, out_sums, after=()):
        results = pl.pallas_call(
            held(
                functools.partial(
                    expert_kernel, parts=parts, le=le, fresh=not out_sums, groups=groups
                ),
                5 + len(out_sums),
                after,
            ),
            out_shape=[block] * parts
            + [
                shape((parts, local_experts, slots, model), bf16),
                stack,
                stack,
            ],
            in_specs=[smem] + [any_space] * (4 + len(out_sums) + len(after)),
            out_specs=[any_space] * (parts + 3),
            input_output_aliases={5 + n: parts + n for n in range(len(out_sums))},
            scratch_shapes=[
                pltpu.VMEM((parts, slots, model), bf16),
                pltpu.VMEM((parts, slots, model), bf16),
                pltpu.VMEM((model, hidden), bf16),
                pltpu.VMEM((hidden, model), bf16),
                pltpu.VMEM((parts, slots, hidden), bf16),
                pltpu.VMEM((parts, slots, hidden), bf16),
                pltpu.VMEM((parts, slots + spare, model), bf16),
                pltpu.VMEM((parts, slots, model), bf16),
                pltpu.SemaphoreType.DMA((parts,)),
                pltpu.SemaphoreType.DMA((parts,)),
                pltpu.SemaphoreType.DMA((2,)),
                pltpu.SemaphoreType.DMA((4, parts)),
            ],
            compiler_params=params(),
            cost_estimate=cost(8 * parts * slots * model * hidden, 2e7),
            name="experts",
        )(place_arr, rows_all, cot_all[le], w_in, w_back, *out_sums, *after)
        backs, (out_sum, act, gp) = results[:parts], results[parts:]
        return backs, [out_sum], (act, gp)

    def run_weights(le, kept, grads, after):
        act, gp = kept
        stack_spec = pl.BlockSpec((parts, slots, model), lambda j: (0, 0, 0))
        hidden_spec = pl.BlockSpec((parts, slots, third), lambda j: (0, 0, j))
        return pl.pallas_call(
            held(
                functools.partial(expert_weights_kernel, le=le, local_experts=local_experts),
                6 + len(grads),
                after,
            ),
            grid=(3,),
            out_shape=[
                shape((local_experts, model, hidden), f32),
                shape((local_experts, hidden, model), f32),
            ],
            in_specs=[
                smem,
                pl.BlockSpec((parts, 1, slots, model), lambda j: (0, le, 0, 0)),
                hidden_spec,
                stack_spec,
                hidden_spec,
                pl.BlockSpec((model, experts), lambda j: (0, 0)),
            ]
            + [any_space] * (len(grads) + len(after)),
            out_specs=[
                pl.BlockSpec((1, model, third), lambda j: (le, 0, j)),
                pl.BlockSpec((1, third, model), lambda j: (le, j, 0)),
            ],
            scratch_shapes=[
                pltpu.VMEM((parts, slots, model), bf16),
                pltpu.VMEM((parts, slots, 1), f32),
            ],
            input_output_aliases={6 + n: n for n in range(len(grads))},
            compiler_params=params(("arbitrary",)),
            cost_estimate=cost(4 * parts * slots * model * hidden, 1.3e7),
            name="expert_weights",
        )(own_arr, rows_all, act, cot_all[le], gp, w_router, *grads, *after)

    def own_slots(le, ids, after):
        return pl.pallas_call(
            held(functools.partial(slots_kernel, parts=parts, le=le), 2 + parts, after),
            out_shape=by_slots(parts),
            in_specs=[smem] + [vmem] * (parts + 1) + [any_space] * len(after),
            out_specs=vmem,
            compiler_params=params(),
            cost_estimate=cost(2e9, 6e6),
            name="slots",
        )(place_arr, *ids, cot_near, *after)

    def exchange_slots(rows):
        if not direct:
            return exchange(rows, 1)
        return exchange(rows).transpose(1, 0, 2, 3).reshape(-1, slots, model)

    here = exchange_slots(sent_rows)
    rows_all = lax.all_gather(here, "hidden", axis=0, tiled=False)
    ids = [id_rows]
    far_ids = tie(id_rows, here)
    for step in range(1, parts):
        ways = [((a + step) % parts, a) for a in range(parts)]
        ids.append(lax.ppermute(far_ids, "hidden", ways))
    cot_slots = [own_slots(0, ids, [here])]
    cot_slots.append(own_slots(1, ids, cot_slots))
    cot_all = [exchange_slots(cot_slots[0])]
    cot_all.append(exchange_slots(tie(cot_slots[1], cot_all[0])))
    backs, out_sums, kept = run_experts(0, [], cot_all[1:])
    sum_first = Scatter(backs)
    sum_first.step()
    backs, out_sums, kept_second = run_experts(1, out_sums)
    sum_second = Scatter(backs)
    sum_first.step()
    sum_second.step()
    grads = run_weights(0, kept, [], kept_second[:1])
    sum_first.step(grads)
    sum_second.step(grads)
    grads = run_weights(1, kept_second, grads, sum_second.last()[:1])

    def with_dots(total):
        rows = total[:slots].reshape(groups, capacity, model)
        dots = total[slots : slots + groups].reshape(groups, 1, model)
        dots = jnp.pad(dots, ((0, 0), (0, stride - capacity - 1), (0, 0)))
        return jnp.concatenate([rows, dots], axis=1).reshape(groups * stride, model)

    stride = -(-(capacity + 1) // 8) * 8
    back_first = exchange(with_dots(sum_first.finish()))
    sum_second.step(grads)
    grad_w_in, grad_w_back = grads
    out_sums = out_sums[0]
    back_second = sum_second.finish(back_first)
    backs = [back_first, exchange(with_dots(back_second))]
    extra_width = -(-(experts + 1) // BLOCK) * BLOCK

    grad_res, grad_branch, grad_att, extra = pl.pallas_call(
        functools.partial(middle_kernel, capacity=capacity, stride=stride),
        out_shape=[
            shape((tok_rows, model), f32),
            shape((tok_rows, model), bf16),
            shape((tok_rows, model), bf16),
            shape((model, extra_width), bf16),
        ],
        in_specs=[vmem] * (7 + local_experts),
        out_specs=[vmem] * 4,
        compiler_params=params(),
        cost_estimate=cost(6e9, 8e6),
        name="middle",
    )(residual, cotangent, gain_two_row, w_router, router, id_cols, w_out, *backs)

    out_sums = tie(out_sums, back_second)
    out_rows = lax.psum_scatter(out_sums, "hidden", scatter_dimension=0, tiled=False)
    out_rows = out_rows.reshape(local_experts, groups, capacity, model).transpose(1, 0, 2, 3)
    out_ready = out_rows
    out_rows = exchange(out_rows).transpose(1, 0, 2, 3).reshape(local_experts, slots, model)
    output = pl.pallas_call(
        output_kernel,
        out_shape=shape((tok_rows, model), bf16),
        in_specs=[vmem] * 4,
        out_specs=vmem,
        compiler_params=params(),
        cost_estimate=cost(1e9, 4e6),
        name="output",
    )(residual, router, id_cols, out_rows)

    def run_back(kind, start, count, extras, width):
        inner = start % steps
        return pl.pallas_call(
            functools.partial(
                attend_back_kernel,
                kind=kind,
                head_start=2 * start,
                buckets=bucket_count,
            ),
            grid=(count,),
            out_shape=[shape((tok_rows, count * BLOCK), bf16)] * 3
            + [shape((model, width), bf16), shape((16, 6 * BLOCK), f32)],
            in_specs=[
                pair_spec(start),
                pair_spec(pairs + start),
                pair_spec(2 * pairs + start),
                pl.BlockSpec((2, tok_rows, tok_rows), lambda p: (inner + p, 0, 0)),
                pair_spec(start),
                pl.BlockSpec((model, tok_rows), lambda p: (0, 0)),
            ]
            + [pl.BlockSpec(item.shape, lambda p: (0, 0)) for item in extras],
            out_specs=[pair_spec(0)] * 3
            + [
                pl.BlockSpec((model, width), lambda p: (0, 0)),
                pl.BlockSpec((16, 6 * BLOCK), lambda p: (0, 0)),
            ],
            scratch_shapes=[pltpu.VMEM((tok_rows, tok_rows), bf16)],
            compiler_params=params(("arbitrary",)),
            cost_estimate=cost(count * 4e9, count * 3e6),
            name="attend_back",
        )(qkv, qkv, qkv, probs[start // steps], grad_att, turned, *extras)

    wide = 3 * BLOCK
    early = pairs // 3
    first = run_back(
        0, 0, early, [*attended, grad_branch, extra], wide * early + model + extra_width
    )
    sum_a = Sum(first[3])
    sum_a.cores()
    second = run_back(1, early, 1, [first[4]], wide)
    sum_a.values = tie(sum_a.values, second[3])
    sum_a.plane()
    third_part = run_back(
        2, early + 1, pairs - early - 1, [second[4], second[3]], wide * (pairs - early) + BLOCK
    )
    sum_b = Sum(tie(third_part[3], sum_a.values))
    sum_b.cores()
    grad_parts = [*first[:3], *second[:3], *third_part[:3]]
    grad_tokens = pl.pallas_call(
        tokens_kernel,
        out_shape=shape((tok_rows, model), f32),
        in_specs=[vmem] * (4 + len(grad_parts)),
        out_specs=vmem,
        compiler_params=params(),
        cost_estimate=cost(3e9, 1e7),
        name="tokens_grad",
    )(tokens, gain_one_row, w_qkv, grad_res, *grad_parts)
    sum_a.line()
    sum_b.values = tie(sum_b.values, grad_tokens)
    sum_b.plane()
    sum_b.values = tie(sum_b.values, out_ready)
    sum_a.line_back()
    sum_b.line()
    sum_b.values = tie(sum_b.values, out_rows)
    sum_a.plane_back()
    sum_b.line_back()
    sum_b.values = tie(sum_b.values, sum_a.values)
    sums = [sum_a.cores_back()]
    sum_b.plane_back()
    sums.append(sum_b.cores_back())

    chips = groups // 2
    rows = model // (groups * parts)
    where = jnp.stack([own % 2, own // 2, place]).astype(i32)

    def own_spec(width):
        return pl.BlockSpec(
            (1, parts, rows, width), lambda c, s, at: (jnp.where(c == 0, s, chips - 1), 0, 0, 0)
        )

    def got_spec(width):
        return pl.BlockSpec(
            (1, parts, rows, width), lambda c, s, at: (jnp.where(c == 0, 0, s), 0, 0, 0)
        )

    def whole_spec(width):
        return pl.BlockSpec(
            (1, parts, rows, width), lambda c, s, at: ((at[0] ^ c) * chips + (at[1] ^ s), 0, 0, 0)
        )

    (own_a, got_a), (own_b, got_b) = sums
    width_a, width_b = own_a.shape[-1], own_b.shape[-1]
    tail = extra_width + BLOCK
    finished = pl.pallas_call(
        finish_kernel,
        grid_spec=pltpu.PrefetchScalarGridSpec(
            num_scalar_prefetch=1,
            grid=(2, chips),
            in_specs=[
                own_spec(width_a),
                got_spec(width_a),
                own_spec(width_b),
                got_spec(width_b),
                whole_spec(3 * model),
            ],
            out_specs=[whole_spec(width) for width in (3 * model, model, BLOCK, tail)],
        ),
        out_shape=[
            shape((groups, parts, rows, width), f32) for width in (3 * model, model, BLOCK, tail)
        ],
        compiler_params=params(("arbitrary", "arbitrary")),
        cost_estimate=cost(1e8, 2e7),
        name="finish",
    )(where, own_a, got_a, own_b, got_b, w_qkv.reshape(groups, parts, rows, 3 * model))
    grad_w_qkv, grad_w_out, gain_sums, extras = [
        item.reshape(model, item.shape[-1]) for item in finished
    ]
    return (
        output,
        grad_tokens,
        gain_sums[:, 0] / gain_one,
        grad_w_qkv,
        grad_w_out,
        extras[:bucket_count, extra_width : extra_width + head_count],
        extras[:, experts],
        extras[:, :experts],
        grad_w_in,
        grad_w_back,
    )


def solution(mesh):
    return jax.shard_map(
        local,
        mesh=mesh,
        in_specs=(
            P(("expert", "hidden"), None),
            P(("expert", "hidden"), None),
            P(("expert", "hidden"), None),
            P(("expert", "hidden")),
            P(("expert", "hidden")),
            P(("expert", "hidden")),
            P(),
            P(),
            P(),
            P(),
            P(),
            P(),
            P("expert", None, "hidden"),
            P("expert", "hidden", None),
        ),
        out_specs=(
            P(("expert", "hidden"), None),
            P(("expert", "hidden"), None),
            P(),
            P(),
            P(),
            P(),
            P(),
            P(),
            P("expert", None, "hidden"),
            P("expert", "hidden", None),
        ),
        check_vma=False,
    )
```

```python
import functools

import jax
import jax.numpy as jnp
from jax import lax
from jax.experimental import pallas as pl
from jax.experimental.pallas import tpu as pltpu
from jax.sharding import PartitionSpec as P

eps = 1e-06
bucket_edges = (12, 16, 23, 32, 46, 64, 91)
highest = lax.Precision.HIGHEST
f32 = jnp.float32
bf16 = jnp.bfloat16
i32 = jnp.int32
BLOCK = 128
VMEM_BYTES = 56 << 20
NN = (((1,), (0,)), ((), ()))
NT = (((1,), (1,)), ((), ()))
TN = (((0,), (0,)), ((), ()))


def mm(left, right, dims=NN):
    return lax.dot_general(left, right, dims, preferred_element_type=f32)


def mm_exact(left, right, dims=NN):
    return lax.dot_general(left, right, dims, precision=highest, preferred_element_type=f32)


def split(values):
    high = values.astype(bf16)
    return high, (values - high.astype(f32)).astype(bf16)


def params(semantics=None):
    if semantics is None:
        return pltpu.CompilerParams(vmem_limit_bytes=VMEM_BYTES)
    return pltpu.CompilerParams(vmem_limit_bytes=VMEM_BYTES, dimension_semantics=semantics)


def cost(flops, moved):
    return pl.CostEstimate(
        flops=int(flops) // 100, bytes_accessed=int(moved) // 100, transcendentals=0
    )


def bucket_of(offset):
    distance = jnp.abs(offset)
    coarse = jnp.full_like(distance, 8)
    for edge_value in bucket_edges:
        coarse = coarse + (distance >= edge_value).astype(i32)
    return jnp.where(distance < 8, distance, coarse) + 16 * (offset > 0).astype(i32)


def one_hot(mask):
    return mask.astype(f32).astype(bf16)


def lane_numbers(rows, width):
    return lax.broadcasted_iota(i32, (rows, width), 1)


def place_kernel(routes_ref, slot_ref, kept_ref, seg_ref, bias_ref, row_ref, col_ref, diag_ref, *, capacity, local_experts):
    tokens = seg_ref.shape[1]
    routes = routes_ref[...]
    seat = (routes // local_experts) * capacity + slot_ref[...]
    kept = kept_ref[...] == 1
    line = lax.broadcasted_iota(i32, (BLOCK, tokens), 0)
    stacked = jnp.where(line == local_experts, routes, 0)
    stacked = jnp.where(line == local_experts + 1, seg_ref[...], stacked)
    for le in range(local_experts):
        key = jnp.where(kept & (routes % local_experts == le), seat, -1)
        stacked = jnp.where(line == le, key, stacked)
    row_ref[...] = stacked[: row_ref.shape[0]]
    col_ref[...] = stacked.T
    buckets = bias_ref.shape[0]
    offset = lane_numbers(buckets, 4 * BLOCK) - 2 * BLOCK
    pick = bucket_of(offset) == lax.broadcasted_iota(i32, (buckets, 4 * BLOCK), 0)
    diag_ref[...] = mm_exact(bias_ref[...], pick.astype(f32), TN)


def slots_kernel(place_ref, *refs, parts, le):
    key_refs = refs[:parts]
    rows_ref, out_ref = refs[parts:]
    direct = len(out_ref.shape) == 4
    slots = out_ref.shape[0] * out_ref.shape[2] if direct else out_ref.shape[1]
    tokens = rows_ref.shape[1]
    for j in range(parts):
        whole = (place_ref[0] + j) % parts
        key = key_refs[j][le : le + 1, :]
        table = lax.broadcasted_iota(i32, (slots, tokens), 0) == key
        rows = mm(one_hot(table), rows_ref[whole])
        if direct:
            by_group(rows, out_ref, whole)
        else:
            out_ref[whole] = rows.astype(bf16)


def by_group(rows, out_ref, place):
    capacity = out_ref.shape[2]
    for group in range(out_ref.shape[0]):
        piece = rows[group * capacity : (group + 1) * capacity]
        out_ref[group, place] = piece.astype(bf16)


def qkv_kernel(tok_ref, gain_ref, w_ref, qkv_ref, turned_ref, low_ref):
    @pl.when(pl.program_id(0) == 0)
    def _():
        values = tok_ref[...].astype(f32)
        inverse = lax.rsqrt(jnp.mean(values * values, axis=-1, keepdims=True) + eps)
        normed = values * inverse * gain_ref[...]
        low_ref[...] = normed.astype(bf16)
        turned_ref[...] = normed.T.astype(bf16)

    qkv_ref[...] = mm(low_ref[...], w_ref[...]).astype(bf16)


def attend_kernel(q_ref, k_ref, v_ref, row_ids_ref, cols_ref, diag_ref, att_ref, probs_ref, *, seg_line, head_start):
    length = k_ref.shape[0]
    blocks = length // BLOCK
    lane = lane_numbers(1, BLOCK)
    half = BLOCK // 2
    scale = half**-0.5
    keys = k_ref[...]
    vals = v_ref[...]
    row_ids = row_ids_ref[seg_line : seg_line + 1, :]
    bias_tiles = []
    for s in range(2):
        diag = diag_ref[pl.ds(head_start + 2 * pl.program_id(0) + s, 1), :]
        spread = jnp.broadcast_to(diag, (BLOCK, 4 * BLOCK))
        tile = pltpu.roll(spread, 0, 1, stride=1, stride_axis=0)[:, BLOCK:].T
        low_far = jnp.broadcast_to(diag[:, 1:2], (BLOCK, BLOCK))
        high_far = jnp.broadcast_to(diag[:, 4 * BLOCK - 1 :], (BLOCK, BLOCK))
        bias_tiles.append((low_far, tile, high_far))
    turned_vals = vals.astype(f32).T.astype(bf16)
    upper = lax.broadcasted_iota(i32, (BLOCK, 1), 0) < half
    for i in range(blocks):
        rows = slice(i * BLOCK, (i + 1) * BLOCK)
        same = cols_ref[:, seg_line : seg_line + 1] == row_ids[:, rows]
        queries = q_ref[rows, :]
        outs = []
        for s in range(2):
            mask = jnp.where(lane // half == s, scale, 0.0).astype(bf16)
            scores = mm(keys, queries * mask, NT)
            low_far, tile, high_far = bias_tiles[s]
            pieces = []
            for j in range(blocks):
                if j - i < -1:
                    pieces.append(low_far)
                elif j - i > 1:
                    pieces.append(high_far)
                else:
                    start = (j - i + 1) * BLOCK
                    pieces.append(tile[start : start + BLOCK])
            scores = scores + jnp.concatenate(pieces, axis=0)
            scores = jnp.where(same, scores, -1000000000.0)
            top = jnp.max(scores, axis=0, keepdims=True)
            grown = jnp.exp(scores - top)
            probs = (grown * (1.0 / jnp.sum(grown, axis=0, keepdims=True))).astype(bf16)
            probs_ref[s, :, rows] = probs
            outs.append(mm(turned_vals, probs))
        att_ref[rows, :] = jnp.where(upper, outs[0], outs[1]).T.astype(bf16)


def chosen_of(router, cols_ref, line):
    pick = cols_ref[:, line : line + 1] == lane_numbers(*router.shape)
    return pick, jnp.sum(jnp.where(pick, router, 0.0), axis=-1, keepdims=True)


def route_kernel(tok_ref, att_a_ref, att_b_ref, w_out_ref, gain_ref, w_router_ref, rows_ref, residual_ref, router_ref, sent_ref):
    near = att_a_ref.shape[1]
    branch = mm(att_a_ref[...], w_out_ref[:near]) + mm(att_b_ref[...], w_out_ref[near:])
    residual = tok_ref[...].astype(f32) + branch
    residual_ref[...] = residual
    inverse = lax.rsqrt(jnp.mean(residual * residual, axis=-1, keepdims=True) + eps)
    normed = residual * inverse * gain_ref[...]
    low = normed.astype(bf16)
    tokens = low.shape[0]
    direct = len(sent_ref.shape) == 4
    local_experts = sent_ref.shape[1] if direct else sent_ref.shape[0]
    slots = sent_ref.shape[0] * sent_ref.shape[2] if direct else sent_ref.shape[1]
    for index in range(local_experts):
        table = lax.broadcasted_iota(i32, (slots, tokens), 0) == rows_ref[index : index + 1, :]
        rows = mm(one_hot(table), low)
        if direct:
            by_group(rows, sent_ref, index)
        else:
            sent_ref[index] = rows.astype(bf16)
    w_high, w_low = split(w_router_ref[...])
    low_rest = (normed - low.astype(f32)).astype(bf16)
    experts = w_high.shape[1]
    logits = mm(low, jnp.concatenate([w_high, w_low], axis=1))
    logits = logits[:, :experts] + logits[:, experts:] + mm(low_rest, w_high)
    top = jnp.max(logits, axis=-1, keepdims=True)
    grown = jnp.exp(logits - top)
    router = grown / jnp.sum(grown, axis=-1, keepdims=True)
    router_ref[...] = router


def expert_kernel(place_ref, x_ref, cot_ref, w_in_ref, w_back_ref, *refs, parts, le, groups, order, olds):
    count = len(order)
    refs = refs[olds:]
    back_refs = refs[:count]
    act_ref, gp_ref = refs[count : count + 2]
    x_buf, g_buf, w_in_buf, w_back_buf, act_buf, gp_buf, back_buf = refs[count + 2 : -4]
    x_sem, g_sem, w_sem, put_sem = refs[-4:]
    place = place_ref[0]
    whole = [(place + j) % parts for j in order]
    load_in = pltpu.make_async_copy(w_in_ref.at[le], w_in_buf, w_sem.at[0])
    load_back = pltpu.make_async_copy(w_back_ref.at[le], w_back_buf, w_sem.at[1])
    load_in.start()
    loads = []
    for at in range(count):
        loads.append(
            (
                pltpu.make_async_copy(x_ref.at[whole[at]], x_buf.at[at], x_sem.at[at]),
                pltpu.make_async_copy(cot_ref.at[whole[at]], g_buf.at[at], g_sem.at[at]),
            )
        )
        loads[at][0].start()
    load_back.start()
    for at in range(count):
        loads[at][1].start()
    load_in.wait()
    scale = (2.0 / jnp.pi) ** 0.5
    slots, model = x_buf.shape[1:]
    hidden = act_buf.shape[2]
    spare = back_buf.shape[1] - slots
    line = lax.broadcasted_iota(i32, (spare, BLOCK), 0)
    capacity = slots // groups
    puts = []

    def put(source, target, kind, at):
        copy = pltpu.make_async_copy(source, target, put_sem.at[kind, at])
        copy.start()
        puts.append(copy)

    span = 2
    for first in range(0, count, span):
        ats = range(first, first + span)
        for at in ats:
            loads[at][0].wait()
        pre = mm(x_buf[first : first + span].reshape(span * slots, model), w_in_buf[...])
        for at in ats:
            loads[at][1].wait()
        if first == 0:
            load_back.wait()
        grad = mm(g_buf[first : first + span].reshape(span * slots, model), w_back_buf[...], NT)
        square = pre * pre
        slant = jnp.tanh(scale * pre * (1.0 + 0.044715 * square))
        act = (0.5 * pre * (1.0 + slant)).astype(bf16)
        act_buf[first : first + span] = act.reshape(span, slots, hidden)
        slope = 0.5 * (1.0 + slant) + 0.5 * pre * (1.0 - slant * slant) * (
            scale * (1.0 + 3.0 * 0.044715 * square)
        )
        gp = (grad * slope).astype(bf16)
        gp_buf[first : first + span] = gp.reshape(span, slots, hidden)
        back = mm(gp, w_in_buf[...], NT).astype(bf16)
        back_buf[first : first + span, :slots] = back.reshape(span, slots, model)
        all_dots = jnp.sum(act.astype(f32) * grad, axis=-1, keepdims=True)
        for at in ats:
            put(act_buf.at[at], act_ref.at[whole[at]], 0, at)
            put(gp_buf.at[at], gp_ref.at[whole[at]], 1, at)
            dots = all_dots[(at - first) * slots : (at - first + 1) * slots]
            dots = jnp.broadcast_to(dots, (slots, BLOCK)).T
            laid = jnp.zeros((spare, BLOCK), f32)
            for group in range(groups):
                piece = dots[:1, group * capacity : (group + 1) * capacity]
                piece = jnp.concatenate([piece, jnp.zeros((1, BLOCK - capacity), f32)], axis=1)
                laid = jnp.where(line == group, piece, laid)
            back_buf[at, slots:] = jnp.zeros((spare, model), bf16)
            back_buf[at, slots:, :BLOCK] = laid.astype(bf16)
            put(back_buf.at[at], back_refs[at], 2, at)
    for copy in puts:
        copy.wait()


def expert_weights_kernel(own_ref, x_ref, act_ref, cot_ref, gp_ref, w_router_ref, all_act_ref, w_back_ref, *refs, le, local_experts):
    in_ref, back_ref, out_ref, gs_ref, gate_ref, turned_ref = refs[-6:]
    parts = x_ref.shape[0]

    def flat(values):
        return values.reshape(-1, values.shape[-1])

    @pl.when(pl.program_id(0) == 0)
    def _():
        w_high, w_low = split(w_router_ref[...])
        number = own_ref[0] * local_experts + le
        for part in range(parts):
            rows = x_ref[part]
            logits = mm(rows, w_high) + mm(rows, w_low)
            grown = jnp.exp(logits - jnp.max(logits, axis=-1, keepdims=True))
            pick = lane_numbers(*logits.shape) == number
            gate = jnp.sum(jnp.where(pick, grown, 0.0), axis=-1, keepdims=True)
            gate = gate / jnp.sum(grown, axis=-1, keepdims=True)
            gate_ref[part] = gate
            gs_ref[part] = (cot_ref[part].astype(f32) * gate).astype(bf16)
        turned_ref[...] = flat(x_ref[...]).T

    gp = (gp_ref[...].astype(f32) * gate_ref[...]).astype(bf16)
    in_ref[0] = mm(turned_ref[...], flat(gp))
    back_ref[0] = mm(flat(act_ref[...]), flat(gs_ref[...]), TN)
    out = mm(flat(all_act_ref[...]), w_back_ref[0]).astype(bf16)
    out_ref[:, 0] = out.reshape(parts, -1, out.shape[-1])


def middle_kernel(residual_ref, cot_ref, gain_ref, w_router_ref, router_ref, cols_ref, w_out_ref, *refs, capacity, stride):
    grad_res_ref, branch_ref, att_ref, extra_ref = refs[-4:]
    back_refs = refs[:-4]
    local_experts = len(back_refs)
    tokens = residual_ref.shape[0]
    rows = None
    grad_gate = None
    for index, back_ref in enumerate(back_refs):
        key = cols_ref[:, index : index + 1]
        group = key // capacity
        number = lane_numbers(tokens, back_ref.shape[0])
        back = back_ref[...]
        part = mm(one_hot(number == key + group * (stride - capacity)), back)
        lines = mm(one_hot(number == group * stride + capacity), back[:, :BLOCK])
        slot = lane_numbers(tokens, BLOCK) == key - group * capacity
        picked = jnp.sum(jnp.where(slot, lines, 0.0), axis=-1, keepdims=True)
        rows = part if rows is None else rows + part
        grad_gate = picked if grad_gate is None else grad_gate + picked
    router = router_ref[...]
    pick, chosen = chosen_of(router, cols_ref, local_experts)
    grad_logits = router * (pick.astype(f32) - chosen) * grad_gate
    residual = residual_ref[...]
    inverse = lax.rsqrt(jnp.mean(residual * residual, axis=-1, keepdims=True) + eps)
    gain = gain_ref[...]
    scaled = residual * inverse
    logits_high, logits_low = split(grad_logits)
    w_high, w_low = split(w_router_ref[...])
    grad_normed = chosen * rows + mm(
        jnp.concatenate([logits_high, logits_low, logits_high], axis=1),
        jnp.concatenate([w_high, w_high, w_low], axis=1),
        NT,
    )
    weighted = grad_normed * gain
    lean = jnp.mean(weighted * residual, axis=-1, keepdims=True)
    grad_res = cot_ref[...].astype(f32) + (
        inverse * weighted - residual * (inverse * inverse * inverse) * lean
    )
    grad_res_ref[...] = grad_res
    low = grad_res.astype(bf16)
    branch_ref[...] = low
    att_ref[...] = mm(low, w_out_ref[...], NT).astype(bf16)
    gain_grad = jnp.sum(grad_normed * scaled, axis=0, keepdims=True)
    normed_high, normed_low = split(scaled * gain)
    experts = logits_high.shape[1]
    router_grad = mm(jnp.concatenate([logits_high, logits_low], axis=1), normed_high, TN)
    router_grad = router_grad[:experts] + router_grad[experts:] + mm(logits_high, normed_low, TN)
    spare = extra_ref.shape[1] - router_grad.shape[0] - 1
    both = jnp.concatenate(
        [router_grad, gain_grad, jnp.zeros((spare, gain_grad.shape[1]), f32)], axis=0
    )
    extra_ref[...] = both.T.astype(bf16)


def attend_back_kernel(q_ref, k_ref, v_ref, probs_ref, grad_ref, turned_ref, *refs, kind, head_start, buckets):
    if kind == 0:
        att_a_ref, att_b_ref, branch_ref, extra_ref = refs[:4]
    else:
        old_diag_ref = refs[0]
    if kind == 2:
        old_weight_ref = refs[1]
    dq_ref, dk_ref, dv_ref, weight_ref, diag_ref, slope_ref = refs[-6:]
    step = pl.program_id(0)
    length = k_ref.shape[0]
    blocks = length // BLOCK
    lane = lane_numbers(1, BLOCK)
    half = BLOCK // 2
    scale = half**-0.5
    keys = k_ref[...]
    vals = v_ref[...]
    queries = q_ref[...]
    grads = grad_ref[...]
    static_columns = weight_ref.shape[1]

    @pl.when(step == 0)
    def _():
        if kind == 0:
            diag_ref[...] = jnp.zeros_like(diag_ref)
            model = branch_ref.shape[1]
            tail = extra_ref.shape[1]
            begin = static_columns - tail - model
            near = att_a_ref.shape[1]
            branch = branch_ref[...]
            weight_ref[:near, begin : begin + model] = mm(att_a_ref[...], branch, TN).astype(bf16)
            weight_ref[near:, begin : begin + model] = mm(att_b_ref[...], branch, TN).astype(bf16)
            weight_ref[:, begin + model :] = extra_ref[...]
        else:
            diag_ref[...] = old_diag_ref[...]
        if kind == 2:
            weight_ref[:, : old_weight_ref.shape[1]] = old_weight_ref[...]

    across = lax.broadcasted_iota(i32, (BLOCK, BLOCK), 0) + lane_numbers(BLOCK, BLOCK)
    flip = (across == BLOCK - 1).astype(f32)
    turned_keys = keys.astype(f32).T.astype(bf16)
    dq = [[] for _ in range(blocks)]
    dk, dv = [], []
    for s in range(2):
        mask = jnp.where(lane // half == s, 1.0, 0.0).astype(bf16)
        near = [None, None, None]
        far = [None, None]
        for i in range(blocks):
            rows = slice(i * BLOCK, (i + 1) * BLOCK)
            probs = probs_ref[s, :, rows].astype(f32)
            grad_probs = mm(vals, grads[rows] * mask, NT)
            delta = jnp.sum(probs * grad_probs, axis=0, keepdims=True)
            slope = probs * (grad_probs - delta)
            low = slope.astype(bf16)
            slope_ref[:, rows] = low
            dq[i].append(mm(turned_keys, low))
            for j in range(blocks):
                piece = slope[j * BLOCK : (j + 1) * BLOCK]
                apart = j - i
                if abs(apart) <= 1:
                    old = near[1 - apart]
                    near[1 - apart] = piece if old is None else old + piece
                else:
                    old = far[int(apart > 0)]
                    far[int(apart > 0)] = piece if old is None else old + piece
        dk.append(mm(slope_ref[...], queries))
        dv.append(mm(probs_ref[s], grads))
        wide = jnp.concatenate([jnp.zeros_like(near[0])] + near, axis=1)
        lined = pltpu.roll(mm_exact(flip, wide), 3 * BLOCK + 1, 1, stride=1, stride_axis=0)
        lined = jnp.concatenate([lined, far[0], far[1]], axis=1)
        diag_ref[pl.ds(head_start + 2 * step + s, 1), :] = jnp.sum(lined, axis=0, keepdims=True)
    upper = lax.broadcasted_iota(i32, (BLOCK, 1), 0) < half
    dq_low = jnp.concatenate([jnp.where(upper, *item).T for item in dq], axis=0)
    dq_low = (dq_low * scale).astype(bf16)
    left = lane < half
    dk_low = (jnp.where(left, dk[0], dk[1]) * scale).astype(bf16)
    dv_low = jnp.where(left, dv[0], dv[1]).astype(bf16)
    dq_ref[...] = dq_low
    dk_ref[...] = dk_low
    dv_ref[...] = dv_low
    begin = 0 if kind < 2 else old_weight_ref.shape[1]
    begin = pl.multiple_of(step * (3 * BLOCK) + begin, 3 * BLOCK)
    weight_ref[:, pl.ds(begin, 3 * BLOCK)] = mm(
        turned_ref[...], jnp.concatenate([dq_low, dk_low, dv_low], axis=1)
    ).astype(bf16)
    if kind == 2:

        @pl.when(step == pl.num_programs(0) - 1)
        def _():
            wide = diag_ref.shape[1]
            number = lane_numbers(buckets, wide)
            bucket = bucket_of(2 * BLOCK - number)
            bucket = jnp.where(number >= 4 * BLOCK, 15, bucket)
            bucket = jnp.where(number >= 5 * BLOCK, 31, bucket)
            pick = bucket == lax.broadcasted_iota(i32, (buckets, wide), 0)
            rows = jnp.concatenate(
                [diag_ref[...], jnp.zeros((BLOCK - diag_ref.shape[0], wide), f32)], axis=0
            )
            bias = mm_exact(pick.astype(f32), rows, NT)
            begin = static_columns - BLOCK
            weight_ref[:, begin:] = jnp.zeros((weight_ref.shape[0], BLOCK), bf16)
            weight_ref[:buckets, begin:] = bias.astype(bf16)


def tokens_kernel(tok_ref, gain_ref, w_ref, grad_res_ref, *refs):
    out_ref = refs[-1]
    parts = refs[:-1]
    groups = len(parts) // 3
    model = tok_ref.shape[1]
    grad_normed = None
    for part in range(3):
        start = part * model
        for group in range(groups):
            block = parts[3 * group + part]
            width = block.shape[1]
            piece = mm(block[...], w_ref[:, start : start + width], NT)
            grad_normed = piece if grad_normed is None else grad_normed + piece
            start += width
    values = tok_ref[...].astype(f32)
    inverse = lax.rsqrt(jnp.mean(values * values, axis=-1, keepdims=True) + eps)
    weighted = grad_normed * gain_ref[...]
    lean = jnp.mean(weighted * values, axis=-1, keepdims=True)
    out_ref[...] = grad_res_ref[...] + (
        inverse * weighted - values * (inverse * inverse * inverse) * lean
    )


def output_kernel(residual_ref, router_ref, cols_ref, rows_ref, out_ref):
    tokens = residual_ref.shape[0]
    local_experts, slots = rows_ref.shape[:2]
    mixture = None
    for index in range(local_experts):
        turned = cols_ref[:, index : index + 1] == lane_numbers(tokens, slots)
        part = mm(one_hot(turned), rows_ref[index])
        mixture = part if mixture is None else mixture + part
    _, chosen = chosen_of(router_ref[...], cols_ref, local_experts)
    out_ref[...] = (residual_ref[...] + chosen * mixture).astype(bf16)


def finish_kernel(where_ref, a_ref, b_ref, w_ref, *refs):
    qkv_ref, out_ref, gain_ref, extra_ref = refs[-4:]
    place = where_ref[2]
    parts = a_ref.shape[1]
    model = out_ref.shape[3]
    pairs = model // BLOCK
    near = pairs // 3
    for k in range(parts):
        z = (place + parts - k) % parts
        a = a_ref[0, k].astype(f32)
        b = b_ref[0, k].astype(f32)
        total = None
        for part in range(3):
            pieces = [
                (a if p < near else b)[:, ((p if p < near else p - near) * 3 + part) * BLOCK :][
                    :, :BLOCK
                ]
                for p in range(pairs)
            ]
            whole = jnp.concatenate(pieces, axis=1)
            span = slice(part * model, (part + 1) * model)
            qkv_ref[0, z, :, span] = whole
            w = w_ref[0, z, :, span].astype(f32)
            share = jnp.sum(whole * w, axis=-1, keepdims=True)
            total = share if total is None else total + share
        gain_ref[0, z] = jnp.broadcast_to(total, gain_ref.shape[2:])
        begin = near * 3 * BLOCK
        out_ref[0, z] = a[:, begin : begin + model]
        tail = a.shape[1] - begin - model
        extra_ref[0, z, :, :tail] = a[:, begin + model :]
        extra_ref[0, z, :, tail:] = b[:, (pairs - near) * 3 * BLOCK :]


def add_low(left, right):
    return (left.astype(f32) + right.astype(f32)).astype(bf16)


def tie(items, after):
    return lax.optimization_barrier((items, after))[0]


def held(kernel, start, after):
    def body(*refs):
        kernel(*refs[:start], *refs[start + len(after) :])

    return body


class Scatter:
    def __init__(self, blocks):
        self.parts = lax.axis_size("hidden")
        self.blocks = blocks
        self.count = 0

    def step(self, after=()):
        self.count += 1
        right, left = self.blocks[self.parts - self.count], self.blocks[self.count]
        if self.count > 1:
            right, left = add_low(right, self.right), add_low(left, self.left)
        right, left = tie((right, left), after)
        ways = [(a, a + 1) for a in range(self.count)]
        self.right = lax.ppermute(right, "hidden", ways)
        ways = [(a, a - 1) for a in range(self.parts - self.count, self.parts)]
        self.left = lax.ppermute(left, "hidden", ways)

    def last(self):
        return self.right, self.left

    def finish(self, after=()):
        right, left = tie(self.last(), after)
        total = self.blocks[0].astype(f32) + right.astype(f32) + left.astype(f32)
        return total.astype(bf16)


def pick_block(blocks, index):
    return lax.dynamic_index_in_dim(blocks, index, 0, keepdims=False)


class Sum:
    def __init__(self, values):
        self.groups = lax.axis_size("expert")
        self.parts = lax.axis_size("hidden")
        self.own = lax.axis_index("expert")
        self.place = lax.axis_index("hidden")
        self.core = self.own % 2
        self.chip = self.own // 2
        self.chips = self.groups // 2
        self.pair = [(a, a ^ 1) for a in range(self.groups)]
        self.width = values.shape[1]
        self.values = values

    def cores(self):
        halves = self.values.reshape(2, -1, self.width)
        got = lax.ppermute(pick_block(halves, 1 - self.core), "expert", self.pair)
        self.values = add_low(pick_block(halves, self.core), got)

    def cores_at_once(self):
        teams = [[2 * a, 2 * a + 1] for a in range(self.chips)]
        got = lax.all_to_all(
            self.values, "expert", split_axis=0, concat_axis=0, tiled=True, axis_index_groups=teams
        ).reshape(2, -1, self.width)
        self.values = add_low(got[0], got[1])

    def plane(self):
        pieces = self.values.reshape(self.chips, -1, self.width)
        total = pick_block(pieces, self.chip).astype(f32)
        for step in range(1, self.chips):
            ways = [(a, a ^ (2 * step)) for a in range(self.groups)]
            got = lax.ppermute(pick_block(pieces, self.chip ^ step), "expert", ways)
            total = total + got.astype(f32)
        self.values = total.astype(bf16)

    def line(self):
        pieces = self.values.reshape(self.parts, -1, self.width)
        total = pick_block(pieces, self.place).astype(f32)
        for step in range(1, self.parts):
            ways = [(a, (a + step) % self.parts) for a in range(self.parts)]
            got = lax.ppermute(pick_block(pieces, (self.place + step) % self.parts), "hidden", ways)
            total = total + got.astype(f32)
        self.values = total.astype(bf16)

    def line_back(self):
        pieces = [self.values]
        for step in range(1, self.parts):
            ways = [(a, (a + step) % self.parts) for a in range(self.parts)]
            pieces.append(lax.ppermute(self.values, "hidden", ways))
        self.values = jnp.stack(pieces)

    def plane_back(self):
        pieces = [self.values]
        for step in range(1, self.chips):
            ways = [(a, a ^ (2 * step)) for a in range(self.groups)]
            pieces.append(lax.ppermute(self.values, "expert", ways))
        self.values = jnp.stack(pieces)

    def cores_back(self):
        return self.values, lax.ppermute(self.values, "expert", self.pair)

    def run(self):
        self.cores()
        self.plane()
        self.line()
        self.line_back()
        self.plane_back()
        return self.cores_back()


def local(tokens, cotangent, segments, routes, slot_ids, kept_flags, gain_one, w_qkv, w_out, bias_table, gain_two, w_router, w_in, w_back):
    tok_rows, model = tokens.shape
    bucket_count, head_count = bias_table.shape
    experts = w_router.shape[1]
    local_experts = w_in.shape[0]
    hidden = w_in.shape[2]
    groups = lax.axis_size("expert")
    parts = lax.axis_size("hidden")
    own = lax.axis_index("expert")
    place = lax.axis_index("hidden")
    capacity = max(2, (5 * tok_rows + 4 * experts - 1) // (4 * experts))
    slots = groups * capacity
    pairs = head_count // 2
    shape = jax.ShapeDtypeStruct
    vmem = pl.BlockSpec(memory_space=pltpu.VMEM)
    any_space = pl.BlockSpec(memory_space=pl.ANY)
    gain_one_row = gain_one[None, :]
    gain_two_row = gain_two[None, :]
    seg_line = local_experts + 1

    def exchange(rows, axis=0):
        return lax.all_to_all(rows, "expert", split_axis=axis, concat_axis=axis, tiled=True)

    cot_near = lax.all_gather(cotangent, "hidden", axis=0, tiled=False)
    id_rows, id_cols, diag_bias = pl.pallas_call(
        functools.partial(place_kernel, capacity=capacity, local_experts=local_experts),
        out_shape=[
            shape((8, tok_rows), i32),
            shape((tok_rows, BLOCK), i32),
            shape((head_count, 4 * BLOCK), f32),
        ],
        in_specs=[vmem] * 5,
        out_specs=[vmem] * 3,
        compiler_params=params(),
        cost_estimate=cost(1e8, 1e6),
        name="place",
    )(routes[None, :], slot_ids[None, :], kept_flags[None, :], segments, bias_table)
    qkv, turned = pl.pallas_call(
        qkv_kernel,
        grid=(3,),
        out_shape=[shape((tok_rows, 3 * model), bf16), shape((model, tok_rows), bf16)],
        in_specs=[
            pl.BlockSpec((tok_rows, model), lambda j: (0, 0)),
            pl.BlockSpec((1, model), lambda j: (0, 0)),
            pl.BlockSpec((model, model), lambda j: (0, j)),
        ],
        out_specs=[
            pl.BlockSpec((tok_rows, model), lambda j: (0, j)),
            pl.BlockSpec((model, tok_rows), lambda j: (0, 0)),
        ],
        scratch_shapes=[pltpu.VMEM((tok_rows, model), bf16)],
        compiler_params=params(("arbitrary",)),
        cost_estimate=cost(6 * tok_rows * model * model, 8 * model * model * 2),
        name="qkv",
    )(tokens, gain_one_row, w_qkv)

    def pair_spec(offset):
        return pl.BlockSpec((tok_rows, BLOCK), lambda p: (0, offset + p))

    steps = pairs // 2
    attended, probs = [], []
    for half in range(2):
        start = half * steps
        att, prob = pl.pallas_call(
            functools.partial(attend_kernel, seg_line=seg_line, head_start=2 * start),
            grid=(steps,),
            out_shape=[
                shape((tok_rows, steps * BLOCK), bf16),
                shape((2 * steps, tok_rows, tok_rows), bf16),
            ],
            in_specs=[
                pair_spec(start),
                pair_spec(pairs + start),
                pair_spec(2 * pairs + start),
                pl.BlockSpec((8, tok_rows), lambda p: (0, 0)),
                pl.BlockSpec((tok_rows, BLOCK), lambda p: (0, 0)),
                pl.BlockSpec((head_count, 4 * BLOCK), lambda p: (0, 0)),
            ],
            out_specs=[
                pair_spec(0),
                pl.BlockSpec((2, tok_rows, tok_rows), lambda p: (p, 0, 0)),
            ],
            compiler_params=params(("arbitrary",)),
            cost_estimate=cost(steps * 4e9, steps * 3e6),
            name="attend",
        )(qkv, qkv, qkv, id_rows, id_cols, diag_bias)
        attended.append(att)
        probs.append(prob)

    def by_slots(count):
        if direct:
            return shape((groups, count, capacity, model), bf16)
        return shape((count, slots, model), bf16)

    direct = capacity % 8 == 0
    residual, router, sent_rows = pl.pallas_call(
        route_kernel,
        out_shape=[
            shape((tok_rows, model), f32),
            shape((tok_rows, experts), f32),
            by_slots(local_experts),
        ],
        in_specs=[vmem] * 7,
        out_specs=[vmem] * 3,
        compiler_params=params(),
        cost_estimate=cost(6e9, 6e6),
        name="route",
    )(tokens, *attended, w_out, gain_two_row, w_router, id_rows)

    place_arr = place.astype(i32).reshape(1)
    own_arr = own.astype(i32).reshape(1)
    spare = -(-groups // 16) * 16
    block = shape((slots + spare, model), bf16)
    stack = shape((parts, slots, hidden), bf16)
    smem = pl.BlockSpec(memory_space=pltpu.SMEM)
    third = hidden // 3

    def run_experts(le, order, olds, after=()):
        count = len(order)
        results = pl.pallas_call(
            held(
                functools.partial(
                    expert_kernel, parts=parts, le=le, groups=groups, order=order, olds=len(olds)
                ),
                5 + len(olds),
                after,
            ),
            out_shape=[block] * count + [stack, stack],
            in_specs=[smem] + [any_space] * (4 + len(olds) + len(after)),
            out_specs=[any_space] * (count + 2),
            input_output_aliases={5 + n: count + n for n in range(len(olds))},
            scratch_shapes=[
                pltpu.VMEM((count, slots, model), bf16),
                pltpu.VMEM((count, slots, model), bf16),
                pltpu.VMEM((model, hidden), bf16),
                pltpu.VMEM((hidden, model), bf16),
                pltpu.VMEM((count, slots, hidden), bf16),
                pltpu.VMEM((count, slots, hidden), bf16),
                pltpu.VMEM((count, slots + spare, model), bf16),
                pltpu.SemaphoreType.DMA((count,)),
                pltpu.SemaphoreType.DMA((count,)),
                pltpu.SemaphoreType.DMA((2,)),
                pltpu.SemaphoreType.DMA((3, count)),
            ],
            compiler_params=params(),
            cost_estimate=cost(4 * count * slots * model * hidden, 1e7),
            name="experts",
        )(place_arr, rows_all[le], cot_all[le], w_in, w_back, *olds, *after)
        return results[:count], list(results[count:])

    def run_both(le, after=()):
        ends = list(range(1, parts, 2))
        rest = list(range(0, parts, 2))
        backs = [None] * parts
        some, kept = run_experts(le, ends, [], after)
        for j, item in zip(ends, some):
            backs[j] = item
        some, kept = run_experts(le, rest, kept)
        for j, item in zip(rest, some):
            backs[j] = item
        return backs, kept

    def run_weights(le, kept, olds, after):
        act, gp = kept
        stack_spec = pl.BlockSpec((parts, slots, model), lambda j: (0, 0, 0))
        hidden_spec = pl.BlockSpec((parts, slots, third), lambda j: (0, 0, j))
        return pl.pallas_call(
            held(
                functools.partial(expert_weights_kernel, le=le, local_experts=local_experts),
                8 + len(olds),
                after,
            ),
            grid=(3,),
            out_shape=[
                shape((local_experts, model, hidden), f32),
                shape((local_experts, hidden, model), f32),
                shape((parts, local_experts, slots, model), bf16),
            ],
            in_specs=[
                smem,
                stack_spec,
                hidden_spec,
                stack_spec,
                hidden_spec,
                pl.BlockSpec((model, experts), lambda j: (0, 0)),
                pl.BlockSpec((parts, slots, hidden), lambda j: (0, 0, 0)),
                pl.BlockSpec((1, hidden, model // 3), lambda j: (le, 0, j)),
            ]
            + [any_space] * (len(olds) + len(after)),
            out_specs=[
                pl.BlockSpec((1, model, third), lambda j: (le, 0, j)),
                pl.BlockSpec((1, third, model), lambda j: (le, j, 0)),
                pl.BlockSpec((parts, 1, slots, model // 3), lambda j: (0, le, 0, j)),
            ],
            scratch_shapes=[
                pltpu.VMEM((parts, slots, model), bf16),
                pltpu.VMEM((parts, slots, 1), f32),
                pltpu.VMEM((model, parts * slots), bf16),
            ],
            input_output_aliases={8 + n: n for n in range(len(olds))},
            compiler_params=params(("arbitrary",)),
            cost_estimate=cost(4 * parts * slots * model * hidden, 1.3e7),
            name="expert_weights",
        )(own_arr, rows_all[le], act, cot_all[le], gp, w_router, act, w_back, *olds, *after)

    def own_slots(le, ids, after):
        return pl.pallas_call(
            held(functools.partial(slots_kernel, parts=parts, le=le), 2 + parts, after),
            out_shape=by_slots(parts),
            in_specs=[smem] + [vmem] * (parts + 1) + [any_space] * len(after),
            out_specs=vmem,
            compiler_params=params(),
            cost_estimate=cost(2e9, 6e6),
            name="slots",
        )(place_arr, *ids, cot_near, *after)

    def exchange_slots(rows):
        if not direct:
            return exchange(rows, 1)
        return exchange(rows).transpose(1, 0, 2, 3).reshape(-1, slots, model)

    here = exchange_slots(sent_rows)
    rows_all = [
        lax.all_gather(here[le], "hidden", axis=0, tiled=False) for le in range(local_experts)
    ]
    ids = [id_rows]
    far_ids = tie(id_rows, here)
    for step in range(1, parts):
        ways = [((a + step) % parts, a) for a in range(parts)]
        ids.append(lax.ppermute(far_ids, "hidden", ways))
    cot_slots = [own_slots(0, ids, [here])]
    cot_slots.append(own_slots(1, ids, cot_slots))
    cot_all = [exchange_slots(cot_slots[0])]
    cot_all.append(exchange_slots(tie(cot_slots[1], cot_all[0])))
    backs, kept = run_both(0, cot_slots[1:])
    sum_first = Scatter(backs)
    sum_first.step()
    grads = run_weights(0, kept, [], [])
    sum_first.step(grads)
    backs, kept_second = run_both(1, grads[:1])
    sum_second = Scatter(backs)
    sum_second.step()
    sum_second.step(sum_first.last())
    sum_first.step()
    grads = run_weights(1, kept_second, grads, sum_second.last()[:1])

    def with_dots(total):
        rows = total[:slots].reshape(groups, capacity, model)
        dots = total[slots : slots + groups].reshape(groups, 1, model)
        dots = jnp.pad(dots, ((0, 0), (0, stride - capacity - 1), (0, 0)))
        return jnp.concatenate([rows, dots], axis=1).reshape(groups * stride, model)

    stride = -(-(capacity + 1) // 8) * 8
    back_first = exchange(with_dots(sum_first.finish()))
    sum_second.step(sum_first.last())
    back_second = sum_second.finish((back_first, grads))
    backs = [back_first, exchange(with_dots(back_second))]
    grad_w_in, grad_w_back, out_sums = grads
    extra_width = -(-(experts + 1) // BLOCK) * BLOCK

    grad_res, grad_branch, grad_att, extra = pl.pallas_call(
        functools.partial(middle_kernel, capacity=capacity, stride=stride),
        out_shape=[
            shape((tok_rows, model), f32),
            shape((tok_rows, model), bf16),
            shape((tok_rows, model), bf16),
            shape((model, extra_width), bf16),
        ],
        in_specs=[vmem] * (7 + local_experts),
        out_specs=[vmem] * 4,
        compiler_params=params(),
        cost_estimate=cost(6e9, 8e6),
        name="middle",
    )(residual, cotangent, gain_two_row, w_router, router, id_cols, w_out, *backs)

    out_rows = lax.psum_scatter(out_sums, "hidden", scatter_dimension=0, tiled=False)
    out_rows = out_rows.reshape(local_experts, groups, capacity, model).transpose(1, 0, 2, 3)
    out_ready = out_rows
    out_rows = exchange(out_rows).transpose(1, 0, 2, 3).reshape(local_experts, slots, model)
    output = pl.pallas_call(
        output_kernel,
        out_shape=shape((tok_rows, model), bf16),
        in_specs=[vmem] * 4,
        out_specs=vmem,
        compiler_params=params(),
        cost_estimate=cost(1e9, 4e6),
        name="output",
    )(residual, router, id_cols, out_rows)

    def run_back(kind, start, count, extras, width):
        inner = start % steps
        return pl.pallas_call(
            functools.partial(
                attend_back_kernel,
                kind=kind,
                head_start=2 * start,
                buckets=bucket_count,
            ),
            grid=(count,),
            out_shape=[shape((tok_rows, count * BLOCK), bf16)] * 3
            + [shape((model, width), bf16), shape((16, 6 * BLOCK), f32)],
            in_specs=[
                pair_spec(start),
                pair_spec(pairs + start),
                pair_spec(2 * pairs + start),
                pl.BlockSpec((2, tok_rows, tok_rows), lambda p: (inner + p, 0, 0)),
                pair_spec(start),
                pl.BlockSpec((model, tok_rows), lambda p: (0, 0)),
            ]
            + [pl.BlockSpec(item.shape, lambda p: (0, 0)) for item in extras],
            out_specs=[pair_spec(0)] * 3
            + [
                pl.BlockSpec((model, width), lambda p: (0, 0)),
                pl.BlockSpec((16, 6 * BLOCK), lambda p: (0, 0)),
            ],
            scratch_shapes=[pltpu.VMEM((tok_rows, tok_rows), bf16)],
            compiler_params=params(("arbitrary",)),
            cost_estimate=cost(count * 4e9, count * 3e6),
            name="attend_back",
        )(qkv, qkv, qkv, probs[start // steps], grad_att, turned, *extras)

    wide = 3 * BLOCK
    early = pairs // 3
    first = run_back(
        0, 0, early, [*attended, grad_branch, extra], wide * early + model + extra_width
    )
    sum_a = Sum(first[3])
    sum_a.cores()
    second = run_back(1, early, 1, [first[4]], wide)
    sum_a.values = tie(sum_a.values, second[3])
    sum_a.plane()
    third_part = run_back(
        2, early + 1, pairs - early - 1, [second[4], second[3]], wide * (pairs - early) + BLOCK
    )
    sum_b = Sum(tie(third_part[3], sum_a.values))
    sum_b.cores()
    grad_parts = [*first[:3], *second[:3], *third_part[:3]]
    grad_tokens = pl.pallas_call(
        held(tokens_kernel, 4 + len(grad_parts), [sum_b.values]),
        out_shape=shape((tok_rows, model), f32),
        in_specs=[vmem] * (4 + len(grad_parts)) + [any_space],
        out_specs=vmem,
        compiler_params=params(),
        cost_estimate=cost(3e9, 1e7),
        name="tokens_grad",
    )(tokens, gain_one_row, w_qkv, grad_res, *grad_parts, sum_b.values)
    sum_a.line()
    sum_b.plane()
    sum_b.values = tie(sum_b.values, (grad_tokens, out_ready))
    sum_a.line_back()
    sum_b.line()
    sum_a.plane_back()
    sum_b.line_back()
    sum_b.values = tie(sum_b.values, (sum_a.values, out_rows))
    sums = [sum_a.cores_back()]
    sum_b.plane_back()
    sum_b.values = tie(sum_b.values, output)
    sums.append(sum_b.cores_back())

    chips = groups // 2
    rows = model // (groups * parts)
    where = jnp.stack([own % 2, own // 2, place]).astype(i32)

    tail = extra_width + BLOCK
    widths = (3 * model, model, BLOCK, tail)

    def finish(team, a, b, olds):
        def piece_spec(width):
            return pl.BlockSpec((1, parts, rows, width), lambda s, at: (s, 0, 0, 0))

        def whole_spec(width):
            return pl.BlockSpec(
                (1, parts, rows, width),
                lambda s, at: ((at[0] ^ team) * chips + (at[1] ^ s), 0, 0, 0),
            )

        return pl.pallas_call(
            finish_kernel,
            grid_spec=pltpu.PrefetchScalarGridSpec(
                num_scalar_prefetch=1,
                grid=(chips,),
                in_specs=[
                    piece_spec(a.shape[-1]),
                    piece_spec(b.shape[-1]),
                    whole_spec(3 * model),
                ]
                + [any_space] * len(olds),
                out_specs=[whole_spec(width) for width in widths],
            ),
            out_shape=[shape((groups, parts, rows, width), f32) for width in widths],
            input_output_aliases={4 + n: n for n in range(len(olds))},
            compiler_params=params(("arbitrary",)),
            cost_estimate=cost(1e8, 1e7),
            name="finish",
        )(where, a, b, w_qkv.reshape(groups, parts, rows, 3 * model), *olds)

    (own_a, got_a), (own_b, got_b) = sums
    finished = finish(0, own_a, own_b, [])
    finished = finish(1, got_a, got_b, finished)
    grad_w_qkv, grad_w_out, gain_sums, extras = [
        item.reshape(model, item.shape[-1]) for item in finished
    ]
    return (
        output,
        grad_tokens,
        gain_sums[:, 0] / gain_one,
        grad_w_qkv,
        grad_w_out,
        extras[:bucket_count, extra_width : extra_width + head_count],
        extras[:, experts],
        extras[:, :experts],
        grad_w_in,
        grad_w_back,
    )


def solution(mesh):
    return jax.shard_map(
        local,
        mesh=mesh,
        in_specs=(
            P(("expert", "hidden"), None),
            P(("expert", "hidden"), None),
            P(("expert", "hidden"), None),
            P(("expert", "hidden")),
            P(("expert", "hidden")),
            P(("expert", "hidden")),
            P(),
            P(),
            P(),
            P(),
            P(),
            P(),
            P("expert", None, "hidden"),
            P("expert", "hidden", None),
        ),
        out_specs=(
            P(("expert", "hidden"), None),
            P(("expert", "hidden"), None),
            P(),
            P(),
            P(),
            P(),
            P(),
            P(),
            P("expert", None, "hidden"),
            P("expert", "hidden", None),
        ),
        check_vma=False,
    )
```

```python
import functools

import jax
import jax.numpy as jnp
from jax import lax
from jax.experimental import pallas as pl
from jax.experimental.pallas import tpu as pltpu
from jax.sharding import PartitionSpec as P

eps = 1e-06
bucket_edges = (12, 16, 23, 32, 46, 64, 91)
highest = lax.Precision.HIGHEST
f32 = jnp.float32
bf16 = jnp.bfloat16
i32 = jnp.int32
BLOCK = 128
VMEM_BYTES = 56 << 20
NN = (((1,), (0,)), ((), ()))
NT = (((1,), (1,)), ((), ()))
TN = (((0,), (0,)), ((), ()))


def mm(left, right, dims=NN):
    return lax.dot_general(left, right, dims, preferred_element_type=f32)


def mm_exact(left, right, dims=NN):
    return lax.dot_general(left, right, dims, precision=highest, preferred_element_type=f32)


def split(values):
    high = values.astype(bf16)
    return high, (values - high.astype(f32)).astype(bf16)


def params(semantics=None):
    if semantics is None:
        return pltpu.CompilerParams(vmem_limit_bytes=VMEM_BYTES)
    return pltpu.CompilerParams(vmem_limit_bytes=VMEM_BYTES, dimension_semantics=semantics)


def cost(flops, moved):
    return pl.CostEstimate(
        flops=int(flops) // 100, bytes_accessed=int(moved) // 100, transcendentals=0
    )


def bucket_of(offset):
    distance = jnp.abs(offset)
    coarse = jnp.full_like(distance, 8)
    for edge_value in bucket_edges:
        coarse = coarse + (distance >= edge_value).astype(i32)
    return jnp.where(distance < 8, distance, coarse) + 16 * (offset > 0).astype(i32)


def one_hot(mask):
    return mask.astype(f32).astype(bf16)


def lane_numbers(rows, width):
    return lax.broadcasted_iota(i32, (rows, width), 1)


def place_kernel(routes_ref, slot_ref, kept_ref, seg_ref, bias_ref, row_ref, col_ref, diag_ref, *, capacity, local_experts):
    tokens = seg_ref.shape[1]
    routes = routes_ref[...]
    seat = (routes // local_experts) * capacity + slot_ref[...]
    kept = kept_ref[...] == 1
    line = lax.broadcasted_iota(i32, (BLOCK, tokens), 0)
    stacked = jnp.where(line == local_experts, routes, 0)
    stacked = jnp.where(line == local_experts + 1, seg_ref[...], stacked)
    for le in range(local_experts):
        key = jnp.where(kept & (routes % local_experts == le), seat, -1)
        stacked = jnp.where(line == le, key, stacked)
    row_ref[...] = stacked[: row_ref.shape[0]]
    col_ref[...] = stacked.T
    buckets = bias_ref.shape[0]
    offset = lane_numbers(buckets, 4 * BLOCK) - 2 * BLOCK
    pick = bucket_of(offset) == lax.broadcasted_iota(i32, (buckets, 4 * BLOCK), 0)
    diag_ref[...] = mm_exact(bias_ref[...], pick.astype(f32), TN)


def slots_kernel(place_ref, *refs, parts, le):
    key_refs = refs[:parts]
    rows_ref, out_ref = refs[parts:]
    direct = len(out_ref.shape) == 4
    slots = out_ref.shape[0] * out_ref.shape[2] if direct else out_ref.shape[1]
    tokens = rows_ref.shape[1]
    for j in range(parts):
        whole = (place_ref[0] + j) % parts
        key = key_refs[j][le : le + 1, :]
        table = lax.broadcasted_iota(i32, (slots, tokens), 0) == key
        rows = mm(one_hot(table), rows_ref[whole])
        if direct:
            by_group(rows, out_ref, whole)
        else:
            out_ref[whole] = rows.astype(bf16)


def by_group(rows, out_ref, place):
    capacity = out_ref.shape[2]
    for group in range(out_ref.shape[0]):
        piece = rows[group * capacity : (group + 1) * capacity]
        out_ref[group, place] = piece.astype(bf16)


def qkv_kernel(tok_ref, gain_ref, w_ref, qkv_ref, turned_ref, low_ref):
    @pl.when(pl.program_id(0) == 0)
    def _():
        values = tok_ref[...].astype(f32)
        inverse = lax.rsqrt(jnp.mean(values * values, axis=-1, keepdims=True) + eps)
        normed = values * inverse * gain_ref[...]
        low_ref[...] = normed.astype(bf16)
        turned_ref[...] = normed.T.astype(bf16)

    qkv_ref[...] = mm(low_ref[...], w_ref[...]).astype(bf16)


def attend_kernel(q_ref, k_ref, v_ref, row_ids_ref, cols_ref, diag_ref, att_ref, probs_ref, *, seg_line, head_start):
    length = k_ref.shape[0]
    blocks = length // BLOCK
    lane = lane_numbers(1, BLOCK)
    half = BLOCK // 2
    scale = half**-0.5
    keys = k_ref[...]
    vals = v_ref[...]
    row_ids = row_ids_ref[seg_line : seg_line + 1, :]
    bias_tiles = []
    for s in range(2):
        diag = diag_ref[pl.ds(head_start + 2 * pl.program_id(0) + s, 1), :]
        spread = jnp.broadcast_to(diag, (BLOCK, 4 * BLOCK))
        tile = pltpu.roll(spread, 0, 1, stride=1, stride_axis=0)[:, BLOCK:].T
        low_far = jnp.broadcast_to(diag[:, 1:2], (BLOCK, BLOCK))
        high_far = jnp.broadcast_to(diag[:, 4 * BLOCK - 1 :], (BLOCK, BLOCK))
        bias_tiles.append((low_far, tile, high_far))
    turned_vals = vals.astype(f32).T.astype(bf16)
    upper = lax.broadcasted_iota(i32, (BLOCK, 1), 0) < half
    for i in range(blocks):
        rows = slice(i * BLOCK, (i + 1) * BLOCK)
        same = cols_ref[:, seg_line : seg_line + 1] == row_ids[:, rows]
        queries = q_ref[rows, :]
        outs = []
        for s in range(2):
            mask = jnp.where(lane // half == s, scale, 0.0).astype(bf16)
            scores = mm(keys, queries * mask, NT)
            low_far, tile, high_far = bias_tiles[s]
            pieces = []
            for j in range(blocks):
                if j - i < -1:
                    pieces.append(low_far)
                elif j - i > 1:
                    pieces.append(high_far)
                else:
                    start = (j - i + 1) * BLOCK
                    pieces.append(tile[start : start + BLOCK])
            scores = scores + jnp.concatenate(pieces, axis=0)
            scores = jnp.where(same, scores, -1000000000.0)
            top = jnp.max(scores, axis=0, keepdims=True)
            grown = jnp.exp(scores - top)
            probs = (grown * (1.0 / jnp.sum(grown, axis=0, keepdims=True))).astype(bf16)
            probs_ref[s, :, rows] = probs
            outs.append(mm(turned_vals, probs))
        att_ref[rows, :] = jnp.where(upper, outs[0], outs[1]).T.astype(bf16)


def chosen_of(router, cols_ref, line):
    pick = cols_ref[:, line : line + 1] == lane_numbers(*router.shape)
    return pick, jnp.sum(jnp.where(pick, router, 0.0), axis=-1, keepdims=True)


def route_kernel(tok_ref, att_a_ref, att_b_ref, w_out_ref, gain_ref, w_router_ref, rows_ref, residual_ref, router_ref, sent_ref):
    near = att_a_ref.shape[1]
    branch = mm(att_a_ref[...], w_out_ref[:near]) + mm(att_b_ref[...], w_out_ref[near:])
    residual = tok_ref[...].astype(f32) + branch
    residual_ref[...] = residual
    inverse = lax.rsqrt(jnp.mean(residual * residual, axis=-1, keepdims=True) + eps)
    normed = residual * inverse * gain_ref[...]
    low = normed.astype(bf16)
    tokens = low.shape[0]
    direct = len(sent_ref.shape) == 4
    local_experts = sent_ref.shape[1] if direct else sent_ref.shape[0]
    slots = sent_ref.shape[0] * sent_ref.shape[2] if direct else sent_ref.shape[1]
    for index in range(local_experts):
        table = lax.broadcasted_iota(i32, (slots, tokens), 0) == rows_ref[index : index + 1, :]
        rows = mm(one_hot(table), low)
        if direct:
            by_group(rows, sent_ref, index)
        else:
            sent_ref[index] = rows.astype(bf16)
    w_high, w_low = split(w_router_ref[...])
    low_rest = (normed - low.astype(f32)).astype(bf16)
    experts = w_high.shape[1]
    logits = mm(low, jnp.concatenate([w_high, w_low], axis=1))
    logits = logits[:, :experts] + logits[:, experts:] + mm(low_rest, w_high)
    top = jnp.max(logits, axis=-1, keepdims=True)
    grown = jnp.exp(logits - top)
    router = grown / jnp.sum(grown, axis=-1, keepdims=True)
    router_ref[...] = router


def expert_kernel(place_ref, x_ref, cot_ref, w_in_ref, w_back_ref, *refs, parts, le, groups, order, olds):
    count = len(order)
    refs = refs[olds:]
    back_refs = refs[:count]
    act_ref, gp_ref = refs[count : count + 2]
    x_buf, g_buf, w_in_buf, w_back_buf, act_buf, gp_buf, back_buf = refs[count + 2 : -4]
    x_sem, g_sem, w_sem, put_sem = refs[-4:]
    place = place_ref[0]
    whole = [(place + j) % parts for j in order]
    load_in = pltpu.make_async_copy(w_in_ref.at[le], w_in_buf, w_sem.at[0])
    load_back = pltpu.make_async_copy(w_back_ref.at[le], w_back_buf, w_sem.at[1])
    load_in.start()
    loads = []
    for at in range(count):
        loads.append(
            (
                pltpu.make_async_copy(x_ref.at[whole[at]], x_buf.at[at], x_sem.at[at]),
                pltpu.make_async_copy(cot_ref.at[whole[at]], g_buf.at[at], g_sem.at[at]),
            )
        )
        loads[at][0].start()
    load_back.start()
    for at in range(count):
        loads[at][1].start()
    load_in.wait()
    scale = (2.0 / jnp.pi) ** 0.5
    slots, model = x_buf.shape[1:]
    hidden = act_buf.shape[2]
    spare = back_buf.shape[1] - slots
    line = lax.broadcasted_iota(i32, (spare, BLOCK), 0)
    capacity = slots // groups
    puts = []

    def put(source, target, kind, at):
        copy = pltpu.make_async_copy(source, target, put_sem.at[kind, at])
        copy.start()
        puts.append(copy)

    span = 2
    for first in range(0, count, span):
        ats = range(first, first + span)
        for at in ats:
            loads[at][0].wait()
        pre = mm(x_buf[first : first + span].reshape(span * slots, model), w_in_buf[...])
        for at in ats:
            loads[at][1].wait()
        if first == 0:
            load_back.wait()
        grad = mm(g_buf[first : first + span].reshape(span * slots, model), w_back_buf[...], NT)
        square = pre * pre
        slant = jnp.tanh(scale * pre * (1.0 + 0.044715 * square))
        act = (0.5 * pre * (1.0 + slant)).astype(bf16)
        act_buf[first : first + span] = act.reshape(span, slots, hidden)
        slope = 0.5 * (1.0 + slant) + 0.5 * pre * (1.0 - slant * slant) * (
            scale * (1.0 + 3.0 * 0.044715 * square)
        )
        gp = (grad * slope).astype(bf16)
        gp_buf[first : first + span] = gp.reshape(span, slots, hidden)
        back = mm(gp, w_in_buf[...], NT).astype(bf16)
        back_buf[first : first + span, :slots] = back.reshape(span, slots, model)
        all_dots = jnp.sum(act.astype(f32) * grad, axis=-1, keepdims=True)
        for at in ats:
            put(act_buf.at[at], act_ref.at[whole[at]], 0, at)
            put(gp_buf.at[at], gp_ref.at[whole[at]], 1, at)
            dots = all_dots[(at - first) * slots : (at - first + 1) * slots]
            dots = jnp.broadcast_to(dots, (slots, BLOCK)).T
            laid = jnp.zeros((spare, BLOCK), f32)
            for group in range(groups):
                piece = dots[:1, group * capacity : (group + 1) * capacity]
                piece = jnp.concatenate([piece, jnp.zeros((1, BLOCK - capacity), f32)], axis=1)
                laid = jnp.where(line == group, piece, laid)
            back_buf[at, slots:] = jnp.zeros((spare, model), bf16)
            back_buf[at, slots:, :BLOCK] = laid.astype(bf16)
            put(back_buf.at[at], back_refs[at], 2, at)
    for copy in puts:
        copy.wait()


def expert_weights_kernel(own_ref, x_ref, act_ref, cot_ref, gp_ref, w_router_ref, all_act_ref, w_back_ref, *refs, le, local_experts):
    in_ref, back_ref, out_ref, gs_ref, gate_ref, turned_ref = refs[-6:]
    parts = x_ref.shape[0]

    def flat(values):
        return values.reshape(-1, values.shape[-1])

    @pl.when(pl.program_id(0) == 0)
    def _():
        w_high, w_low = split(w_router_ref[...])
        number = own_ref[0] * local_experts + le
        for part in range(parts):
            rows = x_ref[part]
            logits = mm(rows, w_high) + mm(rows, w_low)
            grown = jnp.exp(logits - jnp.max(logits, axis=-1, keepdims=True))
            pick = lane_numbers(*logits.shape) == number
            gate = jnp.sum(jnp.where(pick, grown, 0.0), axis=-1, keepdims=True)
            gate = gate / jnp.sum(grown, axis=-1, keepdims=True)
            gate_ref[part] = gate
            gs_ref[part] = (cot_ref[part].astype(f32) * gate).astype(bf16)
        turned_ref[...] = flat(x_ref[...]).T

    gp = (gp_ref[...].astype(f32) * gate_ref[...]).astype(bf16)
    in_ref[0] = mm(turned_ref[...], flat(gp))
    back_ref[0] = mm(flat(act_ref[...]), flat(gs_ref[...]), TN)
    out = mm(flat(all_act_ref[...]), w_back_ref[0])
    slots = out.shape[0] // parts
    for part in range(parts):
        rows = out[part * slots : (part + 1) * slots]
        if len(out_ref.shape) == 5:
            by_group(rows, out_ref.at[part], 0)
        else:
            out_ref[part, 0] = rows.astype(bf16)


def middle_kernel(residual_ref, cot_ref, gain_ref, w_router_ref, router_ref, cols_ref, w_out_ref, *refs, capacity, stride):
    grad_res_ref, branch_ref, att_ref, extra_ref = refs[-4:]
    back_refs = refs[:-4]
    local_experts = len(back_refs)
    tokens = residual_ref.shape[0]
    rows = None
    grad_gate = None
    for index, back_ref in enumerate(back_refs):
        key = cols_ref[:, index : index + 1]
        group = key // capacity
        number = lane_numbers(tokens, back_ref.shape[0])
        back = back_ref[...]
        part = mm(one_hot(number == key + group * (stride - capacity)), back)
        lines = mm(one_hot(number == group * stride + capacity), back[:, :BLOCK])
        slot = lane_numbers(tokens, BLOCK) == key - group * capacity
        picked = jnp.sum(jnp.where(slot, lines, 0.0), axis=-1, keepdims=True)
        rows = part if rows is None else rows + part
        grad_gate = picked if grad_gate is None else grad_gate + picked
    router = router_ref[...]
    pick, chosen = chosen_of(router, cols_ref, local_experts)
    grad_logits = router * (pick.astype(f32) - chosen) * grad_gate
    residual = residual_ref[...]
    inverse = lax.rsqrt(jnp.mean(residual * residual, axis=-1, keepdims=True) + eps)
    gain = gain_ref[...]
    scaled = residual * inverse
    logits_high, logits_low = split(grad_logits)
    w_high, w_low = split(w_router_ref[...])
    grad_normed = chosen * rows + mm(
        jnp.concatenate([logits_high, logits_low, logits_high], axis=1),
        jnp.concatenate([w_high, w_high, w_low], axis=1),
        NT,
    )
    weighted = grad_normed * gain
    lean = jnp.mean(weighted * residual, axis=-1, keepdims=True)
    grad_res = cot_ref[...].astype(f32) + (
        inverse * weighted - residual * (inverse * inverse * inverse) * lean
    )
    grad_res_ref[...] = grad_res
    low = grad_res.astype(bf16)
    branch_ref[...] = low
    att_ref[...] = mm(low, w_out_ref[...], NT).astype(bf16)
    gain_grad = jnp.sum(grad_normed * scaled, axis=0, keepdims=True)
    normed_high, normed_low = split(scaled * gain)
    experts = logits_high.shape[1]
    router_grad = mm(jnp.concatenate([logits_high, logits_low], axis=1), normed_high, TN)
    router_grad = router_grad[:experts] + router_grad[experts:] + mm(logits_high, normed_low, TN)
    spare = extra_ref.shape[1] - router_grad.shape[0] - 1
    both = jnp.concatenate(
        [router_grad, gain_grad, jnp.zeros((spare, gain_grad.shape[1]), f32)], axis=0
    )
    extra_ref[...] = both.T.astype(bf16)


def attend_back_kernel(q_ref, k_ref, v_ref, probs_ref, grad_ref, turned_ref, *refs, kind, head_start, buckets):
    if kind == 0:
        att_a_ref, att_b_ref, branch_ref, extra_ref = refs[:4]
    else:
        old_diag_ref = refs[0]
    if kind == 2:
        old_weight_ref = refs[1]
    dq_ref, dk_ref, dv_ref, weight_ref, diag_ref, slope_ref = refs[-6:]
    step = pl.program_id(0)
    length = k_ref.shape[0]
    blocks = length // BLOCK
    lane = lane_numbers(1, BLOCK)
    half = BLOCK // 2
    scale = half**-0.5
    keys = k_ref[...]
    vals = v_ref[...]
    queries = q_ref[...]
    grads = grad_ref[...]
    static_columns = weight_ref.shape[1]

    @pl.when(step == 0)
    def _():
        if kind == 0:
            diag_ref[...] = jnp.zeros_like(diag_ref)
            model = branch_ref.shape[1]
            tail = extra_ref.shape[1]
            begin = static_columns - tail - model
            near = att_a_ref.shape[1]
            branch = branch_ref[...]
            weight_ref[:near, begin : begin + model] = mm(att_a_ref[...], branch, TN).astype(bf16)
            weight_ref[near:, begin : begin + model] = mm(att_b_ref[...], branch, TN).astype(bf16)
            weight_ref[:, begin + model :] = extra_ref[...]
        else:
            diag_ref[...] = old_diag_ref[...]
        if kind == 2:
            weight_ref[:, : old_weight_ref.shape[1]] = old_weight_ref[...]

    across = lax.broadcasted_iota(i32, (BLOCK, BLOCK), 0) + lane_numbers(BLOCK, BLOCK)
    flip = one_hot(across == BLOCK - 1)
    turned_keys = keys.astype(f32).T.astype(bf16)
    dq = [[] for _ in range(blocks)]
    dk, dv = [], []
    for s in range(2):
        mask = jnp.where(lane // half == s, 1.0, 0.0).astype(bf16)
        near = [None, None, None]
        far = [None, None]
        for i in range(blocks):
            rows = slice(i * BLOCK, (i + 1) * BLOCK)
            probs = probs_ref[s, :, rows].astype(f32)
            grad_probs = mm(vals, grads[rows] * mask, NT)
            delta = jnp.sum(probs * grad_probs, axis=0, keepdims=True)
            slope = probs * (grad_probs - delta)
            low = slope.astype(bf16)
            slope_ref[s, :, rows] = low
            dq[i].append(mm(turned_keys, low))
            for j in range(blocks):
                piece = slope[j * BLOCK : (j + 1) * BLOCK]
                apart = j - i
                if abs(apart) <= 1:
                    old = near[1 - apart]
                    near[1 - apart] = piece if old is None else old + piece
                else:
                    old = far[int(apart > 0)]
                    far[int(apart > 0)] = piece if old is None else old + piece
        dk.append(mm(slope_ref[s], queries))
        dv.append(mm(probs_ref[s], grads))
        wide = jnp.concatenate([jnp.zeros_like(near[0])] + near, axis=1)
        lined = pltpu.roll(mm(flip, wide.astype(bf16)), 3 * BLOCK + 1, 1, stride=1, stride_axis=0)
        lined = jnp.concatenate([lined, far[0], far[1]], axis=1)
        diag_ref[pl.ds(head_start + 2 * step + s, 1), :] = jnp.sum(lined, axis=0, keepdims=True)
    upper = lax.broadcasted_iota(i32, (BLOCK, 1), 0) < half
    dq_low = jnp.concatenate([jnp.where(upper, *item).T for item in dq], axis=0)
    dq_low = (dq_low * scale).astype(bf16)
    left = lane < half
    dk_low = (jnp.where(left, dk[0], dk[1]) * scale).astype(bf16)
    dv_low = jnp.where(left, dv[0], dv[1]).astype(bf16)
    dq_ref[...] = dq_low
    dk_ref[...] = dk_low
    dv_ref[...] = dv_low
    begin = 0 if kind < 2 else old_weight_ref.shape[1]
    begin = pl.multiple_of(step * (3 * BLOCK) + begin, 3 * BLOCK)
    weight_ref[:, pl.ds(begin, 3 * BLOCK)] = mm(
        turned_ref[...], jnp.concatenate([dq_low, dk_low, dv_low], axis=1)
    ).astype(bf16)
    if kind == 2:

        @pl.when(step == pl.num_programs(0) - 1)
        def _():
            wide = diag_ref.shape[1]
            number = lane_numbers(buckets, wide)
            bucket = bucket_of(2 * BLOCK - number)
            bucket = jnp.where(number >= 4 * BLOCK, 15, bucket)
            bucket = jnp.where(number >= 5 * BLOCK, 31, bucket)
            pick = bucket == lax.broadcasted_iota(i32, (buckets, wide), 0)
            rows = jnp.concatenate(
                [diag_ref[...], jnp.zeros((BLOCK - diag_ref.shape[0], wide), f32)], axis=0
            )
            bias = mm_exact(pick.astype(f32), rows, NT)
            begin = static_columns - BLOCK
            weight_ref[:, begin:] = jnp.zeros((weight_ref.shape[0], BLOCK), bf16)
            weight_ref[:buckets, begin:] = bias.astype(bf16)


def tokens_kernel(tok_ref, gain_ref, w_ref, grad_res_ref, *refs):
    out_ref = refs[-1]
    parts = refs[:-1]
    groups = len(parts) // 3
    model = tok_ref.shape[1]
    grad_normed = None
    for part in range(3):
        start = part * model
        for group in range(groups):
            block = parts[3 * group + part]
            width = block.shape[1]
            piece = mm(block[...], w_ref[:, start : start + width], NT)
            grad_normed = piece if grad_normed is None else grad_normed + piece
            start += width
    values = tok_ref[...].astype(f32)
    inverse = lax.rsqrt(jnp.mean(values * values, axis=-1, keepdims=True) + eps)
    weighted = grad_normed * gain_ref[...]
    lean = jnp.mean(weighted * values, axis=-1, keepdims=True)
    out_ref[...] = grad_res_ref[...] + (
        inverse * weighted - values * (inverse * inverse * inverse) * lean
    )


def output_kernel(residual_ref, router_ref, cols_ref, rows_ref, out_ref):
    tokens = residual_ref.shape[0]
    local_experts, slots = rows_ref.shape[:2]
    mixture = None
    for index in range(local_experts):
        turned = cols_ref[:, index : index + 1] == lane_numbers(tokens, slots)
        part = mm(one_hot(turned), rows_ref[index])
        mixture = part if mixture is None else mixture + part
    _, chosen = chosen_of(router_ref[...], cols_ref, local_experts)
    out_ref[...] = (residual_ref[...] + chosen * mixture).astype(bf16)


def finish_kernel(where_ref, a_ref, b_ref, w_ref, *refs):
    qkv_ref, out_ref, gain_ref, extra_ref = refs[-4:]
    place = where_ref[2]
    parts = a_ref.shape[1]
    model = out_ref.shape[3]
    pairs = model // BLOCK
    near = pairs // 3
    for k in range(parts):
        z = (place + parts - k) % parts
        a = a_ref[0, k].astype(f32)
        b = b_ref[0, k].astype(f32)
        total = None
        for part in range(3):
            pieces = [
                (a if p < near else b)[:, ((p if p < near else p - near) * 3 + part) * BLOCK :][
                    :, :BLOCK
                ]
                for p in range(pairs)
            ]
            whole = jnp.concatenate(pieces, axis=1)
            span = slice(part * model, (part + 1) * model)
            qkv_ref[0, z, :, span] = whole
            w = w_ref[0, z, :, span].astype(f32)
            share = jnp.sum(whole * w, axis=-1, keepdims=True)
            total = share if total is None else total + share
        gain_ref[0, z] = jnp.broadcast_to(total, gain_ref.shape[2:])
        begin = near * 3 * BLOCK
        out_ref[0, z] = a[:, begin : begin + model]
        tail = a.shape[1] - begin - model
        extra_ref[0, z, :, :tail] = a[:, begin + model :]
        extra_ref[0, z, :, tail:] = b[:, (pairs - near) * 3 * BLOCK :]


def small_kernel(gain_ref, sums_ref, extra_ref, router_ref, gains_ref, bias_ref, *, experts, at):
    extras = extra_ref[:, :at].T
    router_ref[...] = extras[:experts]
    gains_ref[0:1, :] = sums_ref[...].T[0:1] / gain_ref[...]
    gains_ref[1:2, :] = extras[experts : experts + 1]
    heads, buckets = bias_ref.shape
    bias_ref[...] = extra_ref[:BLOCK, at:].T[:heads, :buckets]


def add_low(left, right):
    return (left.astype(f32) + right.astype(f32)).astype(bf16)


def tie(items, after):
    return lax.optimization_barrier((items, after))[0]


def held(kernel, start, after):
    def body(*refs):
        kernel(*refs[:start], *refs[start + len(after) :])

    return body


class Scatter:
    def __init__(self, blocks):
        self.parts = lax.axis_size("hidden")
        self.blocks = blocks
        self.count = 0

    def step(self, after=()):
        self.count += 1
        right, left = self.blocks[self.parts - self.count], self.blocks[self.count]
        if self.count > 1:
            right, left = add_low(right, self.right), add_low(left, self.left)
        right, left = tie((right, left), after)
        ways = [(a, a + 1) for a in range(self.count)]
        self.right = lax.ppermute(right, "hidden", ways)
        ways = [(a, a - 1) for a in range(self.parts - self.count, self.parts)]
        self.left = lax.ppermute(left, "hidden", ways)

    def last(self):
        return self.right, self.left

    def finish(self, after=()):
        right, left = tie(self.last(), after)
        total = self.blocks[0].astype(f32) + right.astype(f32) + left.astype(f32)
        return total.astype(bf16)


def pick_block(blocks, index):
    return lax.dynamic_index_in_dim(blocks, index, 0, keepdims=False)


class Sum:
    def __init__(self, values):
        self.groups = lax.axis_size("expert")
        self.parts = lax.axis_size("hidden")
        self.own = lax.axis_index("expert")
        self.place = lax.axis_index("hidden")
        self.core = self.own % 2
        self.chip = self.own // 2
        self.chips = self.groups // 2
        self.pair = [(a, a ^ 1) for a in range(self.groups)]
        self.width = values.shape[1]
        self.values = values

    def cores(self):
        halves = self.values.reshape(2, -1, self.width)
        got = lax.ppermute(pick_block(halves, 1 - self.core), "expert", self.pair)
        self.values = add_low(pick_block(halves, self.core), got)

    def cores_at_once(self):
        teams = [[2 * a, 2 * a + 1] for a in range(self.chips)]
        got = lax.all_to_all(
            self.values, "expert", split_axis=0, concat_axis=0, tiled=True, axis_index_groups=teams
        ).reshape(2, -1, self.width)
        self.values = add_low(got[0], got[1])

    def plane(self):
        pieces = self.values.reshape(self.chips, -1, self.width)
        total = pick_block(pieces, self.chip).astype(f32)
        for step in range(1, self.chips):
            ways = [(a, a ^ (2 * step)) for a in range(self.groups)]
            got = lax.ppermute(pick_block(pieces, self.chip ^ step), "expert", ways)
            total = total + got.astype(f32)
        self.values = total.astype(bf16)

    def line(self):
        pieces = self.values.reshape(self.parts, -1, self.width)
        total = pick_block(pieces, self.place).astype(f32)
        for step in range(1, self.parts):
            ways = [(a, (a + step) % self.parts) for a in range(self.parts)]
            got = lax.ppermute(pick_block(pieces, (self.place + step) % self.parts), "hidden", ways)
            total = total + got.astype(f32)
        self.values = total.astype(bf16)

    def line_back(self):
        pieces = [self.values]
        for step in range(1, self.parts):
            ways = [(a, (a + step) % self.parts) for a in range(self.parts)]
            pieces.append(lax.ppermute(self.values, "hidden", ways))
        self.values = jnp.stack(pieces)

    def plane_back(self):
        pieces = [self.values]
        for step in range(1, self.chips):
            ways = [(a, a ^ (2 * step)) for a in range(self.groups)]
            pieces.append(lax.ppermute(self.values, "expert", ways))
        self.values = jnp.stack(pieces)

    def cores_back(self):
        return self.values, lax.ppermute(self.values, "expert", self.pair)

    def run(self):
        self.cores()
        self.plane()
        self.line()
        self.line_back()
        self.plane_back()
        return self.cores_back()


def local(tokens, cotangent, segments, routes, slot_ids, kept_flags, gain_one, w_qkv, w_out, bias_table, gain_two, w_router, w_in, w_back):
    tok_rows, model = tokens.shape
    bucket_count, head_count = bias_table.shape
    experts = w_router.shape[1]
    local_experts = w_in.shape[0]
    hidden = w_in.shape[2]
    groups = lax.axis_size("expert")
    parts = lax.axis_size("hidden")
    own = lax.axis_index("expert")
    place = lax.axis_index("hidden")
    capacity = max(2, (5 * tok_rows + 4 * experts - 1) // (4 * experts))
    slots = groups * capacity
    pairs = head_count // 2
    shape = jax.ShapeDtypeStruct
    vmem = pl.BlockSpec(memory_space=pltpu.VMEM)
    any_space = pl.BlockSpec(memory_space=pl.ANY)
    gain_one_row = gain_one[None, :]
    gain_two_row = gain_two[None, :]
    seg_line = local_experts + 1

    def exchange(rows, axis=0):
        return lax.all_to_all(rows, "expert", split_axis=axis, concat_axis=axis, tiled=True)

    cot_near = lax.all_gather(cotangent, "hidden", axis=0, tiled=False)
    id_rows, id_cols, diag_bias = pl.pallas_call(
        functools.partial(place_kernel, capacity=capacity, local_experts=local_experts),
        out_shape=[
            shape((8, tok_rows), i32),
            shape((tok_rows, BLOCK), i32),
            shape((head_count, 4 * BLOCK), f32),
        ],
        in_specs=[vmem] * 5,
        out_specs=[vmem] * 3,
        compiler_params=params(),
        cost_estimate=cost(1e8, 1e6),
        name="place",
    )(routes[None, :], slot_ids[None, :], kept_flags[None, :], segments, bias_table)
    qkv, turned = pl.pallas_call(
        qkv_kernel,
        grid=(3,),
        out_shape=[shape((tok_rows, 3 * model), bf16), shape((model, tok_rows), bf16)],
        in_specs=[
            pl.BlockSpec((tok_rows, model), lambda j: (0, 0)),
            pl.BlockSpec((1, model), lambda j: (0, 0)),
            pl.BlockSpec((model, model), lambda j: (0, j)),
        ],
        out_specs=[
            pl.BlockSpec((tok_rows, model), lambda j: (0, j)),
            pl.BlockSpec((model, tok_rows), lambda j: (0, 0)),
        ],
        scratch_shapes=[pltpu.VMEM((tok_rows, model), bf16)],
        compiler_params=params(("arbitrary",)),
        cost_estimate=cost(6 * tok_rows * model * model, 8 * model * model * 2),
        name="qkv",
    )(tokens, gain_one_row, w_qkv)

    def pair_spec(offset):
        return pl.BlockSpec((tok_rows, BLOCK), lambda p: (0, offset + p))

    steps = pairs // 2
    attended, probs = [], []
    for half in range(2):
        start = half * steps
        att, prob = pl.pallas_call(
            functools.partial(attend_kernel, seg_line=seg_line, head_start=2 * start),
            grid=(steps,),
            out_shape=[
                shape((tok_rows, steps * BLOCK), bf16),
                shape((2 * steps, tok_rows, tok_rows), bf16),
            ],
            in_specs=[
                pair_spec(start),
                pair_spec(pairs + start),
                pair_spec(2 * pairs + start),
                pl.BlockSpec((8, tok_rows), lambda p: (0, 0)),
                pl.BlockSpec((tok_rows, BLOCK), lambda p: (0, 0)),
                pl.BlockSpec((head_count, 4 * BLOCK), lambda p: (0, 0)),
            ],
            out_specs=[
                pair_spec(0),
                pl.BlockSpec((2, tok_rows, tok_rows), lambda p: (p, 0, 0)),
            ],
            compiler_params=params(("arbitrary",)),
            cost_estimate=cost(steps * 4e9, steps * 3e6),
            name="attend",
        )(qkv, qkv, qkv, id_rows, id_cols, diag_bias)
        attended.append(att)
        probs.append(prob)

    def by_slots(count):
        if direct:
            return shape((groups, count, capacity, model), bf16)
        return shape((count, slots, model), bf16)

    direct = capacity % 8 == 0
    residual, router, sent_rows = pl.pallas_call(
        route_kernel,
        out_shape=[
            shape((tok_rows, model), f32),
            shape((tok_rows, experts), f32),
            by_slots(local_experts),
        ],
        in_specs=[vmem] * 7,
        out_specs=[vmem] * 3,
        compiler_params=params(),
        cost_estimate=cost(6e9, 6e6),
        name="route",
    )(tokens, *attended, w_out, gain_two_row, w_router, id_rows)

    place_arr = place.astype(i32).reshape(1)
    own_arr = own.astype(i32).reshape(1)
    spare = -(-groups // 16) * 16
    block = shape((slots + spare, model), bf16)
    stack = shape((parts, slots, hidden), bf16)
    smem = pl.BlockSpec(memory_space=pltpu.SMEM)
    third = hidden // 3

    def run_experts(le, order, olds, after=()):
        count = len(order)
        results = pl.pallas_call(
            held(
                functools.partial(
                    expert_kernel, parts=parts, le=le, groups=groups, order=order, olds=len(olds)
                ),
                5 + len(olds),
                after,
            ),
            out_shape=[block] * count + [stack, stack],
            in_specs=[smem] + [any_space] * (4 + len(olds) + len(after)),
            out_specs=[any_space] * (count + 2),
            input_output_aliases={5 + n: count + n for n in range(len(olds))},
            scratch_shapes=[
                pltpu.VMEM((count, slots, model), bf16),
                pltpu.VMEM((count, slots, model), bf16),
                pltpu.VMEM((model, hidden), bf16),
                pltpu.VMEM((hidden, model), bf16),
                pltpu.VMEM((count, slots, hidden), bf16),
                pltpu.VMEM((count, slots, hidden), bf16),
                pltpu.VMEM((count, slots + spare, model), bf16),
                pltpu.SemaphoreType.DMA((count,)),
                pltpu.SemaphoreType.DMA((count,)),
                pltpu.SemaphoreType.DMA((2,)),
                pltpu.SemaphoreType.DMA((3, count)),
            ],
            compiler_params=params(),
            cost_estimate=cost(4 * count * slots * model * hidden, 1e7),
            name="experts",
        )(place_arr, rows_all[le], cot_all[le], w_in, w_back, *olds, *after)
        return results[:count], list(results[count:])

    def run_both(le, after=()):
        ends = list(range(1, parts, 2))
        rest = list(range(0, parts, 2))
        backs = [None] * parts
        some, kept = run_experts(le, ends, [], after)
        for j, item in zip(ends, some):
            backs[j] = item
        some, kept = run_experts(le, rest, kept)
        for j, item in zip(rest, some):
            backs[j] = item
        return backs, kept

    def run_weights(le, kept, olds, after):
        act, gp = kept
        stack_spec = pl.BlockSpec((parts, slots, model), lambda j: (0, 0, 0))
        hidden_spec = pl.BlockSpec((parts, slots, third), lambda j: (0, 0, j))
        return pl.pallas_call(
            held(
                functools.partial(expert_weights_kernel, le=le, local_experts=local_experts),
                8 + len(olds),
                after,
            ),
            grid=(3,),
            out_shape=[
                shape((local_experts, model, hidden), f32),
                shape((local_experts, hidden, model), f32),
                shape((parts,) + by_slots(local_experts).shape, bf16),
            ],
            in_specs=[
                smem,
                stack_spec,
                hidden_spec,
                stack_spec,
                hidden_spec,
                pl.BlockSpec((model, experts), lambda j: (0, 0)),
                pl.BlockSpec((parts, slots, hidden), lambda j: (0, 0, 0)),
                pl.BlockSpec((1, hidden, model // 3), lambda j: (le, 0, j)),
            ]
            + [any_space] * (len(olds) + len(after)),
            out_specs=[
                pl.BlockSpec((1, model, third), lambda j: (le, 0, j)),
                pl.BlockSpec((1, third, model), lambda j: (le, j, 0)),
                pl.BlockSpec(
                    (parts, groups, 1, capacity, model // 3), lambda j: (0, 0, le, 0, j)
                )
                if direct
                else pl.BlockSpec((parts, 1, slots, model // 3), lambda j: (0, le, 0, j)),
            ],
            scratch_shapes=[
                pltpu.VMEM((parts, slots, model), bf16),
                pltpu.VMEM((parts, slots, 1), f32),
                pltpu.VMEM((model, parts * slots), bf16),
            ],
            input_output_aliases={8 + n: n for n in range(len(olds))},
            compiler_params=params(("arbitrary",)),
            cost_estimate=cost(4 * parts * slots * model * hidden, 1.3e7),
            name="expert_weights",
        )(own_arr, rows_all[le], act, cot_all[le], gp, w_router, act, w_back, *olds, *after)

    def own_slots(le, ids, after):
        return pl.pallas_call(
            held(functools.partial(slots_kernel, parts=parts, le=le), 2 + parts, after),
            out_shape=by_slots(parts),
            in_specs=[smem] + [vmem] * (parts + 1) + [any_space] * len(after),
            out_specs=vmem,
            compiler_params=params(),
            cost_estimate=cost(2e9, 6e6),
            name="slots",
        )(place_arr, *ids, cot_near, *after)

    def exchange_slots(rows):
        if not direct:
            return exchange(rows, 1)
        return exchange(rows).transpose(1, 0, 2, 3).reshape(-1, slots, model)

    here = exchange_slots(sent_rows)
    rows_all = [
        lax.all_gather(here[le], "hidden", axis=0, tiled=False) for le in range(local_experts)
    ]
    ids = [id_rows]
    far_ids = tie(id_rows, here)
    for step in range(1, parts):
        ways = [((a + step) % parts, a) for a in range(parts)]
        ids.append(lax.ppermute(far_ids, "hidden", ways))
    cot_slots = [own_slots(0, ids, [here])]
    cot_slots.append(own_slots(1, ids, cot_slots))
    cot_all = [exchange_slots(cot_slots[0])]
    cot_all.append(exchange_slots(tie(cot_slots[1], cot_all[0])))
    backs, kept = run_both(0, cot_slots[1:])
    sum_first = Scatter(backs)
    sum_first.step()
    grads = run_weights(0, kept, [], [])
    sum_first.step(grads)
    backs, kept_second = run_both(1, grads[:1])
    sum_second = Scatter(backs)
    sum_second.step()
    sum_second.step(sum_first.last())
    sum_first.step()
    grads = run_weights(1, kept_second, grads, sum_second.last()[:1])

    def with_dots(total):
        rows = total[:slots].reshape(groups, capacity, model)
        dots = total[slots : slots + groups].reshape(groups, 1, model)
        dots = jnp.pad(dots, ((0, 0), (0, stride - capacity - 1), (0, 0)))
        return jnp.concatenate([rows, dots], axis=1).reshape(groups * stride, model)

    stride = -(-(capacity + 1) // 8) * 8
    back_first = exchange(with_dots(sum_first.finish()))
    sum_second.step(sum_first.last())
    back_second = sum_second.finish((back_first, grads))
    backs = [back_first, exchange(with_dots(back_second))]
    grad_w_in, grad_w_back, out_sums = grads
    extra_width = -(-(experts + 1) // BLOCK) * BLOCK

    grad_res, grad_branch, grad_att, extra = pl.pallas_call(
        functools.partial(middle_kernel, capacity=capacity, stride=stride),
        out_shape=[
            shape((tok_rows, model), f32),
            shape((tok_rows, model), bf16),
            shape((tok_rows, model), bf16),
            shape((model, extra_width), bf16),
        ],
        in_specs=[vmem] * (7 + local_experts),
        out_specs=[vmem] * 4,
        compiler_params=params(),
        cost_estimate=cost(6e9, 8e6),
        name="middle",
    )(residual, cotangent, gain_two_row, w_router, router, id_cols, w_out, *backs)

    out_rows = lax.psum_scatter(out_sums, "hidden", scatter_dimension=0, tiled=False)
    out_ready = out_rows
    out_rows = exchange_slots(out_rows)
    output = pl.pallas_call(
        output_kernel,
        out_shape=shape((tok_rows, model), bf16),
        in_specs=[vmem] * 4,
        out_specs=vmem,
        compiler_params=params(),
        cost_estimate=cost(1e9, 4e6),
        name="output",
    )(residual, router, id_cols, out_rows)

    def run_back(kind, start, count, extras, width):
        inner = start % steps
        return pl.pallas_call(
            functools.partial(
                attend_back_kernel,
                kind=kind,
                head_start=2 * start,
                buckets=bucket_count,
            ),
            grid=(count,),
            out_shape=[shape((tok_rows, count * BLOCK), bf16)] * 3
            + [shape((model, width), bf16), shape((16, 6 * BLOCK), f32)],
            in_specs=[
                pair_spec(start),
                pair_spec(pairs + start),
                pair_spec(2 * pairs + start),
                pl.BlockSpec((2, tok_rows, tok_rows), lambda p: (inner + p, 0, 0)),
                pair_spec(start),
                pl.BlockSpec((model, tok_rows), lambda p: (0, 0)),
            ]
            + [pl.BlockSpec(item.shape, lambda p: (0, 0)) for item in extras],
            out_specs=[pair_spec(0)] * 3
            + [
                pl.BlockSpec((model, width), lambda p: (0, 0)),
                pl.BlockSpec((16, 6 * BLOCK), lambda p: (0, 0)),
            ],
            scratch_shapes=[pltpu.VMEM((2, tok_rows, tok_rows), bf16)],
            compiler_params=params(("arbitrary",)),
            cost_estimate=cost(count * 4e9, count * 3e6),
            name="attend_back",
        )(qkv, qkv, qkv, probs[start // steps], grad_att, turned, *extras)

    wide = 3 * BLOCK
    early = pairs // 3
    first = run_back(
        0, 0, early, [*attended, grad_branch, extra], wide * early + model + extra_width
    )
    sum_a = Sum(first[3])
    sum_a.cores()
    second = run_back(1, early, 1, [first[4]], wide)
    sum_a.values = tie(sum_a.values, second[3])
    sum_a.plane()
    third_part = run_back(
        2, early + 1, pairs - early - 1, [second[4], second[3]], wide * (pairs - early) + BLOCK
    )
    sum_b = Sum(tie(third_part[3], sum_a.values))
    sum_b.cores()
    grad_parts = [*first[:3], *second[:3], *third_part[:3]]
    grad_tokens = pl.pallas_call(
        held(tokens_kernel, 4 + len(grad_parts), [sum_b.values]),
        out_shape=shape((tok_rows, model), f32),
        in_specs=[vmem] * (4 + len(grad_parts)) + [any_space],
        out_specs=vmem,
        compiler_params=params(),
        cost_estimate=cost(3e9, 1e7),
        name="tokens_grad",
    )(tokens, gain_one_row, w_qkv, grad_res, *grad_parts, sum_b.values)
    sum_a.line()
    sum_b.plane()
    sum_b.values = tie(sum_b.values, (grad_tokens, out_ready))
    sum_a.line_back()
    sum_b.line()
    sum_a.plane_back()
    sum_b.line_back()
    sum_b.values = tie(sum_b.values, out_rows)
    sums = [sum_a.cores_back()]
    sum_b.plane_back()
    sum_b.values = tie(sum_b.values, output)
    sums.append(sum_b.cores_back())

    chips = groups // 2
    rows = model // (groups * parts)
    where = jnp.stack([own % 2, own // 2, place]).astype(i32)

    tail = extra_width + BLOCK
    widths = (3 * model, model, BLOCK, tail)

    def finish(team, a, b, olds):
        def piece_spec(width):
            return pl.BlockSpec((1, parts, rows, width), lambda s, at: (s, 0, 0, 0))

        def whole_spec(width):
            return pl.BlockSpec(
                (1, parts, rows, width),
                lambda s, at: ((at[0] ^ team) * chips + (at[1] ^ s), 0, 0, 0),
            )

        return pl.pallas_call(
            finish_kernel,
            grid_spec=pltpu.PrefetchScalarGridSpec(
                num_scalar_prefetch=1,
                grid=(chips,),
                in_specs=[
                    piece_spec(a.shape[-1]),
                    piece_spec(b.shape[-1]),
                    whole_spec(3 * model),
                ]
                + [any_space] * len(olds),
                out_specs=[whole_spec(width) for width in widths],
            ),
            out_shape=[shape((groups, parts, rows, width), f32) for width in widths],
            input_output_aliases={4 + n: n for n in range(len(olds))},
            compiler_params=params(("arbitrary",)),
            cost_estimate=cost(1e8, 1e7),
            name="finish",
        )(where, a, b, w_qkv.reshape(groups, parts, rows, 3 * model), *olds)

    (own_a, got_a), (own_b, got_b) = sums
    finished = finish(0, own_a, own_b, [])
    finished = finish(1, got_a, got_b, finished)
    grad_w_qkv, grad_w_out, gain_sums, extras = [
        item.reshape(model, item.shape[-1]) for item in finished
    ]
    grad_router, gains, grad_bias = pl.pallas_call(
        functools.partial(small_kernel, experts=experts, at=extra_width),
        out_shape=[
            shape((experts, model), f32),
            shape((2, model), f32),
            shape((head_count, bucket_count), f32),
        ],
        in_specs=[vmem] * 3,
        out_specs=[vmem] * 3,
        compiler_params=params(),
        cost_estimate=cost(1e6, 2e6),
        name="small",
    )(gain_one_row, gain_sums, extras)
    return (
        output,
        grad_tokens,
        gains[0],
        grad_w_qkv,
        grad_w_out,
        grad_bias.T,
        gains[1],
        grad_router.T,
        grad_w_in,
        grad_w_back,
    )


def solution(mesh):
    return jax.shard_map(
        local,
        mesh=mesh,
        in_specs=(
            P(("expert", "hidden"), None),
            P(("expert", "hidden"), None),
            P(("expert", "hidden"), None),
            P(("expert", "hidden")),
            P(("expert", "hidden")),
            P(("expert", "hidden")),
            P(),
            P(),
            P(),
            P(),
            P(),
            P(),
            P("expert", None, "hidden"),
            P("expert", "hidden", None),
        ),
        out_specs=(
            P(("expert", "hidden"), None),
            P(("expert", "hidden"), None),
            P(),
            P(),
            P(),
            P(),
            P(),
            P(),
            P("expert", None, "hidden"),
            P("expert", "hidden", None),
        ),
        check_vma=False,
    )
```

```python
import functools

import jax
import jax.numpy as jnp
from jax import lax
from jax.experimental import pallas as pl
from jax.experimental.pallas import tpu as pltpu
from jax.sharding import PartitionSpec as P

eps = 1e-06
bucket_edges = (12, 16, 23, 32, 46, 64, 91)
highest = lax.Precision.HIGHEST
f32 = jnp.float32
bf16 = jnp.bfloat16
i32 = jnp.int32
BLOCK = 128
VMEM_BYTES = 56 << 20
NN = (((1,), (0,)), ((), ()))
NT = (((1,), (1,)), ((), ()))
TN = (((0,), (0,)), ((), ()))


def mm(left, right, dims=NN):
    return lax.dot_general(left, right, dims, preferred_element_type=f32)


def mm_exact(left, right, dims=NN):
    return lax.dot_general(left, right, dims, precision=highest, preferred_element_type=f32)


def split(values):
    high = values.astype(bf16)
    return high, (values - high.astype(f32)).astype(bf16)


def params(semantics=None):
    if semantics is None:
        return pltpu.CompilerParams(vmem_limit_bytes=VMEM_BYTES)
    return pltpu.CompilerParams(vmem_limit_bytes=VMEM_BYTES, dimension_semantics=semantics)


def cost(flops, moved):
    return pl.CostEstimate(
        flops=int(flops) // 100, bytes_accessed=int(moved) // 100, transcendentals=0
    )


def bucket_of(offset):
    distance = jnp.abs(offset)
    coarse = jnp.full_like(distance, 8)
    for edge_value in bucket_edges:
        coarse = coarse + (distance >= edge_value).astype(i32)
    return jnp.where(distance < 8, distance, coarse) + 16 * (offset > 0).astype(i32)


def one_hot(mask):
    return mask.astype(f32).astype(bf16)


def lane_numbers(rows, width):
    return lax.broadcasted_iota(i32, (rows, width), 1)


def place_kernel(routes_ref, slot_ref, kept_ref, seg_ref, bias_ref, row_ref, col_ref, diag_ref, *, capacity, local_experts):
    tokens = seg_ref.shape[1]
    routes = routes_ref[...]
    seat = (routes // local_experts) * capacity + slot_ref[...]
    kept = kept_ref[...] == 1
    line = lax.broadcasted_iota(i32, (BLOCK, tokens), 0)
    stacked = jnp.where(line == local_experts, routes, 0)
    stacked = jnp.where(line == local_experts + 1, seg_ref[...], stacked)
    for le in range(local_experts):
        key = jnp.where(kept & (routes % local_experts == le), seat, -1)
        stacked = jnp.where(line == le, key, stacked)
    row_ref[...] = stacked[: row_ref.shape[0]]
    col_ref[...] = stacked.T
    buckets = bias_ref.shape[0]
    offset = lane_numbers(buckets, 4 * BLOCK) - 2 * BLOCK
    pick = bucket_of(offset) == lax.broadcasted_iota(i32, (buckets, 4 * BLOCK), 0)
    diag_ref[...] = mm_exact(bias_ref[...], pick.astype(f32), TN)


def slots_kernel(place_ref, *refs, parts, le):
    key_refs = refs[:parts]
    rows_ref, out_ref = refs[parts:]
    direct = len(out_ref.shape) == 4
    slots = out_ref.shape[0] * out_ref.shape[2] if direct else out_ref.shape[1]
    tokens = rows_ref.shape[1]
    for j in range(parts):
        whole = (place_ref[0] + j) % parts
        key = key_refs[j][le : le + 1, :]
        table = lax.broadcasted_iota(i32, (slots, tokens), 0) == key
        rows = mm(one_hot(table), rows_ref[whole])
        if direct:
            by_group(rows, out_ref, whole)
        else:
            out_ref[whole] = rows.astype(bf16)


def by_group(rows, out_ref, place):
    capacity = out_ref.shape[2]
    for group in range(out_ref.shape[0]):
        piece = rows[group * capacity : (group + 1) * capacity]
        out_ref[group, place] = piece.astype(bf16)


def qkv_kernel(tok_ref, gain_ref, w_ref, qkv_ref, turned_ref, low_ref):
    @pl.when(pl.program_id(0) == 0)
    def _():
        values = tok_ref[...].astype(f32)
        inverse = lax.rsqrt(jnp.mean(values * values, axis=-1, keepdims=True) + eps)
        normed = values * inverse * gain_ref[...]
        low_ref[...] = normed.astype(bf16)
        turned_ref[...] = normed.T.astype(bf16)

    qkv_ref[...] = mm(low_ref[...], w_ref[...]).astype(bf16)


def attend_kernel(q_ref, k_ref, v_ref, row_ids_ref, cols_ref, diag_ref, att_ref, probs_ref, *, seg_line, head_start):
    length = k_ref.shape[0]
    blocks = length // BLOCK
    lane = lane_numbers(1, BLOCK)
    half = BLOCK // 2
    scale = half**-0.5
    keys = k_ref[...]
    vals = v_ref[...]
    row_ids = row_ids_ref[seg_line : seg_line + 1, :]
    bias_tiles = []
    for s in range(2):
        diag = diag_ref[pl.ds(head_start + 2 * pl.program_id(0) + s, 1), :]
        spread = jnp.broadcast_to(diag, (BLOCK, 4 * BLOCK))
        tile = pltpu.roll(spread, 0, 1, stride=1, stride_axis=0)[:, BLOCK:].T
        low_far = jnp.broadcast_to(diag[:, 1:2], (BLOCK, BLOCK))
        high_far = jnp.broadcast_to(diag[:, 4 * BLOCK - 1 :], (BLOCK, BLOCK))
        bias_tiles.append((low_far, tile, high_far))
    turned_vals = vals.astype(f32).T.astype(bf16)
    upper = lax.broadcasted_iota(i32, (BLOCK, 1), 0) < half
    for i in range(blocks):
        rows = slice(i * BLOCK, (i + 1) * BLOCK)
        same = cols_ref[:, seg_line : seg_line + 1] == row_ids[:, rows]
        queries = q_ref[rows, :]
        outs = []
        for s in range(2):
            mask = jnp.where(lane // half == s, scale, 0.0).astype(bf16)
            scores = mm(keys, queries * mask, NT)
            low_far, tile, high_far = bias_tiles[s]
            pieces = []
            for j in range(blocks):
                if j - i < -1:
                    pieces.append(low_far)
                elif j - i > 1:
                    pieces.append(high_far)
                else:
                    start = (j - i + 1) * BLOCK
                    pieces.append(tile[start : start + BLOCK])
            scores = scores + jnp.concatenate(pieces, axis=0)
            scores = jnp.where(same, scores, -1000000000.0)
            top = jnp.max(scores, axis=0, keepdims=True)
            grown = jnp.exp(scores - top)
            probs = (grown * (1.0 / jnp.sum(grown, axis=0, keepdims=True))).astype(bf16)
            probs_ref[s, :, rows] = probs
            outs.append(mm(turned_vals, probs))
        att_ref[rows, :] = jnp.where(upper, outs[0], outs[1]).T.astype(bf16)


def chosen_of(router, cols_ref, line):
    pick = cols_ref[:, line : line + 1] == lane_numbers(*router.shape)
    return pick, jnp.sum(jnp.where(pick, router, 0.0), axis=-1, keepdims=True)


def route_kernel(tok_ref, att_a_ref, att_b_ref, w_out_ref, gain_ref, w_router_ref, rows_ref, residual_ref, router_ref, sent_ref):
    near = att_a_ref.shape[1]
    branch = mm(att_a_ref[...], w_out_ref[:near]) + mm(att_b_ref[...], w_out_ref[near:])
    residual = tok_ref[...].astype(f32) + branch
    residual_ref[...] = residual
    inverse = lax.rsqrt(jnp.mean(residual * residual, axis=-1, keepdims=True) + eps)
    normed = residual * inverse * gain_ref[...]
    low = normed.astype(bf16)
    tokens = low.shape[0]
    direct = len(sent_ref.shape) == 4
    local_experts = sent_ref.shape[1] if direct else sent_ref.shape[0]
    slots = sent_ref.shape[0] * sent_ref.shape[2] if direct else sent_ref.shape[1]
    for index in range(local_experts):
        table = lax.broadcasted_iota(i32, (slots, tokens), 0) == rows_ref[index : index + 1, :]
        rows = mm(one_hot(table), low)
        if direct:
            by_group(rows, sent_ref, index)
        else:
            sent_ref[index] = rows.astype(bf16)
    w_high, w_low = split(w_router_ref[...])
    low_rest = (normed - low.astype(f32)).astype(bf16)
    experts = w_high.shape[1]
    logits = mm(low, jnp.concatenate([w_high, w_low], axis=1))
    logits = logits[:, :experts] + logits[:, experts:] + mm(low_rest, w_high)
    top = jnp.max(logits, axis=-1, keepdims=True)
    grown = jnp.exp(logits - top)
    router = grown / jnp.sum(grown, axis=-1, keepdims=True)
    router_ref[...] = router


def expert_kernel(place_ref, x_ref, cot_ref, w_in_ref, w_back_ref, *refs, parts, le, groups, order, olds):
    count = len(order)
    refs = refs[olds:]
    back_refs = refs[:count]
    act_ref, gp_ref = refs[count : count + 2]
    x_buf, g_buf, w_in_buf, w_back_buf, act_buf, gp_buf, back_buf = refs[count + 2 : -4]
    x_sem, g_sem, w_sem, put_sem = refs[-4:]
    place = place_ref[0]
    whole = [(place + j) % parts for j in order]
    load_in = pltpu.make_async_copy(w_in_ref.at[le], w_in_buf, w_sem.at[0])
    load_back = pltpu.make_async_copy(w_back_ref.at[le], w_back_buf, w_sem.at[1])
    load_in.start()
    loads = []
    for at in range(count):
        loads.append(
            (
                pltpu.make_async_copy(x_ref.at[whole[at]], x_buf.at[at], x_sem.at[at]),
                pltpu.make_async_copy(cot_ref.at[whole[at]], g_buf.at[at], g_sem.at[at]),
            )
        )
        loads[at][0].start()
    load_back.start()
    for at in range(count):
        loads[at][1].start()
    load_in.wait()
    scale = (2.0 / jnp.pi) ** 0.5
    slots, model = x_buf.shape[1:]
    hidden = act_buf.shape[2]
    spare = back_buf.shape[1] - slots
    line = lax.broadcasted_iota(i32, (spare, BLOCK), 0)
    capacity = slots // groups
    puts = []

    def put(source, target, kind, at):
        copy = pltpu.make_async_copy(source, target, put_sem.at[kind, at])
        copy.start()
        puts.append(copy)

    span = 2
    for first in range(0, count, span):
        ats = range(first, first + span)
        for at in ats:
            loads[at][0].wait()
        pre = mm(x_buf[first : first + span].reshape(span * slots, model), w_in_buf[...])
        for at in ats:
            loads[at][1].wait()
        if first == 0:
            load_back.wait()
        grad = mm(g_buf[first : first + span].reshape(span * slots, model), w_back_buf[...], NT)
        square = pre * pre
        slant = jnp.tanh(scale * pre * (1.0 + 0.044715 * square))
        act = (0.5 * pre * (1.0 + slant)).astype(bf16)
        act_buf[first : first + span] = act.reshape(span, slots, hidden)
        slope = 0.5 * (1.0 + slant) + 0.5 * pre * (1.0 - slant * slant) * (
            scale * (1.0 + 3.0 * 0.044715 * square)
        )
        gp = (grad * slope).astype(bf16)
        gp_buf[first : first + span] = gp.reshape(span, slots, hidden)
        back = mm(gp, w_in_buf[...], NT).astype(bf16)
        back_buf[first : first + span, :slots] = back.reshape(span, slots, model)
        all_dots = jnp.sum(act.astype(f32) * grad, axis=-1, keepdims=True)
        for at in ats:
            put(act_buf.at[at], act_ref.at[whole[at]], 0, at)
            put(gp_buf.at[at], gp_ref.at[whole[at]], 1, at)
            dots = all_dots[(at - first) * slots : (at - first + 1) * slots]
            dots = jnp.broadcast_to(dots, (slots, BLOCK)).T
            laid = jnp.zeros((spare, BLOCK), f32)
            for group in range(groups):
                piece = dots[:1, group * capacity : (group + 1) * capacity]
                piece = jnp.concatenate([piece, jnp.zeros((1, BLOCK - capacity), f32)], axis=1)
                laid = jnp.where(line == group, piece, laid)
            back_buf[at, slots:] = jnp.zeros((spare, model), bf16)
            back_buf[at, slots:, :BLOCK] = laid.astype(bf16)
            put(back_buf.at[at], back_refs[at], 2, at)
    for copy in puts:
        copy.wait()


def expert_weights_kernel(own_ref, x_ref, cot_ref, gp_ref, w_router_ref, all_act_ref, w_back_ref, *refs, le, local_experts):
    in_ref, back_ref, out_ref, gs_ref, gate_ref, turned_ref = refs[-6:]
    parts = x_ref.shape[0]

    def flat(values):
        return values.reshape(-1, values.shape[-1])

    @pl.when(pl.program_id(0) == 0)
    def _():
        w_high, w_low = split(w_router_ref[...])
        number = own_ref[0] * local_experts + le
        for part in range(parts):
            rows = x_ref[part]
            logits = mm(rows, w_high) + mm(rows, w_low)
            grown = jnp.exp(logits - jnp.max(logits, axis=-1, keepdims=True))
            pick = lane_numbers(*logits.shape) == number
            gate = jnp.sum(jnp.where(pick, grown, 0.0), axis=-1, keepdims=True)
            gate = gate / jnp.sum(grown, axis=-1, keepdims=True)
            gate_ref[part] = gate
            gs_ref[part] = (cot_ref[part].astype(f32) * gate).astype(bf16)
        turned_ref[...] = flat(x_ref[...]).T

    gp = (gp_ref[...].astype(f32) * gate_ref[...]).astype(bf16)
    in_ref[0] = mm(turned_ref[...], flat(gp))
    third = back_ref.shape[1]
    begin = pl.multiple_of(pl.program_id(0) * third, third)
    back_ref[0] = mm(flat(all_act_ref[:, :, pl.ds(begin, third)]), flat(gs_ref[...]), TN)
    out = mm(flat(all_act_ref[...]), w_back_ref[0])
    slots = out.shape[0] // parts
    for part in range(parts):
        rows = out[part * slots : (part + 1) * slots]
        if len(out_ref.shape) == 5:
            by_group(rows, out_ref.at[part], 0)
        else:
            out_ref[part, 0] = rows.astype(bf16)


def middle_kernel(residual_ref, cot_ref, gain_ref, w_router_ref, router_ref, cols_ref, w_out_ref, *refs, capacity, stride):
    grad_res_ref, branch_ref, att_ref, extra_ref = refs[-4:]
    back_refs = refs[:-4]
    local_experts = len(back_refs)
    tokens = residual_ref.shape[0]
    rows = None
    grad_gate = None
    for index, back_ref in enumerate(back_refs):
        key = cols_ref[:, index : index + 1]
        group = key // capacity
        number = lane_numbers(tokens, back_ref.shape[0])
        back = back_ref[...]
        part = mm(one_hot(number == key + group * (stride - capacity)), back)
        lines = mm(one_hot(number == group * stride + capacity), back[:, :BLOCK])
        slot = lane_numbers(tokens, BLOCK) == key - group * capacity
        picked = jnp.sum(jnp.where(slot, lines, 0.0), axis=-1, keepdims=True)
        rows = part if rows is None else rows + part
        grad_gate = picked if grad_gate is None else grad_gate + picked
    router = router_ref[...]
    pick, chosen = chosen_of(router, cols_ref, local_experts)
    grad_logits = router * (pick.astype(f32) - chosen) * grad_gate
    residual = residual_ref[...]
    inverse = lax.rsqrt(jnp.mean(residual * residual, axis=-1, keepdims=True) + eps)
    gain = gain_ref[...]
    scaled = residual * inverse
    logits_high, logits_low = split(grad_logits)
    w_high, w_low = split(w_router_ref[...])
    grad_normed = chosen * rows + mm(
        jnp.concatenate([logits_high, logits_low, logits_high], axis=1),
        jnp.concatenate([w_high, w_high, w_low], axis=1),
        NT,
    )
    weighted = grad_normed * gain
    lean = jnp.mean(weighted * residual, axis=-1, keepdims=True)
    grad_res = cot_ref[...].astype(f32) + (
        inverse * weighted - residual * (inverse * inverse * inverse) * lean
    )
    grad_res_ref[...] = grad_res
    low = grad_res.astype(bf16)
    branch_ref[...] = low
    att_ref[...] = mm(low, w_out_ref[...], NT).astype(bf16)
    gain_grad = jnp.sum(grad_normed * scaled, axis=0, keepdims=True)
    normed_high, normed_low = split(scaled * gain)
    experts = logits_high.shape[1]
    router_grad = mm(jnp.concatenate([logits_high, logits_low], axis=1), normed_high, TN)
    router_grad = router_grad[:experts] + router_grad[experts:] + mm(logits_high, normed_low, TN)
    spare = extra_ref.shape[1] - router_grad.shape[0] - 1
    both = jnp.concatenate(
        [router_grad, gain_grad, jnp.zeros((spare, gain_grad.shape[1]), f32)], axis=0
    )
    extra_ref[...] = both.T.astype(bf16)


def attend_back_kernel(q_ref, k_ref, v_ref, probs_ref, grad_ref, turned_ref, *refs, kind, head_start, buckets):
    if kind == 0:
        att_a_ref, att_b_ref, branch_ref, extra_ref = refs[:4]
    else:
        old_diag_ref = refs[0]
    if kind == 2:
        old_weight_ref = refs[1]
    dq_ref, dk_ref, dv_ref, weight_ref, diag_ref, slope_ref = refs[-6:]
    step = pl.program_id(0)
    length = k_ref.shape[0]
    blocks = length // BLOCK
    lane = lane_numbers(1, BLOCK)
    half = BLOCK // 2
    scale = half**-0.5
    keys = k_ref[...]
    vals = v_ref[...]
    queries = q_ref[...]
    grads = grad_ref[...]
    static_columns = weight_ref.shape[1]

    @pl.when(step == 0)
    def _():
        if kind == 0:
            diag_ref[...] = jnp.zeros_like(diag_ref)
            model = branch_ref.shape[1]
            tail = extra_ref.shape[1]
            begin = static_columns - tail - model
            near = att_a_ref.shape[1]
            branch = branch_ref[...]
            weight_ref[:near, begin : begin + model] = mm(att_a_ref[...], branch, TN).astype(bf16)
            weight_ref[near:, begin : begin + model] = mm(att_b_ref[...], branch, TN).astype(bf16)
            weight_ref[:, begin + model :] = extra_ref[...]
        else:
            diag_ref[...] = old_diag_ref[...]
        if kind == 2:
            weight_ref[:, : old_weight_ref.shape[1]] = old_weight_ref[...]

    across = lax.broadcasted_iota(i32, (BLOCK, BLOCK), 0) + lane_numbers(BLOCK, BLOCK)
    flip = one_hot(across == BLOCK - 1)
    turned_keys = keys.astype(f32).T.astype(bf16)
    dq = [[] for _ in range(blocks)]
    dk, dv = [], []
    for s in range(2):
        mask = jnp.where(lane // half == s, 1.0, 0.0).astype(bf16)
        near = [None, None, None]
        far = [None, None]
        for i in range(blocks):
            rows = slice(i * BLOCK, (i + 1) * BLOCK)
            probs = probs_ref[s, :, rows].astype(f32)
            grad_probs = mm(vals, grads[rows] * mask, NT)
            delta = jnp.sum(probs * grad_probs, axis=0, keepdims=True)
            slope = probs * (grad_probs - delta)
            low = slope.astype(bf16)
            slope_ref[s, :, rows] = low
            dq[i].append(mm(turned_keys, low))
            for j in range(blocks):
                piece = slope[j * BLOCK : (j + 1) * BLOCK]
                apart = j - i
                if abs(apart) <= 1:
                    old = near[1 - apart]
                    near[1 - apart] = piece if old is None else old + piece
                else:
                    old = far[int(apart > 0)]
                    far[int(apart > 0)] = piece if old is None else old + piece
        dk.append(mm(slope_ref[s], queries))
        dv.append(mm(probs_ref[s], grads))
        wide = jnp.concatenate([jnp.zeros_like(near[0])] + near, axis=1)
        lined = pltpu.roll(mm(flip, wide.astype(bf16)), 3 * BLOCK + 1, 1, stride=1, stride_axis=0)
        lined = jnp.concatenate([lined, far[0], far[1]], axis=1)
        diag_ref[pl.ds(head_start + 2 * step + s, 1), :] = jnp.sum(lined, axis=0, keepdims=True)
    upper = lax.broadcasted_iota(i32, (BLOCK, 1), 0) < half
    dq_low = jnp.concatenate([jnp.where(upper, *item).T for item in dq], axis=0)
    dq_low = (dq_low * scale).astype(bf16)
    left = lane < half
    dk_low = (jnp.where(left, dk[0], dk[1]) * scale).astype(bf16)
    dv_low = jnp.where(left, dv[0], dv[1]).astype(bf16)
    dq_ref[...] = dq_low
    dk_ref[...] = dk_low
    dv_ref[...] = dv_low
    begin = 0 if kind < 2 else old_weight_ref.shape[1]
    begin = pl.multiple_of(step * (3 * BLOCK) + begin, 3 * BLOCK)
    weight_ref[:, pl.ds(begin, 3 * BLOCK)] = mm(
        turned_ref[...], jnp.concatenate([dq_low, dk_low, dv_low], axis=1)
    ).astype(bf16)
    if kind == 2:

        @pl.when(step == pl.num_programs(0) - 1)
        def _():
            wide = diag_ref.shape[1]
            number = lane_numbers(buckets, wide)
            bucket = bucket_of(2 * BLOCK - number)
            bucket = jnp.where(number >= 4 * BLOCK, 15, bucket)
            bucket = jnp.where(number >= 5 * BLOCK, 31, bucket)
            pick = bucket == lax.broadcasted_iota(i32, (buckets, wide), 0)
            rows = jnp.concatenate(
                [diag_ref[...], jnp.zeros((BLOCK - diag_ref.shape[0], wide), f32)], axis=0
            )
            bias = mm_exact(pick.astype(f32), rows, NT)
            begin = static_columns - BLOCK
            weight_ref[:, begin:] = jnp.zeros((weight_ref.shape[0], BLOCK), bf16)
            weight_ref[:buckets, begin:] = bias.astype(bf16)


def tokens_kernel(tok_ref, gain_ref, w_ref, grad_res_ref, *refs):
    out_ref = refs[-1]
    parts = refs[:-1]
    groups = len(parts) // 3
    model = tok_ref.shape[1]
    grad_normed = None
    for part in range(3):
        start = part * model
        for group in range(groups):
            block = parts[3 * group + part]
            width = block.shape[1]
            piece = mm(block[...], w_ref[:, start : start + width], NT)
            grad_normed = piece if grad_normed is None else grad_normed + piece
            start += width
    values = tok_ref[...].astype(f32)
    inverse = lax.rsqrt(jnp.mean(values * values, axis=-1, keepdims=True) + eps)
    weighted = grad_normed * gain_ref[...]
    lean = jnp.mean(weighted * values, axis=-1, keepdims=True)
    out_ref[...] = grad_res_ref[...] + (
        inverse * weighted - values * (inverse * inverse * inverse) * lean
    )


def output_kernel(residual_ref, router_ref, cols_ref, rows_ref, out_ref):
    tokens = residual_ref.shape[0]
    local_experts, slots = rows_ref.shape[:2]
    mixture = None
    for index in range(local_experts):
        turned = cols_ref[:, index : index + 1] == lane_numbers(tokens, slots)
        part = mm(one_hot(turned), rows_ref[index])
        mixture = part if mixture is None else mixture + part
    _, chosen = chosen_of(router_ref[...], cols_ref, local_experts)
    out_ref[...] = (residual_ref[...] + chosen * mixture).astype(bf16)


def finish_kernel(where_ref, a_ref, b_ref, w_ref, *refs):
    qkv_ref, out_ref, gain_ref, extra_ref = refs[-4:]
    place = where_ref[2]
    parts = a_ref.shape[1]
    model = out_ref.shape[3]
    pairs = model // BLOCK
    near = pairs // 3
    for k in range(parts):
        z = (place + parts - k) % parts
        a = a_ref[0, k].astype(f32)
        b = b_ref[0, k].astype(f32)
        total = None
        for part in range(3):
            pieces = [
                (a if p < near else b)[:, ((p if p < near else p - near) * 3 + part) * BLOCK :][
                    :, :BLOCK
                ]
                for p in range(pairs)
            ]
            whole = jnp.concatenate(pieces, axis=1)
            span = slice(part * model, (part + 1) * model)
            qkv_ref[0, z, :, span] = whole
            w = w_ref[0, z, :, span].astype(f32)
            share = jnp.sum(whole * w, axis=-1, keepdims=True)
            total = share if total is None else total + share
        gain_ref[0, z] = jnp.broadcast_to(total, gain_ref.shape[2:])
        begin = near * 3 * BLOCK
        out_ref[0, z] = a[:, begin : begin + model]
        tail = a.shape[1] - begin - model
        extra_ref[0, z, :, :tail] = a[:, begin + model :]
        extra_ref[0, z, :, tail:] = b[:, (pairs - near) * 3 * BLOCK :]


def small_kernel(gain_ref, sums_ref, extra_ref, router_ref, gains_ref, bias_ref, *, experts, at):
    extras = extra_ref[:, :at].T
    router_ref[...] = extras[:experts]
    gains_ref[0:1, :] = sums_ref[...].T[0:1] / gain_ref[...]
    gains_ref[1:2, :] = extras[experts : experts + 1]
    heads, buckets = bias_ref.shape
    bias_ref[...] = extra_ref[:BLOCK, at:].T[:heads, :buckets]


def add_low(left, right):
    return (left.astype(f32) + right.astype(f32)).astype(bf16)


def tie(items, after):
    return lax.optimization_barrier((items, after))[0]


def held(kernel, start, after):
    def body(*refs):
        kernel(*refs[:start], *refs[start + len(after) :])

    return body


class Scatter:
    def __init__(self, blocks):
        self.parts = lax.axis_size("hidden")
        self.blocks = blocks
        self.count = 0

    def step(self, after=()):
        self.count += 1
        right, left = self.blocks[self.parts - self.count], self.blocks[self.count]
        if self.count > 1:
            right, left = add_low(right, self.right), add_low(left, self.left)
        right, left = tie((right, left), after)
        ways = [(a, a + 1) for a in range(self.count)]
        self.right = lax.ppermute(right, "hidden", ways)
        ways = [(a, a - 1) for a in range(self.parts - self.count, self.parts)]
        self.left = lax.ppermute(left, "hidden", ways)

    def last(self):
        return self.right, self.left

    def finish(self, after=()):
        right, left = tie(self.last(), after)
        total = self.blocks[0].astype(f32) + right.astype(f32) + left.astype(f32)
        return total.astype(bf16)


def pick_block(blocks, index):
    return lax.dynamic_index_in_dim(blocks, index, 0, keepdims=False)


class Sum:
    def __init__(self, values):
        self.groups = lax.axis_size("expert")
        self.parts = lax.axis_size("hidden")
        self.own = lax.axis_index("expert")
        self.place = lax.axis_index("hidden")
        self.core = self.own % 2
        self.chip = self.own // 2
        self.chips = self.groups // 2
        self.pair = [(a, a ^ 1) for a in range(self.groups)]
        self.width = values.shape[1]
        self.values = values

    def cores(self):
        halves = self.values.reshape(2, -1, self.width)
        got = lax.ppermute(pick_block(halves, 1 - self.core), "expert", self.pair)
        self.values = add_low(pick_block(halves, self.core), got)

    def cores_at_once(self):
        teams = [[2 * a, 2 * a + 1] for a in range(self.chips)]
        got = lax.all_to_all(
            self.values, "expert", split_axis=0, concat_axis=0, tiled=True, axis_index_groups=teams
        ).reshape(2, -1, self.width)
        self.values = add_low(got[0], got[1])

    def plane(self):
        pieces = self.values.reshape(self.chips, -1, self.width)
        total = pick_block(pieces, self.chip).astype(f32)
        for step in range(1, self.chips):
            ways = [(a, a ^ (2 * step)) for a in range(self.groups)]
            got = lax.ppermute(pick_block(pieces, self.chip ^ step), "expert", ways)
            total = total + got.astype(f32)
        self.values = total.astype(bf16)

    def line(self):
        pieces = self.values.reshape(self.parts, -1, self.width)
        total = pick_block(pieces, self.place).astype(f32)
        for step in range(1, self.parts):
            ways = [(a, (a + step) % self.parts) for a in range(self.parts)]
            got = lax.ppermute(pick_block(pieces, (self.place + step) % self.parts), "hidden", ways)
            total = total + got.astype(f32)
        self.values = total.astype(bf16)

    def line_back(self):
        pieces = [self.values]
        for step in range(1, self.parts):
            ways = [(a, (a + step) % self.parts) for a in range(self.parts)]
            pieces.append(lax.ppermute(self.values, "hidden", ways))
        self.values = jnp.stack(pieces)

    def plane_back(self):
        pieces = [self.values]
        for step in range(1, self.chips):
            ways = [(a, a ^ (2 * step)) for a in range(self.groups)]
            pieces.append(lax.ppermute(self.values, "expert", ways))
        self.values = jnp.stack(pieces)

    def cores_back(self):
        return self.values, lax.ppermute(self.values, "expert", self.pair)

    def run(self):
        self.cores()
        self.plane()
        self.line()
        self.line_back()
        self.plane_back()
        return self.cores_back()


def local(tokens, cotangent, segments, routes, slot_ids, kept_flags, gain_one, w_qkv, w_out, bias_table, gain_two, w_router, w_in, w_back):
    tok_rows, model = tokens.shape
    bucket_count, head_count = bias_table.shape
    experts = w_router.shape[1]
    local_experts = w_in.shape[0]
    hidden = w_in.shape[2]
    groups = lax.axis_size("expert")
    parts = lax.axis_size("hidden")
    own = lax.axis_index("expert")
    place = lax.axis_index("hidden")
    capacity = max(2, (5 * tok_rows + 4 * experts - 1) // (4 * experts))
    slots = groups * capacity
    pairs = head_count // 2
    shape = jax.ShapeDtypeStruct
    vmem = pl.BlockSpec(memory_space=pltpu.VMEM)
    any_space = pl.BlockSpec(memory_space=pl.ANY)
    gain_one_row = gain_one[None, :]
    gain_two_row = gain_two[None, :]
    seg_line = local_experts + 1

    def exchange(rows, axis=0):
        return lax.all_to_all(rows, "expert", split_axis=axis, concat_axis=axis, tiled=True)

    cot_near = lax.all_gather(cotangent, "hidden", axis=0, tiled=False)
    id_rows, id_cols, diag_bias = pl.pallas_call(
        functools.partial(place_kernel, capacity=capacity, local_experts=local_experts),
        out_shape=[
            shape((8, tok_rows), i32),
            shape((tok_rows, BLOCK), i32),
            shape((head_count, 4 * BLOCK), f32),
        ],
        in_specs=[vmem] * 5,
        out_specs=[vmem] * 3,
        compiler_params=params(),
        cost_estimate=cost(1e8, 1e6),
        name="place",
    )(routes[None, :], slot_ids[None, :], kept_flags[None, :], segments, bias_table)
    qkv, turned = pl.pallas_call(
        qkv_kernel,
        grid=(3,),
        out_shape=[shape((tok_rows, 3 * model), bf16), shape((model, tok_rows), bf16)],
        in_specs=[
            pl.BlockSpec((tok_rows, model), lambda j: (0, 0)),
            pl.BlockSpec((1, model), lambda j: (0, 0)),
            pl.BlockSpec((model, model), lambda j: (0, j)),
        ],
        out_specs=[
            pl.BlockSpec((tok_rows, model), lambda j: (0, j)),
            pl.BlockSpec((model, tok_rows), lambda j: (0, 0)),
        ],
        scratch_shapes=[pltpu.VMEM((tok_rows, model), bf16)],
        compiler_params=params(("arbitrary",)),
        cost_estimate=cost(6 * tok_rows * model * model, 8 * model * model * 2),
        name="qkv",
    )(tokens, gain_one_row, w_qkv)

    def pair_spec(offset):
        return pl.BlockSpec((tok_rows, BLOCK), lambda p: (0, offset + p))

    steps = pairs // 2
    attended, probs = [], []
    for half in range(2):
        start = half * steps
        att, prob = pl.pallas_call(
            functools.partial(attend_kernel, seg_line=seg_line, head_start=2 * start),
            grid=(steps,),
            out_shape=[
                shape((tok_rows, steps * BLOCK), bf16),
                shape((2 * steps, tok_rows, tok_rows), bf16),
            ],
            in_specs=[
                pair_spec(start),
                pair_spec(pairs + start),
                pair_spec(2 * pairs + start),
                pl.BlockSpec((8, tok_rows), lambda p: (0, 0)),
                pl.BlockSpec((tok_rows, BLOCK), lambda p: (0, 0)),
                pl.BlockSpec((head_count, 4 * BLOCK), lambda p: (0, 0)),
            ],
            out_specs=[
                pair_spec(0),
                pl.BlockSpec((2, tok_rows, tok_rows), lambda p: (p, 0, 0)),
            ],
            compiler_params=params(("arbitrary",)),
            cost_estimate=cost(steps * 4e9, steps * 3e6),
            name="attend",
        )(qkv, qkv, qkv, id_rows, id_cols, diag_bias)
        attended.append(att)
        probs.append(prob)

    def by_slots(count):
        if direct:
            return shape((groups, count, capacity, model), bf16)
        return shape((count, slots, model), bf16)

    direct = capacity % 8 == 0
    residual, router, sent_rows = pl.pallas_call(
        route_kernel,
        out_shape=[
            shape((tok_rows, model), f32),
            shape((tok_rows, experts), f32),
            by_slots(local_experts),
        ],
        in_specs=[vmem] * 7,
        out_specs=[vmem] * 3,
        compiler_params=params(),
        cost_estimate=cost(6e9, 6e6),
        name="route",
    )(tokens, *attended, w_out, gain_two_row, w_router, id_rows)

    place_arr = place.astype(i32).reshape(1)
    own_arr = own.astype(i32).reshape(1)
    spare = -(-groups // 16) * 16
    block = shape((slots + spare, model), bf16)
    stack = shape((parts, slots, hidden), bf16)
    smem = pl.BlockSpec(memory_space=pltpu.SMEM)
    third = hidden // 3

    def run_experts(le, order, olds, after=()):
        count = len(order)
        results = pl.pallas_call(
            held(
                functools.partial(
                    expert_kernel, parts=parts, le=le, groups=groups, order=order, olds=len(olds)
                ),
                5 + len(olds),
                after,
            ),
            out_shape=[block] * count + [stack, stack],
            in_specs=[smem] + [any_space] * (4 + len(olds) + len(after)),
            out_specs=[any_space] * (count + 2),
            input_output_aliases={5 + n: count + n for n in range(len(olds))},
            scratch_shapes=[
                pltpu.VMEM((count, slots, model), bf16),
                pltpu.VMEM((count, slots, model), bf16),
                pltpu.VMEM((model, hidden), bf16),
                pltpu.VMEM((hidden, model), bf16),
                pltpu.VMEM((count, slots, hidden), bf16),
                pltpu.VMEM((count, slots, hidden), bf16),
                pltpu.VMEM((count, slots + spare, model), bf16),
                pltpu.SemaphoreType.DMA((count,)),
                pltpu.SemaphoreType.DMA((count,)),
                pltpu.SemaphoreType.DMA((2,)),
                pltpu.SemaphoreType.DMA((3, count)),
            ],
            compiler_params=params(),
            cost_estimate=cost(4 * count * slots * model * hidden, 1e7),
            name="experts",
        )(place_arr, rows_all[le], cot_all[le], w_in, w_back, *olds, *after)
        return results[:count], list(results[count:])

    def run_both(le, after=()):
        ends = list(range(1, parts, 2))
        rest = list(range(0, parts, 2))
        backs = [None] * parts
        some, kept = run_experts(le, ends, [], after)
        for j, item in zip(ends, some):
            backs[j] = item
        some, kept = run_experts(le, rest, kept)
        for j, item in zip(rest, some):
            backs[j] = item
        return backs, kept

    def run_weights(le, kept, olds, after):
        act, gp = kept
        stack_spec = pl.BlockSpec((parts, slots, model), lambda j: (0, 0, 0))
        hidden_spec = pl.BlockSpec((parts, slots, third), lambda j: (0, 0, j))
        return pl.pallas_call(
            held(
                functools.partial(expert_weights_kernel, le=le, local_experts=local_experts),
                7 + len(olds),
                after,
            ),
            grid=(3,),
            out_shape=[
                shape((local_experts, model, hidden), f32),
                shape((local_experts, hidden, model), f32),
                shape((parts,) + by_slots(local_experts).shape, bf16),
            ],
            in_specs=[
                smem,
                stack_spec,
                stack_spec,
                hidden_spec,
                pl.BlockSpec((model, experts), lambda j: (0, 0)),
                pl.BlockSpec((parts, slots, hidden), lambda j: (0, 0, 0)),
                pl.BlockSpec((1, hidden, model // 3), lambda j: (le, 0, j)),
            ]
            + [any_space] * (len(olds) + len(after)),
            out_specs=[
                pl.BlockSpec((1, model, third), lambda j: (le, 0, j)),
                pl.BlockSpec((1, third, model), lambda j: (le, j, 0)),
                pl.BlockSpec(
                    (parts, groups, 1, capacity, model // 3), lambda j: (0, 0, le, 0, j)
                )
                if direct
                else pl.BlockSpec((parts, 1, slots, model // 3), lambda j: (0, le, 0, j)),
            ],
            scratch_shapes=[
                pltpu.VMEM((parts, slots, model), bf16),
                pltpu.VMEM((parts, slots, 1), f32),
                pltpu.VMEM((model, parts * slots), bf16),
            ],
            input_output_aliases={7 + n: n for n in range(len(olds))},
            compiler_params=params(("arbitrary",)),
            cost_estimate=cost(4 * parts * slots * model * hidden, 1.3e7),
            name="expert_weights",
        )(own_arr, rows_all[le], cot_all[le], gp, w_router, act, w_back, *olds, *after)

    def own_slots(le, ids, after):
        return pl.pallas_call(
            held(functools.partial(slots_kernel, parts=parts, le=le), 2 + parts, after),
            out_shape=by_slots(parts),
            in_specs=[smem] + [vmem] * (parts + 1) + [any_space] * len(after),
            out_specs=vmem,
            compiler_params=params(),
            cost_estimate=cost(2e9, 6e6),
            name="slots",
        )(place_arr, *ids, cot_near, *after)

    def exchange_slots(rows):
        if not direct:
            return exchange(rows, 1)
        return exchange(rows).transpose(1, 0, 2, 3).reshape(-1, slots, model)

    here = exchange_slots(sent_rows)
    rows_all = [
        lax.all_gather(here[le], "hidden", axis=0, tiled=False) for le in range(local_experts)
    ]
    ids = [id_rows]
    far_ids = tie(id_rows, here)
    for step in range(1, parts):
        ways = [((a + step) % parts, a) for a in range(parts)]
        ids.append(lax.ppermute(far_ids, "hidden", ways))
    cot_slots = [own_slots(0, ids, [here])]
    cot_slots.append(own_slots(1, ids, cot_slots))
    cot_all = [exchange_slots(cot_slots[0])]
    cot_all.append(exchange_slots(tie(cot_slots[1], cot_all[0])))
    backs, kept = run_both(0, cot_slots[1:])
    sum_first = Scatter(backs)
    sum_first.step()
    grads = run_weights(0, kept, [], [])
    sum_first.step(grads)
    backs, kept_second = run_both(1, grads[:1])
    sum_second = Scatter(backs)
    sum_second.step()
    sum_second.step(sum_first.last())
    sum_first.step()
    grads = run_weights(1, kept_second, grads, sum_second.last()[:1])

    def with_dots(total):
        rows = total[:slots].reshape(groups, capacity, model)
        dots = total[slots : slots + groups].reshape(groups, 1, model)
        dots = jnp.pad(dots, ((0, 0), (0, stride - capacity - 1), (0, 0)))
        return jnp.concatenate([rows, dots], axis=1).reshape(groups * stride, model)

    stride = -(-(capacity + 1) // 8) * 8
    back_first = exchange(with_dots(sum_first.finish()))
    sum_second.step(sum_first.last())
    back_second = sum_second.finish((back_first, grads))
    backs = [back_first, exchange(with_dots(back_second))]
    grad_w_in, grad_w_back, out_sums = grads
    extra_width = -(-(experts + 1) // BLOCK) * BLOCK

    grad_res, grad_branch, grad_att, extra = pl.pallas_call(
        functools.partial(middle_kernel, capacity=capacity, stride=stride),
        out_shape=[
            shape((tok_rows, model), f32),
            shape((tok_rows, model), bf16),
            shape((tok_rows, model), bf16),
            shape((model, extra_width), bf16),
        ],
        in_specs=[vmem] * (7 + local_experts),
        out_specs=[vmem] * 4,
        compiler_params=params(),
        cost_estimate=cost(6e9, 8e6),
        name="middle",
    )(residual, cotangent, gain_two_row, w_router, router, id_cols, w_out, *backs)

    out_rows = lax.psum_scatter(out_sums, "hidden", scatter_dimension=0, tiled=False)
    out_ready = out_rows
    out_rows = exchange_slots(out_rows)
    output = pl.pallas_call(
        output_kernel,
        out_shape=shape((tok_rows, model), bf16),
        in_specs=[vmem] * 4,
        out_specs=vmem,
        compiler_params=params(),
        cost_estimate=cost(1e9, 4e6),
        name="output",
    )(residual, router, id_cols, out_rows)

    def run_back(kind, start, count, extras, width):
        inner = start % steps
        return pl.pallas_call(
            functools.partial(
                attend_back_kernel,
                kind=kind,
                head_start=2 * start,
                buckets=bucket_count,
            ),
            grid=(count,),
            out_shape=[shape((tok_rows, count * BLOCK), bf16)] * 3
            + [shape((model, width), bf16), shape((16, 6 * BLOCK), f32)],
            in_specs=[
                pair_spec(start),
                pair_spec(pairs + start),
                pair_spec(2 * pairs + start),
                pl.BlockSpec((2, tok_rows, tok_rows), lambda p: (inner + p, 0, 0)),
                pair_spec(start),
                pl.BlockSpec((model, tok_rows), lambda p: (0, 0)),
            ]
            + [pl.BlockSpec(item.shape, lambda p: (0, 0)) for item in extras],
            out_specs=[pair_spec(0)] * 3
            + [
                pl.BlockSpec((model, width), lambda p: (0, 0)),
                pl.BlockSpec((16, 6 * BLOCK), lambda p: (0, 0)),
            ],
            scratch_shapes=[pltpu.VMEM((2, tok_rows, tok_rows), bf16)],
            compiler_params=params(("arbitrary",)),
            cost_estimate=cost(count * 4e9, count * 3e6),
            name="attend_back",
        )(qkv, qkv, qkv, probs[start // steps], grad_att, turned, *extras)

    wide = 3 * BLOCK
    early = pairs // 3
    first = run_back(
        0, 0, early, [*attended, grad_branch, extra], wide * early + model + extra_width
    )
    sum_a = Sum(first[3])
    sum_a.cores()
    second = run_back(1, early, 1, [first[4]], wide)
    sum_a.values = tie(sum_a.values, second[3])
    sum_a.plane()
    third_part = run_back(
        2, early + 1, pairs - early - 1, [second[4], second[3]], wide * (pairs - early) + BLOCK
    )
    sum_b = Sum(tie(third_part[3], sum_a.values))
    sum_b.cores()
    grad_parts = [*first[:3], *second[:3], *third_part[:3]]
    grad_tokens = pl.pallas_call(
        held(tokens_kernel, 4 + len(grad_parts), [sum_b.values]),
        out_shape=shape((tok_rows, model), f32),
        in_specs=[vmem] * (4 + len(grad_parts)) + [any_space],
        out_specs=vmem,
        compiler_params=params(),
        cost_estimate=cost(3e9, 1e7),
        name="tokens_grad",
    )(tokens, gain_one_row, w_qkv, grad_res, *grad_parts, sum_b.values)
    sum_a.line()
    sum_b.plane()
    sum_a.line_back()
    sum_b.line()
    sum_a.plane_back()
    sum_b.line_back()
    sum_b.values = tie(sum_b.values, (out_rows, grad_tokens))
    sums = [sum_a.cores_back()]
    sum_b.plane_back()
    sum_b.values = tie(sum_b.values, output)
    sums.append(sum_b.cores_back())

    chips = groups // 2
    rows = model // (groups * parts)
    where = jnp.stack([own % 2, own // 2, place]).astype(i32)

    tail = extra_width + BLOCK
    widths = (3 * model, model, BLOCK, tail)

    def finish(team, a, b, olds):
        def piece_spec(width):
            return pl.BlockSpec((1, parts, rows, width), lambda s, at: (s, 0, 0, 0))

        def whole_spec(width):
            return pl.BlockSpec(
                (1, parts, rows, width),
                lambda s, at: ((at[0] ^ team) * chips + (at[1] ^ s), 0, 0, 0),
            )

        return pl.pallas_call(
            finish_kernel,
            grid_spec=pltpu.PrefetchScalarGridSpec(
                num_scalar_prefetch=1,
                grid=(chips,),
                in_specs=[
                    piece_spec(a.shape[-1]),
                    piece_spec(b.shape[-1]),
                    whole_spec(3 * model),
                ]
                + [any_space] * len(olds),
                out_specs=[whole_spec(width) for width in widths],
            ),
            out_shape=[shape((groups, parts, rows, width), f32) for width in widths],
            input_output_aliases={4 + n: n for n in range(len(olds))},
            compiler_params=params(("arbitrary",)),
            cost_estimate=cost(1e8, 1e7),
            name="finish",
        )(where, a, b, w_qkv.reshape(groups, parts, rows, 3 * model), *olds)

    (own_a, got_a), (own_b, got_b) = sums
    finished = finish(0, own_a, own_b, [])
    finished = finish(1, got_a, got_b, finished)
    grad_w_qkv, grad_w_out, gain_sums, extras = [
        item.reshape(model, item.shape[-1]) for item in finished
    ]
    grad_router, gains, grad_bias = pl.pallas_call(
        functools.partial(small_kernel, experts=experts, at=extra_width),
        out_shape=[
            shape((experts, model), f32),
            shape((2, model), f32),
            shape((head_count, bucket_count), f32),
        ],
        in_specs=[vmem] * 3,
        out_specs=[vmem] * 3,
        compiler_params=params(),
        cost_estimate=cost(1e6, 2e6),
        name="small",
    )(gain_one_row, gain_sums, extras)
    return (
        output,
        grad_tokens,
        gains[0],
        grad_w_qkv,
        grad_w_out,
        grad_bias.T,
        gains[1],
        grad_router.T,
        grad_w_in,
        grad_w_back,
    )


def solution(mesh):
    return jax.shard_map(
        local,
        mesh=mesh,
        in_specs=(
            P(("expert", "hidden"), None),
            P(("expert", "hidden"), None),
            P(("expert", "hidden"), None),
            P(("expert", "hidden")),
            P(("expert", "hidden")),
            P(("expert", "hidden")),
            P(),
            P(),
            P(),
            P(),
            P(),
            P(),
            P("expert", None, "hidden"),
            P("expert", "hidden", None),
        ),
        out_specs=(
            P(("expert", "hidden"), None),
            P(("expert", "hidden"), None),
            P(),
            P(),
            P(),
            P(),
            P(),
            P(),
            P("expert", None, "hidden"),
            P("expert", "hidden", None),
        ),
        check_vma=False,
    )
```

```python
import functools

import jax
import jax.numpy as jnp
from jax import lax
from jax.experimental import pallas as pl
from jax.experimental.pallas import tpu as pltpu
from jax.sharding import PartitionSpec as P

eps = 1e-06
bucket_edges = (12, 16, 23, 32, 46, 64, 91)
highest = lax.Precision.HIGHEST
f32 = jnp.float32
bf16 = jnp.bfloat16
i32 = jnp.int32
BLOCK = 128
VMEM_BYTES = 56 << 20
NN = (((1,), (0,)), ((), ()))
NT = (((1,), (1,)), ((), ()))
TN = (((0,), (0,)), ((), ()))


def mm(left, right, dims=NN):
    return lax.dot_general(left, right, dims, preferred_element_type=f32)


def mm_exact(left, right, dims=NN):
    return lax.dot_general(left, right, dims, precision=highest, preferred_element_type=f32)


def split(values):
    high = values.astype(bf16)
    return high, (values - high.astype(f32)).astype(bf16)


def params(semantics=None):
    if semantics is None:
        return pltpu.CompilerParams(vmem_limit_bytes=VMEM_BYTES)
    return pltpu.CompilerParams(vmem_limit_bytes=VMEM_BYTES, dimension_semantics=semantics)


def cost(flops, moved):
    return pl.CostEstimate(
        flops=int(flops) // 100, bytes_accessed=int(moved) // 100, transcendentals=0
    )


def bucket_of(offset):
    distance = jnp.abs(offset)
    coarse = jnp.full_like(distance, 8)
    for edge_value in bucket_edges:
        coarse = coarse + (distance >= edge_value).astype(i32)
    return jnp.where(distance < 8, distance, coarse) + 16 * (offset > 0).astype(i32)


def one_hot(mask):
    return mask.astype(f32).astype(bf16)


def lane_numbers(rows, width):
    return lax.broadcasted_iota(i32, (rows, width), 1)


def place_kernel(routes_ref, slot_ref, kept_ref, seg_ref, bias_ref, row_ref, col_ref, diag_ref, *, capacity, local_experts):
    tokens = seg_ref.shape[1]
    routes = routes_ref[...]
    seat = (routes // local_experts) * capacity + slot_ref[...]
    kept = kept_ref[...] == 1
    line = lax.broadcasted_iota(i32, (BLOCK, tokens), 0)
    stacked = jnp.where(line == local_experts, routes, 0)
    stacked = jnp.where(line == local_experts + 1, seg_ref[...], stacked)
    for le in range(local_experts):
        key = jnp.where(kept & (routes % local_experts == le), seat, -1)
        stacked = jnp.where(line == le, key, stacked)
    row_ref[...] = stacked[: row_ref.shape[0]]
    col_ref[...] = stacked.T
    buckets = bias_ref.shape[0]
    offset = lane_numbers(buckets, 4 * BLOCK) - 2 * BLOCK
    pick = bucket_of(offset) == lax.broadcasted_iota(i32, (buckets, 4 * BLOCK), 0)
    diag_ref[...] = mm_exact(bias_ref[...], pick.astype(f32), TN)


def slots_kernel(place_ref, *refs, parts, le):
    key_refs = refs[:parts]
    rows_ref, out_ref = refs[parts:]
    direct = len(out_ref.shape) == 4
    slots = out_ref.shape[0] * out_ref.shape[2] if direct else out_ref.shape[1]
    tokens = rows_ref.shape[1]
    for j in range(parts):
        whole = (place_ref[0] + j) % parts
        key = key_refs[j][le : le + 1, :]
        table = lax.broadcasted_iota(i32, (slots, tokens), 0) == key
        rows = mm(one_hot(table), rows_ref[whole])
        if direct:
            by_group(rows, out_ref, whole)
        else:
            out_ref[whole] = rows.astype(bf16)


def by_group(rows, out_ref, place):
    capacity = out_ref.shape[2]
    for group in range(out_ref.shape[0]):
        piece = rows[group * capacity : (group + 1) * capacity]
        out_ref[group, place] = piece.astype(bf16)


def qkv_kernel(tok_ref, gain_ref, w_ref, qkv_ref, turned_ref, low_ref):
    @pl.when(pl.program_id(0) == 0)
    def _():
        values = tok_ref[...].astype(f32)
        inverse = lax.rsqrt(jnp.mean(values * values, axis=-1, keepdims=True) + eps)
        normed = values * inverse * gain_ref[...]
        low_ref[...] = normed.astype(bf16)
        turned_ref[...] = normed.T.astype(bf16)

    qkv_ref[...] = mm(low_ref[...], w_ref[...]).astype(bf16)


def attend_kernel(q_ref, k_ref, v_ref, row_ids_ref, cols_ref, diag_ref, att_ref, probs_ref, *, seg_line, head_start):
    length = k_ref.shape[0]
    blocks = length // BLOCK
    lane = lane_numbers(1, BLOCK)
    half = BLOCK // 2
    scale = half**-0.5
    keys = k_ref[...]
    vals = v_ref[...]
    row_ids = row_ids_ref[seg_line : seg_line + 1, :]
    bias_tiles = []
    for s in range(2):
        diag = diag_ref[pl.ds(head_start + 2 * pl.program_id(0) + s, 1), :]
        spread = jnp.broadcast_to(diag, (BLOCK, 4 * BLOCK))
        tile = pltpu.roll(spread, 0, 1, stride=1, stride_axis=0)[:, BLOCK:].T
        low_far = jnp.broadcast_to(diag[:, 1:2], (BLOCK, BLOCK))
        high_far = jnp.broadcast_to(diag[:, 4 * BLOCK - 1 :], (BLOCK, BLOCK))
        bias_tiles.append((low_far, tile, high_far))
    turned_vals = vals.astype(f32).T.astype(bf16)
    upper = lax.broadcasted_iota(i32, (BLOCK, 1), 0) < half
    for i in range(blocks):
        rows = slice(i * BLOCK, (i + 1) * BLOCK)
        same = cols_ref[:, seg_line : seg_line + 1] == row_ids[:, rows]
        queries = q_ref[rows, :]
        outs = []
        for s in range(2):
            mask = jnp.where(lane // half == s, scale, 0.0).astype(bf16)
            scores = mm(keys, queries * mask, NT)
            low_far, tile, high_far = bias_tiles[s]
            pieces = []
            for j in range(blocks):
                if j - i < -1:
                    pieces.append(low_far)
                elif j - i > 1:
                    pieces.append(high_far)
                else:
                    start = (j - i + 1) * BLOCK
                    pieces.append(tile[start : start + BLOCK])
            scores = scores + jnp.concatenate(pieces, axis=0)
            scores = jnp.where(same, scores, -1000000000.0)
            top = jnp.max(scores, axis=0, keepdims=True)
            grown = jnp.exp(scores - top)
            probs = (grown * (1.0 / jnp.sum(grown, axis=0, keepdims=True))).astype(bf16)
            probs_ref[s, :, rows] = probs
            outs.append(mm(turned_vals, probs))
        att_ref[rows, :] = jnp.where(upper, outs[0], outs[1]).T.astype(bf16)


def chosen_of(router, cols_ref, line):
    pick = cols_ref[:, line : line + 1] == lane_numbers(*router.shape)
    return pick, jnp.sum(jnp.where(pick, router, 0.0), axis=-1, keepdims=True)


def route_kernel(tok_ref, att_a_ref, att_b_ref, w_out_ref, gain_ref, w_router_ref, rows_ref, residual_ref, router_ref, sent_ref):
    near = att_a_ref.shape[1]
    branch = mm(att_a_ref[...], w_out_ref[:near]) + mm(att_b_ref[...], w_out_ref[near:])
    residual = tok_ref[...].astype(f32) + branch
    residual_ref[...] = residual
    inverse = lax.rsqrt(jnp.mean(residual * residual, axis=-1, keepdims=True) + eps)
    normed = residual * inverse * gain_ref[...]
    low = normed.astype(bf16)
    tokens = low.shape[0]
    direct = len(sent_ref.shape) == 4
    local_experts = sent_ref.shape[1] if direct else sent_ref.shape[0]
    slots = sent_ref.shape[0] * sent_ref.shape[2] if direct else sent_ref.shape[1]
    for index in range(local_experts):
        table = lax.broadcasted_iota(i32, (slots, tokens), 0) == rows_ref[index : index + 1, :]
        rows = mm(one_hot(table), low)
        if direct:
            by_group(rows, sent_ref, index)
        else:
            sent_ref[index] = rows.astype(bf16)
    w_high, w_low = split(w_router_ref[...])
    low_rest = (normed - low.astype(f32)).astype(bf16)
    experts = w_high.shape[1]
    logits = mm(low, jnp.concatenate([w_high, w_low], axis=1))
    logits = logits[:, :experts] + logits[:, experts:] + mm(low_rest, w_high)
    top = jnp.max(logits, axis=-1, keepdims=True)
    grown = jnp.exp(logits - top)
    router = grown / jnp.sum(grown, axis=-1, keepdims=True)
    router_ref[...] = router


def expert_kernel(place_ref, x_ref, cot_ref, w_in_ref, w_back_ref, *refs, parts, le, groups, order, olds):
    count = len(order)
    refs = refs[olds:]
    back_refs = refs[:count]
    act_ref, gp_ref = refs[count : count + 2]
    x_buf, g_buf, w_in_buf, w_back_buf, act_buf, gp_buf, back_buf = refs[count + 2 : -4]
    x_sem, g_sem, w_sem, put_sem = refs[-4:]
    place = place_ref[0]
    whole = [(place + j) % parts for j in order]
    load_in = pltpu.make_async_copy(w_in_ref.at[le], w_in_buf, w_sem.at[0])
    load_back = pltpu.make_async_copy(w_back_ref.at[le], w_back_buf, w_sem.at[1])
    load_in.start()
    loads = []
    for at in range(count):
        loads.append(
            (
                pltpu.make_async_copy(x_ref.at[whole[at]], x_buf.at[at], x_sem.at[at]),
                pltpu.make_async_copy(cot_ref.at[whole[at]], g_buf.at[at], g_sem.at[at]),
            )
        )
        loads[at][0].start()
    load_back.start()
    for at in range(count):
        loads[at][1].start()
    load_in.wait()
    scale = (2.0 / jnp.pi) ** 0.5
    slots, model = x_buf.shape[1:]
    hidden = act_buf.shape[2]
    spare = back_buf.shape[1] - slots
    line = lax.broadcasted_iota(i32, (spare, BLOCK), 0)
    capacity = slots // groups
    puts = []

    def put(source, target, kind, at):
        copy = pltpu.make_async_copy(source, target, put_sem.at[kind, at])
        copy.start()
        puts.append(copy)

    span = 2
    for first in range(0, count, span):
        ats = range(first, first + span)
        for at in ats:
            loads[at][0].wait()
        pre = mm(x_buf[first : first + span].reshape(span * slots, model), w_in_buf[...])
        for at in ats:
            loads[at][1].wait()
        if first == 0:
            load_back.wait()
        grad = mm(g_buf[first : first + span].reshape(span * slots, model), w_back_buf[...], NT)
        square = pre * pre
        slant = jnp.tanh(scale * pre * (1.0 + 0.044715 * square))
        act = (0.5 * pre * (1.0 + slant)).astype(bf16)
        act_buf[first : first + span] = act.reshape(span, slots, hidden)
        slope = 0.5 * (1.0 + slant) + 0.5 * pre * (1.0 - slant * slant) * (
            scale * (1.0 + 3.0 * 0.044715 * square)
        )
        gp = (grad * slope).astype(bf16)
        gp_buf[first : first + span] = gp.reshape(span, slots, hidden)
        back = mm(gp, w_in_buf[...], NT).astype(bf16)
        back_buf[first : first + span, :slots] = back.reshape(span, slots, model)
        all_dots = jnp.sum(act.astype(f32) * grad, axis=-1, keepdims=True)
        for at in ats:
            put(act_buf.at[at], act_ref.at[whole[at]], 0, at)
            put(gp_buf.at[at], gp_ref.at[whole[at]], 1, at)
            dots = all_dots[(at - first) * slots : (at - first + 1) * slots]
            dots = jnp.broadcast_to(dots, (slots, BLOCK)).T
            laid = jnp.zeros((spare, BLOCK), f32)
            for group in range(groups):
                piece = dots[:1, group * capacity : (group + 1) * capacity]
                piece = jnp.concatenate([piece, jnp.zeros((1, BLOCK - capacity), f32)], axis=1)
                laid = jnp.where(line == group, piece, laid)
            back_buf[at, slots:] = jnp.zeros((spare, model), bf16)
            back_buf[at, slots:, :BLOCK] = laid.astype(bf16)
            put(back_buf.at[at], back_refs[at], 2, at)
    for copy in puts:
        copy.wait()


def expert_weights_kernel(own_ref, x_ref, cot_ref, gp_ref, w_router_ref, all_act_ref, w_back_ref, *refs, le, local_experts):
    in_ref, back_ref, out_ref, gs_ref, gate_ref, turned_ref = refs[-6:]
    parts = x_ref.shape[0]

    def flat(values):
        return values.reshape(-1, values.shape[-1])

    @pl.when(pl.program_id(0) == 0)
    def _():
        w_high, w_low = split(w_router_ref[...])
        number = own_ref[0] * local_experts + le
        for part in range(parts):
            rows = x_ref[part]
            logits = mm(rows, w_high) + mm(rows, w_low)
            grown = jnp.exp(logits - jnp.max(logits, axis=-1, keepdims=True))
            pick = lane_numbers(*logits.shape) == number
            gate = jnp.sum(jnp.where(pick, grown, 0.0), axis=-1, keepdims=True)
            gate = gate / jnp.sum(grown, axis=-1, keepdims=True)
            gate_ref[part] = gate
            gs_ref[part] = (cot_ref[part].astype(f32) * gate).astype(bf16)
        turned_ref[...] = flat(x_ref[...]).T

    gp = (gp_ref[...].astype(f32) * gate_ref[...]).astype(bf16)
    in_ref[0] = mm(turned_ref[...], flat(gp))
    third = back_ref.shape[1]
    begin = pl.multiple_of(pl.program_id(0) * third, third)
    back_ref[0] = mm(flat(all_act_ref[:, :, pl.ds(begin, third)]), flat(gs_ref[...]), TN)
    out = mm(flat(all_act_ref[...]), w_back_ref[0])
    slots = out.shape[0] // parts
    for part in range(parts):
        rows = out[part * slots : (part + 1) * slots]
        if len(out_ref.shape) == 5:
            by_group(rows, out_ref.at[part], 0)
        else:
            out_ref[part, 0] = rows.astype(bf16)


def middle_kernel(residual_ref, cot_ref, gain_ref, w_router_ref, router_ref, cols_ref, w_out_ref, *refs, capacity, stride):
    grad_res_ref, branch_ref, att_ref, extra_ref, sums_ref = refs[-5:]
    back_refs = refs[:-5]
    local_experts = len(back_refs)
    tokens = residual_ref.shape[0]
    rows = None
    grad_gate = None
    for index, back_ref in enumerate(back_refs):
        key = cols_ref[:, index : index + 1]
        group = key // capacity
        number = lane_numbers(tokens, back_ref.shape[0])
        back = back_ref[...]
        part = mm(one_hot(number == key + group * (stride - capacity)), back)
        lines = mm(one_hot(number == group * stride + capacity), back[:, :BLOCK])
        slot = lane_numbers(tokens, BLOCK) == key - group * capacity
        picked = jnp.sum(jnp.where(slot, lines, 0.0), axis=-1, keepdims=True)
        rows = part if rows is None else rows + part
        grad_gate = picked if grad_gate is None else grad_gate + picked
    router = router_ref[...]
    pick, chosen = chosen_of(router, cols_ref, local_experts)
    grad_logits = router * (pick.astype(f32) - chosen) * grad_gate
    residual = residual_ref[...]
    inverse = lax.rsqrt(jnp.mean(residual * residual, axis=-1, keepdims=True) + eps)
    gain = gain_ref[...]
    scaled = residual * inverse
    logits_high, logits_low = split(grad_logits)
    w_high, w_low = split(w_router_ref[...])
    grad_normed = chosen * rows + mm(
        jnp.concatenate([logits_high, logits_low, logits_high], axis=1),
        jnp.concatenate([w_high, w_high, w_low], axis=1),
        NT,
    )
    weighted = grad_normed * gain
    lean = jnp.mean(weighted * residual, axis=-1, keepdims=True)
    grad_res = cot_ref[...].astype(f32) + (
        inverse * weighted - residual * (inverse * inverse * inverse) * lean
    )
    grad_res_ref[...] = grad_res
    low = grad_res.astype(bf16)
    branch_ref[...] = low
    att_ref[...] = mm(low, w_out_ref[...], NT).astype(bf16)
    gain_grad = jnp.sum(grad_normed * scaled, axis=0, keepdims=True)
    normed_high, normed_low = split(scaled * gain)
    experts = logits_high.shape[1]
    router_grad = mm(jnp.concatenate([logits_high, logits_low], axis=1), normed_high, TN)
    router_grad = router_grad[:experts] + router_grad[experts:] + mm(logits_high, normed_low, TN)
    spare = sums_ref.shape[0] - router_grad.shape[0] - 1
    both = jnp.concatenate(
        [router_grad, gain_grad, jnp.zeros((spare, gain_grad.shape[1]), f32)], axis=0
    )
    step = pl.program_id(0)

    @pl.when(step == 0)
    def _():
        sums_ref[...] = both

    @pl.when(step > 0)
    def _():
        sums_ref[...] += both

    @pl.when(step == pl.num_programs(0) - 1)
    def _():
        extra_ref[...] = sums_ref[...].T.astype(bf16)


def attend_back_kernel(q_ref, k_ref, v_ref, probs_ref, grad_ref, turned_ref, *refs, kind, head_start, buckets):
    if kind == 0:
        att_a_ref, att_b_ref, branch_ref, extra_ref = refs[:4]
    else:
        old_diag_ref = refs[0]
    if kind == 2:
        old_weight_ref = refs[1]
    dq_ref, dk_ref, dv_ref, weight_ref, diag_ref, slope_ref = refs[-6:]
    step = pl.program_id(0)
    length = k_ref.shape[0]
    blocks = length // BLOCK
    lane = lane_numbers(1, BLOCK)
    half = BLOCK // 2
    scale = half**-0.5
    keys = k_ref[...]
    vals = v_ref[...]
    queries = q_ref[...]
    grads = grad_ref[...]
    static_columns = weight_ref.shape[1]

    @pl.when(step == 0)
    def _():
        if kind == 0:
            diag_ref[...] = jnp.zeros_like(diag_ref)
            model = branch_ref.shape[1]
            tail = extra_ref.shape[1]
            begin = static_columns - tail - model
            near = att_a_ref.shape[1]
            branch = branch_ref[...]
            weight_ref[:near, begin : begin + model] = mm(att_a_ref[...], branch, TN).astype(bf16)
            weight_ref[near:, begin : begin + model] = mm(att_b_ref[...], branch, TN).astype(bf16)
            weight_ref[:, begin + model :] = extra_ref[...]
        else:
            diag_ref[...] = old_diag_ref[...]
        if kind == 2:
            weight_ref[:, : old_weight_ref.shape[1]] = old_weight_ref[...]

    across = lax.broadcasted_iota(i32, (BLOCK, BLOCK), 0) + lane_numbers(BLOCK, BLOCK)
    flip = one_hot(across == BLOCK - 1)
    turned_keys = keys.astype(f32).T.astype(bf16)
    dq = [[] for _ in range(blocks)]
    dk, dv = [], []
    for s in range(2):
        mask = jnp.where(lane // half == s, 1.0, 0.0).astype(bf16)
        near = [None, None, None]
        far = [None, None]
        for i in range(blocks):
            rows = slice(i * BLOCK, (i + 1) * BLOCK)
            probs = probs_ref[s, :, rows].astype(f32)
            grad_probs = mm(vals, grads[rows] * mask, NT)
            delta = jnp.sum(probs * grad_probs, axis=0, keepdims=True)
            slope = probs * (grad_probs - delta)
            low = slope.astype(bf16)
            slope_ref[s, :, rows] = low
            dq[i].append(mm(turned_keys, low))
            for j in range(blocks):
                piece = slope[j * BLOCK : (j + 1) * BLOCK]
                apart = j - i
                if abs(apart) <= 1:
                    old = near[1 - apart]
                    near[1 - apart] = piece if old is None else old + piece
                else:
                    old = far[int(apart > 0)]
                    far[int(apart > 0)] = piece if old is None else old + piece
        dk.append(mm(slope_ref[s], queries))
        dv.append(mm(probs_ref[s], grads))
        wide = jnp.concatenate([jnp.zeros_like(near[0])] + near, axis=1)
        lined = pltpu.roll(mm(flip, wide.astype(bf16)), 3 * BLOCK + 1, 1, stride=1, stride_axis=0)
        lined = jnp.concatenate([lined, far[0], far[1]], axis=1)
        diag_ref[pl.ds(head_start + 2 * step + s, 1), :] = jnp.sum(lined, axis=0, keepdims=True)
    upper = lax.broadcasted_iota(i32, (BLOCK, 1), 0) < half
    dq_low = jnp.concatenate([jnp.where(upper, *item).T for item in dq], axis=0)
    dq_low = (dq_low * scale).astype(bf16)
    left = lane < half
    dk_low = (jnp.where(left, dk[0], dk[1]) * scale).astype(bf16)
    dv_low = jnp.where(left, dv[0], dv[1]).astype(bf16)
    dq_ref[...] = dq_low
    dk_ref[...] = dk_low
    dv_ref[...] = dv_low
    begin = 0 if kind < 2 else old_weight_ref.shape[1]
    begin = pl.multiple_of(step * (3 * BLOCK) + begin, 3 * BLOCK)
    weight_ref[:, pl.ds(begin, 3 * BLOCK)] = mm(
        turned_ref[...], jnp.concatenate([dq_low, dk_low, dv_low], axis=1)
    ).astype(bf16)
    if kind == 2:

        @pl.when(step == pl.num_programs(0) - 1)
        def _():
            wide = diag_ref.shape[1]
            number = lane_numbers(buckets, wide)
            bucket = bucket_of(2 * BLOCK - number)
            bucket = jnp.where(number >= 4 * BLOCK, 15, bucket)
            bucket = jnp.where(number >= 5 * BLOCK, 31, bucket)
            pick = bucket == lax.broadcasted_iota(i32, (buckets, wide), 0)
            rows = jnp.concatenate(
                [diag_ref[...], jnp.zeros((BLOCK - diag_ref.shape[0], wide), f32)], axis=0
            )
            bias = mm_exact(pick.astype(f32), rows, NT)
            begin = static_columns - BLOCK
            weight_ref[:, begin:] = jnp.zeros((weight_ref.shape[0], BLOCK), bf16)
            weight_ref[:buckets, begin:] = bias.astype(bf16)


def tokens_kernel(tok_ref, gain_ref, w_ref, grad_res_ref, *refs):
    out_ref = refs[-1]
    parts = refs[:-1]
    groups = len(parts) // 3
    model = tok_ref.shape[1]
    grad_normed = None
    for part in range(3):
        start = part * model
        for group in range(groups):
            block = parts[3 * group + part]
            width = block.shape[1]
            piece = mm(block[...], w_ref[:, start : start + width], NT)
            grad_normed = piece if grad_normed is None else grad_normed + piece
            start += width
    values = tok_ref[...].astype(f32)
    inverse = lax.rsqrt(jnp.mean(values * values, axis=-1, keepdims=True) + eps)
    weighted = grad_normed * gain_ref[...]
    lean = jnp.mean(weighted * values, axis=-1, keepdims=True)
    out_ref[...] = grad_res_ref[...] + (
        inverse * weighted - values * (inverse * inverse * inverse) * lean
    )


def output_kernel(residual_ref, router_ref, cols_ref, rows_ref, out_ref):
    tokens = residual_ref.shape[0]
    local_experts, slots = rows_ref.shape[:2]
    mixture = None
    for index in range(local_experts):
        turned = cols_ref[:, index : index + 1] == lane_numbers(tokens, slots)
        part = mm(one_hot(turned), rows_ref[index])
        mixture = part if mixture is None else mixture + part
    _, chosen = chosen_of(router_ref[...], cols_ref, local_experts)
    out_ref[...] = (residual_ref[...] + chosen * mixture).astype(bf16)


def finish_kernel(where_ref, a_ref, b_ref, w_ref, *refs):
    qkv_ref, out_ref, gain_ref, extra_ref = refs[-4:]
    place = where_ref[2]
    parts = a_ref.shape[1]
    model = out_ref.shape[3]
    pairs = model // BLOCK
    near = pairs // 3
    for k in range(parts):
        z = (place + parts - k) % parts
        a = a_ref[0, k].astype(f32)
        b = b_ref[0, k].astype(f32)
        total = None
        for part in range(3):
            pieces = [
                (a if p < near else b)[:, ((p if p < near else p - near) * 3 + part) * BLOCK :][
                    :, :BLOCK
                ]
                for p in range(pairs)
            ]
            whole = jnp.concatenate(pieces, axis=1)
            span = slice(part * model, (part + 1) * model)
            qkv_ref[0, z, :, span] = whole
            w = w_ref[0, z, :, span].astype(f32)
            share = jnp.sum(whole * w, axis=-1, keepdims=True)
            total = share if total is None else total + share
        gain_ref[0, z] = jnp.broadcast_to(total, gain_ref.shape[2:])
        begin = near * 3 * BLOCK
        out_ref[0, z] = a[:, begin : begin + model]
        tail = a.shape[1] - begin - model
        extra_ref[0, z, :, :tail] = a[:, begin + model :]
        extra_ref[0, z, :, tail:] = b[:, (pairs - near) * 3 * BLOCK :]


def small_kernel(gain_ref, sums_ref, extra_ref, router_ref, gains_ref, bias_ref, *, experts, at):
    extras = extra_ref[:, :at].T
    router_ref[...] = extras[:experts]
    gains_ref[0:1, :] = sums_ref[...].T[0:1] / gain_ref[...]
    gains_ref[1:2, :] = extras[experts : experts + 1]
    heads, buckets = bias_ref.shape
    bias_ref[...] = extra_ref[:BLOCK, at:].T[:heads, :buckets]


def add_low(left, right):
    return (left.astype(f32) + right.astype(f32)).astype(bf16)


def tie(items, after):
    return lax.optimization_barrier((items, after))[0]


def held(kernel, start, after):
    def body(*refs):
        kernel(*refs[:start], *refs[start + len(after) :])

    return body


class Scatter:
    def __init__(self, blocks):
        self.parts = lax.axis_size("hidden")
        self.blocks = blocks
        self.count = 0

    def step(self, after=()):
        self.count += 1
        right, left = self.blocks[self.parts - self.count], self.blocks[self.count]
        if self.count > 1:
            right, left = add_low(right, self.right), add_low(left, self.left)
        right, left = tie((right, left), after)
        ways = [(a, a + 1) for a in range(self.count)]
        self.right = lax.ppermute(right, "hidden", ways)
        ways = [(a, a - 1) for a in range(self.parts - self.count, self.parts)]
        self.left = lax.ppermute(left, "hidden", ways)

    def last(self):
        return self.right, self.left

    def finish(self, after=()):
        right, left = tie(self.last(), after)
        total = self.blocks[0].astype(f32) + right.astype(f32) + left.astype(f32)
        return total.astype(bf16)


def pick_block(blocks, index):
    return lax.dynamic_index_in_dim(blocks, index, 0, keepdims=False)


class Sum:
    def __init__(self, values):
        self.groups = lax.axis_size("expert")
        self.parts = lax.axis_size("hidden")
        self.own = lax.axis_index("expert")
        self.place = lax.axis_index("hidden")
        self.core = self.own % 2
        self.chip = self.own // 2
        self.chips = self.groups // 2
        self.pair = [(a, a ^ 1) for a in range(self.groups)]
        self.width = values.shape[1]
        self.values = values

    def cores(self):
        halves = self.values.reshape(2, -1, self.width)
        got = lax.ppermute(pick_block(halves, 1 - self.core), "expert", self.pair)
        self.values = add_low(pick_block(halves, self.core), got)

    def cores_at_once(self):
        teams = [[2 * a, 2 * a + 1] for a in range(self.chips)]
        got = lax.all_to_all(
            self.values, "expert", split_axis=0, concat_axis=0, tiled=True, axis_index_groups=teams
        ).reshape(2, -1, self.width)
        self.values = add_low(got[0], got[1])

    def plane(self):
        pieces = self.values.reshape(self.chips, -1, self.width)
        total = pick_block(pieces, self.chip).astype(f32)
        for step in range(1, self.chips):
            ways = [(a, a ^ (2 * step)) for a in range(self.groups)]
            got = lax.ppermute(pick_block(pieces, self.chip ^ step), "expert", ways)
            total = total + got.astype(f32)
        self.values = total.astype(bf16)

    def line(self):
        pieces = self.values.reshape(self.parts, -1, self.width)
        total = pick_block(pieces, self.place).astype(f32)
        for step in range(1, self.parts):
            ways = [(a, (a + step) % self.parts) for a in range(self.parts)]
            got = lax.ppermute(pick_block(pieces, (self.place + step) % self.parts), "hidden", ways)
            total = total + got.astype(f32)
        self.values = total.astype(bf16)

    def line_back(self):
        pieces = [self.values]
        for step in range(1, self.parts):
            ways = [(a, (a + step) % self.parts) for a in range(self.parts)]
            pieces.append(lax.ppermute(self.values, "hidden", ways))
        self.values = jnp.stack(pieces)

    def plane_back(self):
        pieces = [self.values]
        for step in range(1, self.chips):
            ways = [(a, a ^ (2 * step)) for a in range(self.groups)]
            pieces.append(lax.ppermute(self.values, "expert", ways))
        self.values = jnp.stack(pieces)

    def cores_back(self):
        return self.values, lax.ppermute(self.values, "expert", self.pair)

    def run(self):
        self.cores()
        self.plane()
        self.line()
        self.line_back()
        self.plane_back()
        return self.cores_back()


def local(tokens, cotangent, segments, routes, slot_ids, kept_flags, gain_one, w_qkv, w_out, bias_table, gain_two, w_router, w_in, w_back):
    tok_rows, model = tokens.shape
    bucket_count, head_count = bias_table.shape
    experts = w_router.shape[1]
    local_experts = w_in.shape[0]
    hidden = w_in.shape[2]
    groups = lax.axis_size("expert")
    parts = lax.axis_size("hidden")
    own = lax.axis_index("expert")
    place = lax.axis_index("hidden")
    capacity = max(2, (5 * tok_rows + 4 * experts - 1) // (4 * experts))
    slots = groups * capacity
    pairs = head_count // 2
    shape = jax.ShapeDtypeStruct
    vmem = pl.BlockSpec(memory_space=pltpu.VMEM)
    any_space = pl.BlockSpec(memory_space=pl.ANY)
    gain_one_row = gain_one[None, :]
    gain_two_row = gain_two[None, :]
    seg_line = local_experts + 1

    def exchange(rows, axis=0):
        return lax.all_to_all(rows, "expert", split_axis=axis, concat_axis=axis, tiled=True)

    cot_near = lax.all_gather(cotangent, "hidden", axis=0, tiled=False)
    id_rows, id_cols, diag_bias = pl.pallas_call(
        functools.partial(place_kernel, capacity=capacity, local_experts=local_experts),
        out_shape=[
            shape((8, tok_rows), i32),
            shape((tok_rows, BLOCK), i32),
            shape((head_count, 4 * BLOCK), f32),
        ],
        in_specs=[vmem] * 5,
        out_specs=[vmem] * 3,
        compiler_params=params(),
        cost_estimate=cost(1e8, 1e6),
        name="place",
    )(routes[None, :], slot_ids[None, :], kept_flags[None, :], segments, bias_table)
    qkv, turned = pl.pallas_call(
        qkv_kernel,
        grid=(3,),
        out_shape=[shape((tok_rows, 3 * model), bf16), shape((model, tok_rows), bf16)],
        in_specs=[
            pl.BlockSpec((tok_rows, model), lambda j: (0, 0)),
            pl.BlockSpec((1, model), lambda j: (0, 0)),
            pl.BlockSpec((model, model), lambda j: (0, j)),
        ],
        out_specs=[
            pl.BlockSpec((tok_rows, model), lambda j: (0, j)),
            pl.BlockSpec((model, tok_rows), lambda j: (0, 0)),
        ],
        scratch_shapes=[pltpu.VMEM((tok_rows, model), bf16)],
        compiler_params=params(("arbitrary",)),
        cost_estimate=cost(6 * tok_rows * model * model, 8 * model * model * 2),
        name="qkv",
    )(tokens, gain_one_row, w_qkv)

    def pair_spec(offset):
        return pl.BlockSpec((tok_rows, BLOCK), lambda p: (0, offset + p))

    steps = pairs // 2
    attended, probs = [], []
    for half in range(2):
        start = half * steps
        att, prob = pl.pallas_call(
            functools.partial(attend_kernel, seg_line=seg_line, head_start=2 * start),
            grid=(steps,),
            out_shape=[
                shape((tok_rows, steps * BLOCK), bf16),
                shape((2 * steps, tok_rows, tok_rows), bf16),
            ],
            in_specs=[
                pair_spec(start),
                pair_spec(pairs + start),
                pair_spec(2 * pairs + start),
                pl.BlockSpec((8, tok_rows), lambda p: (0, 0)),
                pl.BlockSpec((tok_rows, BLOCK), lambda p: (0, 0)),
                pl.BlockSpec((head_count, 4 * BLOCK), lambda p: (0, 0)),
            ],
            out_specs=[
                pair_spec(0),
                pl.BlockSpec((2, tok_rows, tok_rows), lambda p: (p, 0, 0)),
            ],
            compiler_params=params(("arbitrary",)),
            cost_estimate=cost(steps * 4e9, steps * 3e6),
            name="attend",
        )(qkv, qkv, qkv, id_rows, id_cols, diag_bias)
        attended.append(att)
        probs.append(prob)

    def by_slots(count):
        if direct:
            return shape((groups, count, capacity, model), bf16)
        return shape((count, slots, model), bf16)

    direct = capacity % 8 == 0
    residual, router, sent_rows = pl.pallas_call(
        route_kernel,
        out_shape=[
            shape((tok_rows, model), f32),
            shape((tok_rows, experts), f32),
            by_slots(local_experts),
        ],
        in_specs=[vmem] * 7,
        out_specs=[vmem] * 3,
        compiler_params=params(),
        cost_estimate=cost(6e9, 6e6),
        name="route",
    )(tokens, *attended, w_out, gain_two_row, w_router, id_rows)

    place_arr = place.astype(i32).reshape(1)
    own_arr = own.astype(i32).reshape(1)
    spare = -(-groups // 16) * 16
    block = shape((slots + spare, model), bf16)
    stack = shape((parts, slots, hidden), bf16)
    smem = pl.BlockSpec(memory_space=pltpu.SMEM)
    third = hidden // 3

    def run_experts(le, order, olds, after=()):
        count = len(order)
        results = pl.pallas_call(
            held(
                functools.partial(
                    expert_kernel, parts=parts, le=le, groups=groups, order=order, olds=len(olds)
                ),
                5 + len(olds),
                after,
            ),
            out_shape=[block] * count + [stack, stack],
            in_specs=[smem] + [any_space] * (4 + len(olds) + len(after)),
            out_specs=[any_space] * (count + 2),
            input_output_aliases={5 + n: count + n for n in range(len(olds))},
            scratch_shapes=[
                pltpu.VMEM((count, slots, model), bf16),
                pltpu.VMEM((count, slots, model), bf16),
                pltpu.VMEM((model, hidden), bf16),
                pltpu.VMEM((hidden, model), bf16),
                pltpu.VMEM((count, slots, hidden), bf16),
                pltpu.VMEM((count, slots, hidden), bf16),
                pltpu.VMEM((count, slots + spare, model), bf16),
                pltpu.SemaphoreType.DMA((count,)),
                pltpu.SemaphoreType.DMA((count,)),
                pltpu.SemaphoreType.DMA((2,)),
                pltpu.SemaphoreType.DMA((3, count)),
            ],
            compiler_params=params(),
            cost_estimate=cost(4 * count * slots * model * hidden, 1e7),
            name="experts",
        )(place_arr, rows_all[le], cot_all[le], w_in, w_back, *olds, *after)
        return results[:count], list(results[count:])

    def run_both(le, after=()):
        ends = list(range(1, parts, 2))
        rest = list(range(0, parts, 2))
        backs = [None] * parts
        some, kept = run_experts(le, ends, [], after)
        for j, item in zip(ends, some):
            backs[j] = item
        some, kept = run_experts(le, rest, kept)
        for j, item in zip(rest, some):
            backs[j] = item
        return backs, kept

    def run_weights(le, kept, olds, after):
        act, gp = kept
        stack_spec = pl.BlockSpec((parts, slots, model), lambda j: (0, 0, 0))
        hidden_spec = pl.BlockSpec((parts, slots, third), lambda j: (0, 0, j))
        return pl.pallas_call(
            held(
                functools.partial(expert_weights_kernel, le=le, local_experts=local_experts),
                7 + len(olds),
                after,
            ),
            grid=(3,),
            out_shape=[
                shape((local_experts, model, hidden), f32),
                shape((local_experts, hidden, model), f32),
                shape((parts,) + by_slots(local_experts).shape, bf16),
            ],
            in_specs=[
                smem,
                stack_spec,
                stack_spec,
                hidden_spec,
                pl.BlockSpec((model, experts), lambda j: (0, 0)),
                pl.BlockSpec((parts, slots, hidden), lambda j: (0, 0, 0)),
                pl.BlockSpec((1, hidden, model // 3), lambda j: (le, 0, j)),
            ]
            + [any_space] * (len(olds) + len(after)),
            out_specs=[
                pl.BlockSpec((1, model, third), lambda j: (le, 0, j)),
                pl.BlockSpec((1, third, model), lambda j: (le, j, 0)),
                pl.BlockSpec(
                    (parts, groups, 1, capacity, model // 3), lambda j: (0, 0, le, 0, j)
                )
                if direct
                else pl.BlockSpec((parts, 1, slots, model // 3), lambda j: (0, le, 0, j)),
            ],
            scratch_shapes=[
                pltpu.VMEM((parts, slots, model), bf16),
                pltpu.VMEM((parts, slots, 1), f32),
                pltpu.VMEM((model, parts * slots), bf16),
            ],
            input_output_aliases={7 + n: n for n in range(len(olds))},
            compiler_params=params(("arbitrary",)),
            cost_estimate=cost(4 * parts * slots * model * hidden, 1.3e7),
            name="expert_weights",
        )(own_arr, rows_all[le], cot_all[le], gp, w_router, act, w_back, *olds, *after)

    def own_slots(le, ids, after):
        return pl.pallas_call(
            held(functools.partial(slots_kernel, parts=parts, le=le), 2 + parts, after),
            out_shape=by_slots(parts),
            in_specs=[smem] + [vmem] * (parts + 1) + [any_space] * len(after),
            out_specs=vmem,
            compiler_params=params(),
            cost_estimate=cost(2e9, 6e6),
            name="slots",
        )(place_arr, *ids, cot_near, *after)

    def exchange_slots(rows):
        if not direct:
            return exchange(rows, 1)
        return exchange(rows).transpose(1, 0, 2, 3).reshape(-1, slots, model)

    here = exchange_slots(sent_rows)
    rows_all = [
        lax.all_gather(here[le], "hidden", axis=0, tiled=False) for le in range(local_experts)
    ]
    ids = [id_rows]
    far_ids = tie(id_rows, here)
    for step in range(1, parts):
        ways = [((a + step) % parts, a) for a in range(parts)]
        ids.append(lax.ppermute(far_ids, "hidden", ways))
    cot_slots = [own_slots(0, ids, [here])]
    cot_slots.append(own_slots(1, ids, cot_slots))
    cot_all = [exchange_slots(cot_slots[0])]
    cot_all.append(exchange_slots(tie(cot_slots[1], cot_all[0])))
    backs, kept = run_both(0, cot_slots[1:])
    sum_first = Scatter(backs)
    sum_first.step()
    grads = run_weights(0, kept, [], [])
    sum_first.step(grads)
    backs, kept_second = run_both(1, grads[:1])
    sum_second = Scatter(backs)
    sum_second.step()
    sum_second.step(sum_first.last())
    sum_first.step()
    grads = run_weights(1, kept_second, grads, sum_second.last()[:1])

    def with_dots(total):
        rows = total[:slots].reshape(groups, capacity, model)
        dots = total[slots : slots + groups].reshape(groups, 1, model)
        dots = jnp.pad(dots, ((0, 0), (0, stride - capacity - 1), (0, 0)))
        return jnp.concatenate([rows, dots], axis=1).reshape(groups * stride, model)

    stride = -(-(capacity + 1) // 8) * 8
    back_first = exchange(with_dots(sum_first.finish()))
    sum_second.step(sum_first.last())
    back_second = sum_second.finish((back_first, grads))
    backs = [back_first, exchange(with_dots(back_second))]
    grad_w_in, grad_w_back, out_sums = grads
    extra_width = -(-(experts + 1) // BLOCK) * BLOCK

    def token_spec(width):
        return pl.BlockSpec((tok_rows // 2, width), lambda t: (t, 0))

    def full_spec(item):
        return pl.BlockSpec(item.shape, lambda t: (0, 0))

    grad_res, grad_branch, grad_att, extra = pl.pallas_call(
        functools.partial(middle_kernel, capacity=capacity, stride=stride),
        grid=(2,),
        out_shape=[
            shape((tok_rows, model), f32),
            shape((tok_rows, model), bf16),
            shape((tok_rows, model), bf16),
            shape((model, extra_width), bf16),
        ],
        in_specs=[
            token_spec(model),
            token_spec(model),
            full_spec(gain_two_row),
            full_spec(w_router),
            token_spec(experts),
            token_spec(BLOCK),
            full_spec(w_out),
            *[full_spec(item) for item in backs],
        ],
        out_specs=[
            token_spec(model),
            token_spec(model),
            token_spec(model),
            pl.BlockSpec((model, extra_width), lambda t: (0, 0)),
        ],
        scratch_shapes=[pltpu.VMEM((extra_width, model), f32)],
        compiler_params=params(("arbitrary",)),
        cost_estimate=cost(6e9, 8e6),
        name="middle",
    )(
        residual,
        cotangent,
        gain_two_row,
        w_router,
        router,
        id_cols,
        w_out,
        *backs,
    )

    out_rows = lax.psum_scatter(out_sums, "hidden", scatter_dimension=0, tiled=False)
    out_ready = out_rows
    out_rows = exchange_slots(out_rows)
    output = pl.pallas_call(
        output_kernel,
        out_shape=shape((tok_rows, model), bf16),
        in_specs=[vmem] * 4,
        out_specs=vmem,
        compiler_params=params(),
        cost_estimate=cost(1e9, 4e6),
        name="output",
    )(residual, router, id_cols, out_rows)

    def run_back(kind, start, count, extras, width):
        inner = start % steps
        return pl.pallas_call(
            functools.partial(
                attend_back_kernel,
                kind=kind,
                head_start=2 * start,
                buckets=bucket_count,
            ),
            grid=(count,),
            out_shape=[shape((tok_rows, count * BLOCK), bf16)] * 3
            + [shape((model, width), bf16), shape((16, 6 * BLOCK), f32)],
            in_specs=[
                pair_spec(start),
                pair_spec(pairs + start),
                pair_spec(2 * pairs + start),
                pl.BlockSpec((2, tok_rows, tok_rows), lambda p: (inner + p, 0, 0)),
                pair_spec(start),
                pl.BlockSpec((model, tok_rows), lambda p: (0, 0)),
            ]
            + [pl.BlockSpec(item.shape, lambda p: (0, 0)) for item in extras],
            out_specs=[pair_spec(0)] * 3
            + [
                pl.BlockSpec((model, width), lambda p: (0, 0)),
                pl.BlockSpec((16, 6 * BLOCK), lambda p: (0, 0)),
            ],
            scratch_shapes=[pltpu.VMEM((2, tok_rows, tok_rows), bf16)],
            compiler_params=params(("arbitrary",)),
            cost_estimate=cost(count * 4e9, count * 3e6),
            name="attend_back",
        )(qkv, qkv, qkv, probs[start // steps], grad_att, turned, *extras)

    wide = 3 * BLOCK
    early = pairs // 3
    first = run_back(
        0, 0, early, [*attended, grad_branch, extra], wide * early + model + extra_width
    )
    sum_a = Sum(first[3])
    sum_a.cores()
    second = run_back(1, early, 1, [first[4]], wide)
    sum_a.values = tie(sum_a.values, second[3])
    sum_a.plane()
    third_part = run_back(
        2, early + 1, pairs - early - 1, [second[4], second[3]], wide * (pairs - early) + BLOCK
    )
    sum_b = Sum(tie(third_part[3], sum_a.values))
    sum_b.cores()
    grad_parts = [*first[:3], *second[:3], *third_part[:3]]
    grad_tokens = pl.pallas_call(
        held(tokens_kernel, 4 + len(grad_parts), [sum_b.values]),
        out_shape=shape((tok_rows, model), f32),
        in_specs=[vmem] * (4 + len(grad_parts)) + [any_space],
        out_specs=vmem,
        compiler_params=params(),
        cost_estimate=cost(3e9, 1e7),
        name="tokens_grad",
    )(tokens, gain_one_row, w_qkv, grad_res, *grad_parts, sum_b.values)
    sum_a.line()
    sum_b.plane()
    sum_a.line_back()
    sum_b.line()
    sum_a.plane_back()
    sum_b.line_back()
    sum_b.values = tie(sum_b.values, (out_rows, grad_tokens))
    sums = [sum_a.cores_back()]
    sum_b.plane_back()
    sum_b.values = tie(sum_b.values, output)
    sums.append(sum_b.cores_back())

    chips = groups // 2
    rows = model // (groups * parts)
    where = jnp.stack([own % 2, own // 2, place]).astype(i32)

    tail = extra_width + BLOCK
    widths = (3 * model, model, BLOCK, tail)

    def finish(team, a, b, olds):
        def piece_spec(width):
            return pl.BlockSpec((1, parts, rows, width), lambda s, at: (s, 0, 0, 0))

        def whole_spec(width):
            return pl.BlockSpec(
                (1, parts, rows, width),
                lambda s, at: ((at[0] ^ team) * chips + (at[1] ^ s), 0, 0, 0),
            )

        return pl.pallas_call(
            finish_kernel,
            grid_spec=pltpu.PrefetchScalarGridSpec(
                num_scalar_prefetch=1,
                grid=(chips,),
                in_specs=[
                    piece_spec(a.shape[-1]),
                    piece_spec(b.shape[-1]),
                    whole_spec(3 * model),
                ]
                + [any_space] * len(olds),
                out_specs=[whole_spec(width) for width in widths],
            ),
            out_shape=[shape((groups, parts, rows, width), f32) for width in widths],
            input_output_aliases={4 + n: n for n in range(len(olds))},
            compiler_params=params(("arbitrary",)),
            cost_estimate=cost(1e8, 1e7),
            name="finish",
        )(where, a, b, w_qkv.reshape(groups, parts, rows, 3 * model), *olds)

    (own_a, got_a), (own_b, got_b) = sums
    finished = finish(0, own_a, own_b, [])
    finished = finish(1, got_a, got_b, finished)
    grad_w_qkv, grad_w_out, gain_sums, extras = [
        item.reshape(model, item.shape[-1]) for item in finished
    ]
    grad_router, gains, grad_bias = pl.pallas_call(
        functools.partial(small_kernel, experts=experts, at=extra_width),
        out_shape=[
            shape((experts, model), f32),
            shape((2, model), f32),
            shape((head_count, bucket_count), f32),
        ],
        in_specs=[vmem] * 3,
        out_specs=[vmem] * 3,
        compiler_params=params(),
        cost_estimate=cost(1e6, 2e6),
        name="small",
    )(gain_one_row, gain_sums, extras)
    return (
        output,
        grad_tokens,
        gains[0],
        grad_w_qkv,
        grad_w_out,
        grad_bias.T,
        gains[1],
        grad_router.T,
        grad_w_in,
        grad_w_back,
    )


def solution(mesh):
    return jax.shard_map(
        local,
        mesh=mesh,
        in_specs=(
            P(("expert", "hidden"), None),
            P(("expert", "hidden"), None),
            P(("expert", "hidden"), None),
            P(("expert", "hidden")),
            P(("expert", "hidden")),
            P(("expert", "hidden")),
            P(),
            P(),
            P(),
            P(),
            P(),
            P(),
            P("expert", None, "hidden"),
            P("expert", "hidden", None),
        ),
        out_specs=(
            P(("expert", "hidden"), None),
            P(("expert", "hidden"), None),
            P(),
            P(),
            P(),
            P(),
            P(),
            P(),
            P("expert", None, "hidden"),
            P("expert", "hidden", None),
        ),
        check_vma=False,
    )
```
